32 devices in a mesh: dp: 8 (over z, y), head: 4 (over x, core).
Axes of the slice: x: 2, y: 2, z: 4, core: 2. Of those that a mesh axis runs over, the one named last changes fastest.
Arguments:
- radar: bfloat16 [16384, 768], P(('dp', 'head')), may hold values from -6 to 6
- optical: bfloat16 [16384, 768], P(('dp', 'head')), may hold values from -6 to 6
- patch_table: int32 [3, 16384], P(None, ('dp', 'head')), may hold values from 0 to 1511, as said below
- cotangent: bfloat16 [16384, 768], P(('dp', 'head')), may hold values from -6 to 6
- norm_self_gain: float32 [768], replicated, may hold values from 0.5 to 1.5
- norm_self_shift: float32 [768], replicated, may hold values from -1.75 to 1.75
- self_query: bfloat16 [768, 768], P(None, 'head'), may hold values from -0.21875 to 0.21875
- self_key: bfloat16 [768, 768], P(None, 'head'), may hold values from -0.21875 to 0.21875
- self_value: bfloat16 [768, 768], P(None, 'head'), may hold values from -0.21875 to 0.21875
- self_out: bfloat16 [768, 768], P('head'), may hold values from -0.625 to 0.625
- self_out_bias: float32 [768], replicated, may hold values from -1.75 to 1.75
- norm_radar_gain: float32 [768], replicated, may hold values from 0.5 to 1.5
- norm_radar_shift: float32 [768], replicated, may hold values from -1.75 to 1.75
- norm_optical_gain: float32 [768], replicated, may hold values from 0.5 to 1.5
- norm_optical_shift: float32 [768], replicated, may hold values from -1.75 to 1.75
- cross_query: bfloat16 [768, 768], P(None, 'head'), may hold values from -0.21875 to 0.21875
- cross_key: bfloat16 [768, 768], P(None, 'head'), may hold values from -0.21875 to 0.21875
- cross_value: bfloat16 [768, 768], P(None, 'head'), may hold values from -0.21875 to 0.21875
- cross_out: bfloat16 [768, 768], P('head'), may hold values from -0.625 to 0.625
- cross_out_bias: float32 [768], replicated, may hold values from -1.75 to 1.75
- norm_feed_gain: float32 [768], replicated, may hold values from 0.5 to 1.5
- norm_feed_shift: float32 [768], replicated, may hold values from -1.75 to 1.75
- feed_in: bfloat16 [768, 3072], replicated, may hold values from -0.21875 to 0.21875
- feed_in_bias: float32 [3072], replicated, may hold values from -1.75 to 1.75
- feed_out: bfloat16 [3072, 768], replicated, may hold values from -0.109375 to 0.109375
- feed_out_bias: float32 [768], replicated, may hold values from -1.75 to 1.75
Outputs:
- merged: bfloat16 [16384, 768], P(('dp', 'head'))
- radar_gradient: float32 [16384, 768], P(('dp', 'head'))
- optical_gradient: float32 [16384, 768], P(('dp', 'head'))
- norm_self_gain_gradient: float32 [768], replicated
- norm_self_shift_gradient: float32 [768], replicated
- self_query_gradient: float32 [768, 768], P(None, 'head')
- self_key_gradient: float32 [768, 768], P(None, 'head')
- self_value_gradient: float32 [768, 768], P(None, 'head')
- self_out_gradient: float32 [768, 768], P('head')
- self_out_bias_gradient: float32 [768], replicated
- norm_radar_gain_gradient: float32 [768], replicated
- norm_radar_shift_gradient: float32 [768], replicated
- norm_optical_gain_gradient: float32 [768], replicated
- norm_optical_shift_gradient: float32 [768], replicated
- cross_query_gradient: float32 [768, 768], P(None, 'head')
- cross_key_gradient: float32 [768, 768], P(None, 'head')
- cross_value_gradient: float32 [768, 768], P(None, 'head')
- cross_out_gradient: float32 [768, 768], P('head')
- cross_out_bias_gradient: float32 [768], replicated
- norm_feed_gain_gradient: float32 [768], replicated
- norm_feed_shift_gradient: float32 [768], replicated
- feed_in_gradient: float32 [768, 3072], P(None, ('dp', 'head'))
- feed_in_bias_gradient: float32 [3072], P(('dp', 'head'))
- feed_out_gradient: float32 [3072, 768], P(('dp', 'head'))
- feed_out_bias_gradient: float32 [768], replicated
The draws below stay inside these ranges and needn't reach their ends.
Inputs may be any that keep to these rules, and one draw needn't show every extreme that they name: `patch_table`: row 0 numbers the items of each buffer of 512 slots from 0 in order. Each item is a square grid of side 12, 15 or 20, whole in consecutive slots of one buffer, patches in row-major order with grid row in row 1 and grid column in row 2. The slots after a buffer's last item (one at least) carry segment 1000 plus the slot's place in its buffer and grid row and column 0.
All inputs are finite; a program needn't handle non-finite values.
Results may differ from the reference program's by a relative error of at most 0.024.
Values may be sent and summed in bfloat16 or wider, within the bound.
A program may use at most 256 MiB of HBM per device.

```python
import jax
import jax.numpy as jnp
from jax import lax

D = 768
HEADS = 12
HEAD_DIM = 64
FF = 3072
SIDE_S = 12
SIDE_M = 15
SIDE_L = 20
TOK_DEV = 512
TOKENS = 16384
N_HEAD = 4


def draw_patch_table(key, part):
    key = jax.random.fold_in(key, 7)
    buffers = TOKENS // TOK_DEV
    count = TOK_DEV // (SIDE_S * SIDE_S) + 1
    sides = jnp.array([SIDE_S, SIDE_M, SIDE_L], jnp.int32)
    pick = jax.random.randint(key, (buffers, count), 0, 3)
    side = sides[pick]
    side = side.at[0, 0].set(SIDE_L)
    size = side * side
    ends = jnp.cumsum(size, axis=1)
    starts = ends - size
    keep = ends <= TOK_DEV - 1
    place = jnp.arange(TOK_DEV, dtype=jnp.int32)
    inside = keep[:, None, :] & (place[None, :, None] >= starts[:, None, :]) & (place[None, :, None] < ends[:, None, :])
    inside_int = inside.astype(jnp.int32)
    covered = jnp.sum(inside_int, axis=2) > 0
    item_number = jnp.sum(inside_int * jnp.arange(count, dtype=jnp.int32)[None, None, :], axis=2)
    offset = place[None, :] - jnp.sum(inside_int * starts[:, None, :], axis=2)
    width = jnp.maximum(jnp.sum(inside_int * side[:, None, :], axis=2), 1)
    grid_row = jnp.where(covered, offset // width, 0)
    grid_col = jnp.where(covered, offset % width, 0)
    segment = jnp.where(covered, item_number, 1000 + place[None, :])
    return jnp.stack([segment, grid_row, grid_col]).reshape(3, TOKENS).astype(jnp.int32)


def block_levels(rng, shape, shards, smallest, high):
    level, own = 1.0, jax.random.fold_in(rng, 6)
    for axis_at, shards_of in shards:
        steps = jnp.exp(jax.random.uniform(jax.random.fold_in(own, axis_at), (shards_of,), jnp.float32, smallest / len(shards), high / len(shards)))
        level = level * jnp.repeat(steps, shape[axis_at] // shards_of).reshape([-1 if axis == axis_at else 1 for axis in range(len(shape))])
    return level


def gaussian(stream_key, extent, scale, most, split=(), held_as=jnp.bfloat16):
    factor_of = block_levels(stream_key, extent, split, -0.22, 0.18) if split else 1.0
    entries = jax.random.normal(stream_key, extent, jnp.float32) * scale * factor_of
    return jnp.minimum(jnp.maximum(entries, -most), most).astype(held_as)


def setup_inputs(seed: int = 0) -> dict:
    key_of = jax.random.split(jax.random.key(seed), 27)
    radar = gaussian(key_of[0], (TOKENS, D), 1.0, 6.0, ((0, 32),))
    optical = gaussian(key_of[1], (TOKENS, D), 1.0, 6.0, ((0, 32),))
    patch_table = draw_patch_table(jax.random.fold_in(key_of[26], 71), 0)
    cotangent = gaussian(key_of[3], (TOKENS, D), 1.0, 6.0, ((0, 32),))
    norm_self_gain = jnp.clip(1.0 + 0.1 * jax.random.normal(key_of[4], (D,), jnp.float32), 0.5, 1.5)
    norm_self_shift = gaussian(key_of[5], (D,), 0.3, 1.75, (), jnp.float32)
    self_query = gaussian(key_of[6], (D, D), D ** -0.5, 0.21875, ((1, 4),))
    self_key = gaussian(key_of[7], (D, D), D ** -0.5, 0.21875, ((1, 4),))
    self_value = gaussian(key_of[8], (D, D), D ** -0.5, 0.21875, ((1, 4),))
    self_out = gaussian(key_of[9], (D, D), (D // 8) ** -0.5, 0.625, ((0, 4),))
    self_out_bias = gaussian(key_of[10], (D,), 0.3, 1.75, (), jnp.float32)
    norm_radar_gain = jnp.clip(1.0 + 0.1 * jax.random.normal(key_of[11], (D,), jnp.float32), 0.5, 1.5)
    norm_radar_shift = gaussian(key_of[12], (D,), 0.3, 1.75, (), jnp.float32)
    norm_optical_gain = jnp.clip(1.0 + 0.1 * jax.random.normal(key_of[13], (D,), jnp.float32), 0.5, 1.5)
    norm_optical_shift = gaussian(key_of[14], (D,), 0.3, 1.75, (), jnp.float32)
    cross_query = gaussian(key_of[15], (D, D), D ** -0.5, 0.21875, ((1, 4),))
    cross_key = gaussian(key_of[16], (D, D), D ** -0.5, 0.21875, ((1, 4),))
    cross_value = gaussian(key_of[17], (D, D), D ** -0.5, 0.21875, ((1, 4),))
    cross_out = gaussian(key_of[18], (D, D), (D // 8) ** -0.5, 0.625, ((0, 4),))
    cross_out_bias = gaussian(key_of[19], (D,), 0.3, 1.75, (), jnp.float32)
    norm_feed_gain = jnp.clip(1.0 + 0.1 * jax.random.normal(key_of[20], (D,), jnp.float32), 0.5, 1.5)
    norm_feed_shift = gaussian(key_of[21], (D,), 0.3, 1.75, (), jnp.float32)
    feed_in = gaussian(key_of[22], (D, FF), D ** -0.5, 0.21875)
    feed_in_bias = gaussian(key_of[23], (FF,), 0.3, 1.75, (), jnp.float32)
    feed_out = gaussian(key_of[24], (FF, D), FF ** -0.5, 0.109375)
    feed_out_bias = gaussian(key_of[25], (D,), 0.3, 1.75, (), jnp.float32)
    return {"radar": radar, "optical": optical, "patch_table": patch_table, "cotangent": cotangent, "norm_self_gain": norm_self_gain, "norm_self_shift": norm_self_shift, "self_query": self_query, "self_key": self_key, "self_value": self_value, "self_out": self_out, "self_out_bias": self_out_bias, "norm_radar_gain": norm_radar_gain, "norm_radar_shift": norm_radar_shift, "norm_optical_gain": norm_optical_gain, "norm_optical_shift": norm_optical_shift, "cross_query": cross_query, "cross_key": cross_key, "cross_value": cross_value, "cross_out": cross_out, "cross_out_bias": cross_out_bias, "norm_feed_gain": norm_feed_gain, "norm_feed_shift": norm_feed_shift, "feed_in": feed_in, "feed_in_bias": feed_in_bias, "feed_out": feed_out, "feed_out_bias": feed_out_bias}


@jax.custom_vjp
def low(v):
    return lax.optimization_barrier(v.astype(jnp.bfloat16)).astype(jnp.float32)

@jax.custom_vjp
def low_back(v):
    return v

def low_keep(v):
    return (low(v), None)

def low_pass(kept, grad):
    return (grad,)

def back_keep(v):
    return (v, None)

def back_low(kept, grad):
    return (low(grad),)
low.defvjp(low_keep, low_pass)
low_back.defvjp(back_keep, back_low)
EPSILON = 1e-06
MASKED = -1000000000.0
HIGH = lax.Precision.HIGHEST

def normalize(values, gain, shift):
    center = values - lax.optimization_barrier(jnp.mean(values, axis=-1, keepdims=True))
    spread = lax.optimization_barrier(jnp.mean(center * center, axis=-1, keepdims=True))
    return center * lax.rsqrt(spread + EPSILON) * gain + shift

def product(left, right):
    return jnp.dot(left, right, precision=HIGH)

def attention(query_rows, key_rows, w_query, w_key, w_value, w_out, table, joint):
    length = query_rows.shape[0]
    group_heads = HEADS // N_HEAD
    width = group_heads * HEAD_DIM
    scale = HEAD_DIM ** (-0.5)
    down = (table[1][:, None] - table[1][None, :]).astype(jnp.float32)
    across = (table[2][:, None] - table[2][None, :]).astype(jnp.float32)
    reach = jnp.sqrt(down * down + across * across)
    same = table[0][:, None] == table[0][None, :]
    total = jnp.zeros((length, w_out.shape[1]), jnp.float32)
    for group in range(N_HEAD):
        lower = group * width
        query_side = low_back(query_rows)
        key_side = query_side if joint else low_back(key_rows)
        query = low_back(low(product(query_side, w_query[:, lower:lower + width]))).reshape(length, group_heads, HEAD_DIM)
        keys = low_back(low(product(key_side, w_key[:, lower:lower + width]))).reshape(length, group_heads, HEAD_DIM)
        values = low_back(low(product(key_side, w_value[:, lower:lower + width]))).reshape(length, group_heads, HEAD_DIM)
        slopes = jnp.exp2(-8.0 * (group * group_heads + jnp.arange(group_heads, dtype=jnp.int32) + 1).astype(jnp.float32) / HEADS)
        score = jnp.einsum('ihd,jhd->hij', query, keys, precision=HIGH) * scale + -slopes[:, None, None] * reach[None]
        score = jnp.where(same[None], low_back(score), MASKED)
        weights = low(jax.nn.softmax(score, axis=-1))
        mixed = low_back(low(jnp.einsum('hij,jhd->ihd', weights, values, precision=HIGH))).reshape(length, width)
        total = total + low_back(low(product(mixed, w_out[lower:lower + width, :])))
    return total

def layer(radar, optical, table, params):
    self_gain, self_shift, self_query, self_key, self_value, self_out, self_bias = params[0:7]
    radar_gain, radar_shift, optical_gain, optical_shift = params[7:11]
    cross_query, cross_key, cross_value, cross_out, cross_bias = params[11:16]
    feed_gain, feed_shift, feed_in, feed_in_bias, feed_out, feed_out_bias = params[16:22]
    normed = low(normalize(radar, self_gain, self_shift))
    mixed_one = radar + attention(normed, normed, self_query, self_key, self_value, self_out, table, True) + self_bias
    radar_side = low(normalize(mixed_one, radar_gain, radar_shift))
    optical_side = low(normalize(optical, optical_gain, optical_shift))
    mixed_two = mixed_one + attention(radar_side, optical_side, cross_query, cross_key, cross_value, cross_out, table, False) + cross_bias
    feed = low(normalize(mixed_two, feed_gain, feed_shift))
    inner = low_back(product(feed, feed_in) + feed_in_bias)
    hidden = low(jax.nn.gelu(inner, approximate=True))
    return mixed_two + low_back(product(hidden, feed_out)) + feed_out_bias

def reference(radar, optical, patch_table, cotangent, norm_self_gain, norm_self_shift, self_query, self_key, self_value, self_out, self_out_bias, norm_radar_gain, norm_radar_shift, norm_optical_gain, norm_optical_shift, cross_query, cross_key, cross_value, cross_out, cross_out_bias, norm_feed_gain, norm_feed_shift, feed_in, feed_in_bias, feed_out, feed_out_bias):
    params = tuple((value.astype(jnp.float32) for value in (norm_self_gain, norm_self_shift, self_query, self_key, self_value, self_out, self_out_bias, norm_radar_gain, norm_radar_shift, norm_optical_gain, norm_optical_shift, cross_query, cross_key, cross_value, cross_out, cross_out_bias, norm_feed_gain, norm_feed_shift, feed_in, feed_in_bias, feed_out, feed_out_bias)))
    count = radar.shape[0] // TOK_DEV
    width = radar.shape[1]
    radar_blocks = radar.astype(jnp.float32).reshape(count, TOK_DEV, width)
    optical_blocks = optical.astype(jnp.float32).reshape(count, TOK_DEV, width)
    cot_blocks = cotangent.astype(jnp.float32).reshape(count, TOK_DEV, width)
    table_blocks = jnp.transpose(patch_table.reshape(3, count, TOK_DEV), (1, 0, 2))

    def step(sums, block):
        radar_part, optical_part, table_part, cot_part = block

        def forward(radar_in, optical_in, weights_in):
            return layer(radar_in, optical_in, table_part, weights_in)
        merged, pullback = jax.vjp(forward, radar_part, optical_part, params)
        radar_grad, optical_grad, weight_grads = pullback(cot_part)
        return (jax.tree.map(jnp.add, sums, weight_grads), (merged.astype(jnp.bfloat16), radar_grad, optical_grad))
    start = jax.tree.map(jnp.zeros_like, params)
    sums, (merged, radar_grad, optical_grad) = lax.scan(step, start, (radar_blocks, optical_blocks, table_blocks, cot_blocks))
    return (merged.reshape(-1, width), radar_grad.reshape(-1, width), optical_grad.reshape(-1, width), sums[0], sums[1], sums[2], sums[3], sums[4], sums[5], sums[6], sums[7], sums[8], sums[9], sums[10], sums[11], sums[12], sums[13], sums[14], sums[15], sums[16], sums[17], sums[18], sums[19], sums[20], sums[21])
```

```python
import functools

import jax
import jax.numpy as jnp
import numpy as np
from jax import lax
from jax.experimental import pallas as pl
from jax.experimental.pallas import tpu as pltpu
from jax.sharding import PartitionSpec as P

F32, BF16 = jnp.float32, jnp.bfloat16
HEADS, HEAD_DIM = 12, 64
EPSILON = 1e-06
FAR = 1e12
LIMIT = 60 * 2**20
VMEM = pl.BlockSpec(memory_space=pltpu.VMEM)
SMEM = pl.BlockSpec(memory_space=pltpu.SMEM)


def nn(a, b):
    return lax.dot_general(a, b, (((1,), (0,)), ((), ())), preferred_element_type=F32)


def nt(a, b):
    return lax.dot_general(a, b, (((1,), (1,)), ((), ())), preferred_element_type=F32)


def tn(a, b):
    return lax.dot_general(a, b, (((0,), (0,)), ((), ())), preferred_element_type=F32)


def rows_loop(total, block, body):
    def step(i, _):
        body(pl.ds(pl.multiple_of(i * block, block), block))
        return 0

    lax.fori_loop(0, total // block, step, 0)


def centred(v):
    c = v - jnp.mean(v, axis=-1, keepdims=True)
    return c, lax.rsqrt(jnp.mean(c * c, axis=-1, keepdims=True) + EPSILON)


def norm_rows(src, gain, shift, dst):
    def body(rows):
        c, r = centred(src[rows, :].astype(F32))
        dst[rows, :] = (c * r * gain[...] + shift[...]).astype(BF16)

    rows_loop(src.shape[0], 128, body)


def norm_back_rows(v, gain, u):
    c, r = centred(v)
    hat = c * r
    w = u * gain
    dv = r * (
        w
        - jnp.mean(w, axis=-1, keepdims=True)
        - hat * jnp.mean(w * hat, axis=-1, keepdims=True)
    )
    return dv, jnp.sum(u * hat, axis=0, keepdims=True), jnp.sum(u, axis=0, keepdims=True)


def project(x, w, dst, scale=None):
    def body(cols):
        y = nt(x[...], w[cols, :])
        dst[:, cols] = (y if scale is None else y * scale).astype(BF16)

    rows_loop(w.shape[0], 256, body)


def fill_reach(table, columns, reach):
    def body(rows):
        col = columns[rows, :]
        down = (col[:, 1:2] - table[1:2, :]).astype(F32)
        across = (col[:, 2:3] - table[2:3, :]).astype(F32)
        same = col[:, 0:1] == table[0:1, :]
        reach[rows, :] = jnp.where(same, jnp.sqrt(down * down + across * across), FAR)

    rows_loop(reach.shape[0], 64, body)


def low_half(length):
    return lax.broadcasted_iota(jnp.int32, (length, 128), 1) < HEAD_DIM


def attend(q, k, v, reach, slope, mixed, lse):
    lo = low_half(q.shape[0])

    def pair(hp, _):
        at = pl.ds(pl.multiple_of(hp * 128, 128), 128)
        qs, ks, vs = q[:, at], k[:, at], v[:, at]
        outs, tops = [], []
        for sub in range(2):
            mine = lo if sub == 0 else jnp.logical_not(lo)
            s = nt(jnp.where(mine, qs, jnp.zeros_like(qs)), ks)
            s = s + slope[2 * hp + sub] * reach[...]
            top = jnp.max(s, axis=-1, keepdims=True)
            e = jnp.exp(s - top).astype(BF16)
            outs.append(nn(e, jnp.where(mine, vs, jnp.ones_like(vs))))
            tops.append(top)
        num = jnp.where(lo, outs[0], outs[1])
        den = pltpu.roll(jnp.where(lo, outs[1], outs[0]), HEAD_DIM, 1)
        mixed[:, at] = (num / den).astype(BF16)
        lse_t = (jnp.where(lo, tops[0], tops[1]) + jnp.log(den)).T
        lse[hp] = jnp.concatenate([lse_t[0:1], lse_t[HEAD_DIM : HEAD_DIM + 1]], axis=0)
        return 0

    lax.fori_loop(0, q.shape[1] // 128, pair, 0)


def attend_back(q, k, v, up, mixed, lse, reach, slope, dq, dk, dv):
    lo = low_half(q.shape[0])

    def pair(hp, _):
        at = pl.ds(pl.multiple_of(hp * 128, 128), 128)
        qs, ks, vs, ups = q[:, at], k[:, at], v[:, at], up[:, at]
        prod = (ups.astype(F32) * mixed[:, at].astype(F32)).T
        tops = lse[hp]
        dqs, dks, dvs = [], [], []
        for sub in range(2):
            mine = lo if sub == 0 else jnp.logical_not(lo)
            delta = jnp.sum(prod[sub * HEAD_DIM : (sub + 1) * HEAD_DIM], axis=0, keepdims=True)
            s = nt(jnp.where(mine, ks, jnp.zeros_like(ks)), qs)
            p = jnp.exp(s + slope[2 * hp + sub] * reach[...] - tops[sub : sub + 1])
            dp = nt(jnp.where(mine, vs, jnp.zeros_like(vs)), ups)
            ds = (p * (dp - delta)).astype(BF16)
            dvs.append(nn(p.astype(BF16), ups))
            dks.append(nn(ds, qs))
            dqs.append(tn(ds, ks))
        dq[:, at] = (jnp.where(lo, dqs[0], dqs[1]) * HEAD_DIM**-0.5).astype(BF16)
        dk[:, at] = jnp.where(lo, dks[0], dks[1]).astype(BF16)
        dv[:, at] = jnp.where(lo, dvs[0], dvs[1]).astype(BF16)
        return 0

    lax.fori_loop(0, q.shape[1] // 128, pair, 0)


def add_out(base, mixed, w_out, bias, dst):
    def body(cols):
        y = nn(mixed[...], w_out[:, cols])
        dst[:, cols] = base[:, cols].astype(F32) + y + bias[:, cols]

    rows_loop(w_out.shape[1], 256, body)


def self_forward(radar, gain, shift, w, bias, table, columns, slope,
                 normed, q, k, v, mixed, lse, one, reach):
    fill_reach(table, columns, reach)
    norm_rows(radar, gain, shift, normed)
    project(normed, w.at[0], q, HEAD_DIM**-0.5)
    project(normed, w.at[1], k)
    project(normed, w.at[2], v)
    attend(q, k, v, reach, slope, mixed, lse)
    add_out(radar, mixed, w.at[3], bias, one)


def cross_forward(one, optical, gain_r, shift_r, gain_o, shift_o, w, bias, reach, slope,
                  radar_low, optical_low, q, k, v, mixed, lse, two):
    norm_rows(optical, gain_o, shift_o, optical_low)
    project(optical_low, w.at[1], k)
    project(optical_low, w.at[2], v)
    norm_rows(one, gain_r, shift_r, radar_low)
    project(radar_low, w.at[0], q, HEAD_DIM**-0.5)
    attend(q, k, v, reach, slope, mixed, lse)
    add_out(one, mixed, w.at[3], bias, two)


def place_shards(full, place, at, keep, send):
    my, mx, mc = place[1], place[2], place[3]
    for x in range(2):
        for y in range(2):
            for c, dst in enumerate((keep, send)):
                row = (((y ^ my) * 2 + (x ^ mx)) * 2 + (c ^ mc)) * 96
                dst[x, y, at] = full[pl.ds(pl.multiple_of(row, 96), 96), :]


def feed_step(place, two, cot, gain, shift, w_in, b_in, w_out, b_out,
              merged, two_grad, keep_in, send_in, keep_out, send_out, bias_in, small,
              low, out, pull, full_in, full_out):
    step = pl.program_id(0)
    width = w_out.shape[0]
    block = 256

    @pl.when(step == 0)
    def _():
        norm_rows(two, gain, shift, low)

    for n in range(width // block):
        at = slice(n * block, (n + 1) * block)
        x = nn(low[...], w_in[:, at]) + b_in[:, at]
        inner = 0.7978845608028654 * x * (1.0 + 0.044715 * x * x)
        t = jnp.tanh(inner)
        half = 0.5 * (1.0 + t)
        hidden = (x * half).astype(BF16)
        slope = half + 0.5 * x * (1.0 - t * t) * (
            0.7978845608028654 * (1.0 + 3 * 0.044715 * x * x)
        )
        grad = (nt(cot[...], w_out[at, :]) * slope).astype(BF16)
        bias_in[0, :, at] = jnp.sum(grad.astype(F32), axis=0, keepdims=True)
        part_out = nn(hidden, w_out[at, :])
        part_pull = nt(grad, w_in[:, at])
        if n == 0:
            @pl.when(step == 0)
            def _():
                out[...] = part_out
                pull[...] = part_pull

            @pl.when(step > 0)
            def _():
                out[...] += part_out
                pull[...] += part_pull
        else:
            out[...] += part_out
            pull[...] += part_pull
        full_out[at, :] = tn(hidden, cot[...]).astype(BF16)
        full_in[at, :] = tn(grad, low[...]).astype(BF16)
    place_shards(full_in, place, 0, keep_in.at[:, :], send_in.at[:, :])
    place_shards(full_out, place, 0, keep_out.at[:, :], send_out.at[:, :])

    @pl.when(step == pl.num_programs(0) - 1)
    def _():
        small[...] = jnp.zeros_like(small)

        def body(rows):
            value, cotangent = two[rows, :], cot[rows, :].astype(F32)
            merged[rows, :] = (value + out[rows, :] + b_out[...]).astype(BF16)
            dv, dgain, dshift = norm_back_rows(value, gain[...], pull[rows, :])
            total = cotangent + dv
            two_grad[rows, :] = total
            small[0:1, :] += dgain
            small[1:2, :] += dshift
            small[2:3, :] += jnp.sum(cotangent, axis=0, keepdims=True)
            small[3:4, :] += jnp.sum(total, axis=0, keepdims=True)

        rows_loop(two.shape[0], 128, body)


def weight_grad(grads, rows, full):
    def body(cols):
        full[cols, :] = tn(grads[:, cols], rows[...]).astype(BF16)

    rows_loop(grads.shape[1], 256, body)


def attn_shards(full, place, mat, keep, send):
    my, mz = place[1], place[0]
    for x in range(2):
        for y in range(2):
            for c, dst in enumerate((keep, send)):
                row = ((x * 2 + c) * 2 + (y ^ my)) * 96
                dst[x, y, mat ^ mz] = full[pl.ds(pl.multiple_of(row, 96), 96), :]


def attention_back(place, grad, low, mixed, q, k, v, lse, reach, slope, x, y, w,
                   keep, send, full, up, dq, dk, dv):
    def cast(rows):
        low[rows, :] = grad[rows, :].astype(BF16)

    rows_loop(grad.shape[0], 128, cast)
    weight_grad(mixed, low, full)
    attn_shards(full, place, 3, keep, send)
    project(low, w.at[3], up)
    attend_back(q, k, v, up, mixed, lse, reach, slope, dq, dk, dv)
    for mat, (side, d) in enumerate(((x, dq), (y, dk), (y, dv))):
        weight_grad(d, side, full)
        attn_shards(full, place, mat, keep, send)


def cross_backward(place, two_grad, mixed, q, k, v, lse, reach, slope, radar_low, optical_low, w,
                   one, optical, gain_r, gain_o,
                   one_grad, optical_grad, keep, send, small,
                   low, full, up, dq, dk, dv):
    attention_back(place, two_grad, low, mixed, q, k, v, lse, reach, slope, radar_low, optical_low,
                   w, keep, send, full, up, dq, dk, dv)
    small[...] = jnp.zeros_like(small)

    def body(rows):
        pull = nn(dq[rows, :], w[0])
        dv_, dgain, dshift = norm_back_rows(one[rows, :], gain_r[...], pull)
        total = two_grad[rows, :] + dv_
        one_grad[rows, :] = total
        small[0:1, :] += dgain
        small[1:2, :] += dshift
        small[4:5, :] += jnp.sum(total, axis=0, keepdims=True)
        pull = nn(dk[rows, :], w[1]) + nn(dv[rows, :], w[2])
        dv_, dgain, dshift = norm_back_rows(optical[rows, :].astype(F32), gain_o[...], pull)
        optical_grad[rows, :] = dv_
        small[2:3, :] += dgain
        small[3:4, :] += dshift

    rows_loop(two_grad.shape[0], 256, body)


def self_backward(place, one_grad, mixed, q, k, v, lse, reach, slope, normed, w, radar, gain,
                  radar_grad, keep, send, small,
                  low, full, up, dq, dk, dv):
    attention_back(place, one_grad, low, mixed, q, k, v, lse, reach, slope, normed, normed,
                   w, keep, send, full, up, dq, dk, dv)
    small[...] = jnp.zeros_like(small)

    def body(rows):
        pull = nn(dq[rows, :], w[0]) + nn(dk[rows, :], w[1]) + nn(dv[rows, :], w[2])
        dv_, dgain, dshift = norm_back_rows(radar[rows, :].astype(F32), gain[...], pull)
        radar_grad[rows, :] = one_grad[rows, :] + dv_
        small[0:1, :] += dgain
        small[1:2, :] += dshift

    rows_loop(one_grad.shape[0], 256, body)


def shape(dims, dtype):
    return jax.ShapeDtypeStruct(dims, dtype)


def call(body, outs, scratch, operands, in_specs, **more):
    return pl.pallas_call(
        body,
        out_shape=outs,
        in_specs=in_specs,
        out_specs=[VMEM] * len(outs),
        scratch_shapes=scratch,
        compiler_params=pltpu.CompilerParams(vmem_limit_bytes=LIMIT),
        **more,
    )(*operands)


def run_self_forward(radar, gain, shift, w, bias, table, columns, slope):
    n, d = radar.shape
    low = shape((n, d), BF16)
    return call(
        self_forward,
        [low, low, low, low, low, shape((6, 2, n), F32), shape((n, d), F32), shape((n, n), F32)],
        [],
        (radar, gain, shift, w, bias, table, columns, slope),
        [VMEM] * 7 + [SMEM],
        name="self_forward",
        cost_estimate=pl.CostEstimate(flops=4 * 10**9, bytes_accessed=10**7, transcendentals=0),
    )


def run_cross_forward(one, optical, gain_r, shift_r, gain_o, shift_o, w, bias, reach, slope):
    n, d = one.shape
    low = shape((n, d), BF16)
    return call(
        cross_forward,
        [low, low, low, low, low, low, shape((6, 2, n), F32), shape((n, d), F32)],
        [],
        (one, optical, gain_r, shift_r, gain_o, shift_o, w, bias, reach, slope),
        [VMEM] * 9 + [SMEM],
        name="cross_forward",
        cost_estimate=pl.CostEstimate(flops=4 * 10**9, bytes_accessed=10**7, transcendentals=0),
    )


def run_feed(place, two, cot, gain, shift, w_in, b_in, w_out, b_out):
    n, d = two.shape
    f = w_in.shape[1]
    tile = 768
    whole = lambda *dims: pl.BlockSpec(dims, lambda i, p: (0,) * len(dims))
    slots = pl.BlockSpec((2, 2, 1, 96, d), lambda i, p: (0, 0, i ^ p[0], 0, 0))
    grad = shape((2, 2, 4, 96, d), BF16)
    return pl.pallas_call(
        feed_step,
        grid_spec=pltpu.PrefetchScalarGridSpec(
            num_scalar_prefetch=1,
            grid=(f // tile,),
            in_specs=[
                whole(n, d), whole(n, d), whole(1, d), whole(1, d),
                pl.BlockSpec((d, tile), lambda i, p: (0, i)),
                pl.BlockSpec((1, tile), lambda i, p: (0, i)),
                pl.BlockSpec((tile, d), lambda i, p: (i, 0)),
                whole(1, d),
            ],
            out_specs=[
                whole(n, d), whole(n, d), slots, slots, slots, slots,
                pl.BlockSpec((1, 1, tile), lambda i, p: (i, 0, 0)),
                whole(8, d),
            ],
            scratch_shapes=[
                pltpu.VMEM((n, d), BF16), pltpu.VMEM((n, d), F32), pltpu.VMEM((n, d), F32),
                pltpu.VMEM((tile, d), BF16), pltpu.VMEM((tile, d), BF16),
            ],
        ),
        out_shape=[
            shape((n, d), BF16), shape((n, d), F32), grad, grad, grad, grad,
            shape((f // tile, 1, tile), F32), shape((8, d), F32),
        ],
        compiler_params=pltpu.CompilerParams(vmem_limit_bytes=LIMIT),
        name="feed",
        cost_estimate=pl.CostEstimate(flops=15 * 10**9, bytes_accessed=25 * 10**6, transcendentals=0),
    )(place, two, cot, gain, shift, w_in, b_in, w_out, b_out)


def back_scratch(n, d):
    low = pltpu.VMEM((n, d), BF16)
    return [low, pltpu.VMEM((d, d), BF16), low, low, low, low]


def run_cross_backward(place, two_grad, mixed, q, k, v, lse, reach, slope, radar_low, optical_low,
                       w, one, optical, gain_r, gain_o):
    n, d = one.shape
    grad = shape((2, 2, 4, 96, d), BF16)
    wide = shape((n, d), F32)
    return call(
        cross_backward,
        [wide, wide, grad, grad, shape((8, d), F32)],
        back_scratch(n, d),
        (place, two_grad, mixed, q, k, v, lse, reach, slope, radar_low, optical_low,
         w, one, optical, gain_r, gain_o),
        [SMEM] + [VMEM] * 7 + [SMEM] + [VMEM] * 7,
        name="cross_backward",
        cost_estimate=pl.CostEstimate(flops=12 * 10**9, bytes_accessed=25 * 10**6, transcendentals=0),
    )


def run_self_backward(place, one_grad, mixed, q, k, v, lse, reach, slope, normed, w, radar, gain):
    n, d = one_grad.shape
    grad = shape((2, 2, 4, 96, d), BF16)
    return call(
        self_backward,
        [shape((n, d), F32), grad, grad, shape((8, d), F32)],
        back_scratch(n, d),
        (place, one_grad, mixed, q, k, v, lse, reach, slope, normed, w, radar, gain),
        [SMEM] + [VMEM] * 7 + [SMEM] + [VMEM] * 4,
        name="self_backward",
        cost_estimate=pl.CostEstimate(flops=12 * 10**9, bytes_accessed=25 * 10**6, transcendentals=0),
    )


def finish(place, got, dq, dk, dv, do):
    for mat, dst in enumerate((dq, dk, dv, do)):
        rows = [got[h ^ place[1], mat ^ place[0]].astype(F32) for h in range(2)]
        if mat == 3:
            dst[0:96, :] = rows[0]
            dst[96:192, :] = rows[1]
        else:
            dst[...] = jnp.concatenate(rows, axis=0).T


def run_finish(place, got):
    d = got.shape[-1]
    col = shape((d, 192), F32)
    return call(
        finish, [col, col, col, shape((192, d), F32)], [], (place, got), [SMEM, VMEM],
        name="finish",
    )


CORE, X_BIT, Y_BIT, Z_NEAR, Z_FAR = 1, 2, 4, 8, 16


def swap(v, bit):
    return lax.ppermute(v, ("dp", "head"), [(i, i ^ bit) for i in range(32)])


def add(a, b):
    return (a.astype(F32) + b.astype(F32)).astype(BF16)


def halves(v, axis):
    return lax.index_in_dim(v, 0, axis, False), lax.index_in_dim(v, 1, axis, False)


def scatter_sum(keep, send, x_first):
    keep = keep.reshape(2, 2, 2, 2, 96, -1)
    got = swap(send.reshape(keep.shape), CORE)
    order = [(X_BIT, 0), (Y_BIT, 0)] if x_first else [(Y_BIT, 1), (X_BIT, 0)]
    for bit, axis in order + [(Z_NEAR, 1), (Z_FAR, 0)]:
        k0, k1 = halves(keep, axis)
        g0, g1 = halves(got, axis)
        got = swap(add(k1, g1), bit)
        keep = add(k0, g0)
    return keep.astype(F32) + got.astype(F32)


def gather_sums(own):
    own = own.astype(BF16)
    both = jnp.stack([own, swap(own, Z_FAR)])
    both = jnp.stack([both, swap(both, Z_NEAR)], axis=1).reshape(4, 96, -1)
    return jnp.stack([both, swap(both, Y_BIT)])


def gather_weights(own):
    core = swap(own, CORE)
    far = swap(own, X_BIT)
    return jnp.stack([own, core, far, swap(far, CORE)], axis=1).reshape(4, -1, own.shape[2])


def shards(
    radar, optical, patch_table, cotangent, norm_self_gain, norm_self_shift,
    self_query, self_key, self_value, self_out, self_out_bias, norm_radar_gain, norm_radar_shift,
    norm_optical_gain, norm_optical_shift, cross_query, cross_key, cross_value, cross_out,
    cross_out_bias, norm_feed_gain, norm_feed_shift, feed_in, feed_in_bias, feed_out, feed_out_bias,
):
    dp, head = lax.axis_size("dp"), lax.axis_size("head")
    near = (dp, head) == (8, 4)
    row = lambda v: v.reshape(1, -1)
    zero = jnp.int32(0)
    if near:
        mine = lax.axis_index("dp") * 4 + lax.axis_index("head")
        place = jnp.stack([mine // 8, mine // 4 % 2, mine // 2 % 2, mine % 2]).astype(jnp.int32)
        group = jnp.arange(4, dtype=jnp.int32) ^ lax.axis_index("head")
    else:
        place = jnp.stack([zero] * 4)
        group = jnp.arange(head, dtype=jnp.int32)
    per = HEADS // head
    heads = (group[:, None] * per + jnp.arange(per, dtype=jnp.int32)[None, :]).reshape(-1)
    slope = -jnp.exp2(-8.0 * (heads + 1).astype(F32) / HEADS)
    w_self = jnp.stack([self_query.T, self_key.T, self_value.T, self_out])
    w_cross = jnp.stack([cross_query.T, cross_key.T, cross_value.T, cross_out])
    if near:
        w_self, w_cross = gather_weights(w_self), gather_weights(w_cross)
    else:
        w_self = lax.all_gather(w_self, "head", axis=1, tiled=True)
        w_cross = lax.all_gather(w_cross, "head", axis=1, tiled=True)
    normed, sq, sk, sv, s_mixed, s_lse, one, reach = run_self_forward(
        radar, row(norm_self_gain), row(norm_self_shift), w_self, row(self_out_bias),
        patch_table, patch_table.T, slope,
    )
    radar_low, optical_low, cq, ck, cv, c_mixed, c_lse, two = run_cross_forward(
        one, optical, row(norm_radar_gain), row(norm_radar_shift), row(norm_optical_gain),
        row(norm_optical_shift), w_cross, row(cross_out_bias), reach, slope,
    )
    merged, two_grad, in_keep, in_send, out_keep, out_send, bias_in, feed_small = run_feed(
        place, two, cotangent, row(norm_feed_gain), row(norm_feed_shift),
        feed_in, row(feed_in_bias), feed_out, row(feed_out_bias),
    )
    one_grad, optical_grad, cross_keep, cross_send, cross_small = run_cross_backward(
        place, two_grad, c_mixed, cq, ck, cv, c_lse, reach, slope, radar_low, optical_low,
        w_cross, one, optical, row(norm_radar_gain), row(norm_optical_gain),
    )
    radar_grad, self_keep, self_send, self_small = run_self_backward(
        place, one_grad, s_mixed, sq, sk, sv, s_lse, reach, slope, normed,
        w_self, radar, row(norm_self_gain),
    )
    d = radar.shape[1]
    small = jnp.concatenate([feed_small, cross_small, self_small, bias_in.reshape(-1, d)])
    if near:
        feed_in_grad = scatter_sum(in_keep, in_send, True)
        feed_out_grad = scatter_sum(out_keep, out_send, False)
        cross = gather_sums(scatter_sum(cross_keep, cross_send, True))
        own = gather_sums(scatter_sum(self_keep, self_send, True))
        cross, own = run_finish(place, cross), run_finish(place, own)
        for bit in (CORE, X_BIT, Y_BIT, Z_NEAR, Z_FAR):
            small = small + swap(small, bit)
    else:
        def logical(keep, send, order):
            both = jnp.stack([keep, send])
            return jnp.transpose(both, order).reshape(-1, d)

        def feed_sum(keep, send):
            return lax.psum_scatter(
                logical(keep, send, (3, 2, 1, 0, 4, 5)).astype(F32),
                ("dp", "head"), scatter_dimension=0, tiled=True,
            )

        def attn_sum(keep, send):
            total = logical(keep, send, (3, 1, 0, 2, 4, 5)).astype(F32).reshape(4, -1, d)
            total = lax.psum_scatter(total, "head", scatter_dimension=1, tiled=True)
            total = lax.psum(total, "dp")
            return total[0].T, total[1].T, total[2].T, total[3]

        feed_in_grad, feed_out_grad = feed_sum(in_keep, in_send), feed_sum(out_keep, out_send)
        cross, own = attn_sum(cross_keep, cross_send), attn_sum(self_keep, self_send)
        small = lax.psum(small, ("dp", "head"))
    bias_part = feed_in_bias.shape[0] // (dp * head)
    feed_in_bias_grad = lax.dynamic_slice_in_dim(
        small[24:28].reshape(-1),
        (lax.axis_index("dp") * head + lax.axis_index("head")) * bias_part,
        bias_part,
    )
    return (
        merged, radar_grad, optical_grad,
        small[16], small[17], *own, small[12],
        small[8], small[9], small[10], small[11], *cross, small[3],
        small[0], small[1], feed_in_grad.T, feed_in_bias_grad, feed_out_grad, small[2],
    )


def solution(mesh):
    token, rep = P(("dp", "head"), None), P()
    col, row = P(None, "head"), P("head", None)
    in_specs = (
        token, token, P(None, ("dp", "head")), token,
        rep, rep, col, col, col, row, rep,
        rep, rep, rep, rep, col, col, col, row, rep,
        rep, rep, rep, rep, rep, rep,
    )
    out_specs = (
        token, token, token,
        rep, rep, col, col, col, row, rep,
        rep, rep, rep, rep, col, col, col, row, rep,
        rep, rep, P(None, ("dp", "head")), P(("dp", "head")), token, rep,
    )
    return jax.shard_map(shards, mesh=mesh, in_specs=in_specs, out_specs=out_specs, check_vma=False)
```

```python
import functools

import jax
import jax.numpy as jnp
import numpy as np
from jax import lax
from jax.experimental import pallas as pl
from jax.experimental.pallas import tpu as pltpu
from jax.sharding import PartitionSpec as P

F32, BF16 = jnp.float32, jnp.bfloat16
HEADS, HEAD_DIM = 12, 64
EPSILON = 1e-06
FAR = 1e12
LIMIT = 60 * 2**20
VMEM = pl.BlockSpec(memory_space=pltpu.VMEM)
SMEM = pl.BlockSpec(memory_space=pltpu.SMEM)


def nn(a, b):
    return lax.dot_general(a, b, (((1,), (0,)), ((), ())), preferred_element_type=F32)


def nt(a, b):
    return lax.dot_general(a, b, (((1,), (1,)), ((), ())), preferred_element_type=F32)


def tn(a, b):
    return lax.dot_general(a, b, (((0,), (0,)), ((), ())), preferred_element_type=F32)


def rows_loop(total, block, body):
    def step(i, _):
        body(pl.ds(pl.multiple_of(i * block, block), block))
        return 0

    lax.fori_loop(0, total // block, step, 0)


def centred(v):
    c = v - jnp.mean(v, axis=-1, keepdims=True)
    return c, lax.rsqrt(jnp.mean(c * c, axis=-1, keepdims=True) + EPSILON)


def norm_rows(src, gain, shift, dst):
    def body(rows):
        c, r = centred(src[rows, :].astype(F32))
        dst[rows, :] = (c * r * gain[...] + shift[...]).astype(BF16)

    rows_loop(src.shape[0], 128, body)


def norm_back_rows(v, gain, u):
    c, r = centred(v)
    hat = c * r
    w = u * gain
    dv = r * (
        w
        - jnp.mean(w, axis=-1, keepdims=True)
        - hat * jnp.mean(w * hat, axis=-1, keepdims=True)
    )
    return dv, jnp.sum(u * hat, axis=0, keepdims=True), jnp.sum(u, axis=0, keepdims=True)


def project(x, w, dst, scale=None):
    def body(cols):
        y = nt(x[...], w[cols, :])
        dst[:, cols] = (y if scale is None else y * scale).astype(BF16)

    rows_loop(w.shape[0], 256, body)


def fill_reach(table, columns, reach):
    def body(rows):
        col = columns[rows, :]
        down = (col[:, 1:2] - table[1:2, :]).astype(F32)
        across = (col[:, 2:3] - table[2:3, :]).astype(F32)
        same = col[:, 0:1] == table[0:1, :]
        reach[rows, :] = jnp.where(same, jnp.sqrt(down * down + across * across), FAR)

    rows_loop(reach.shape[0], 64, body)


def low_half(length):
    return lax.broadcasted_iota(jnp.int32, (length, 128), 1) < HEAD_DIM


def attend(q, k, v, reach, slope, mixed, lse, tick):
    lo = low_half(q.shape[0])

    def pair(hp, _):
        tick(hp)
        at = pl.ds(pl.multiple_of(hp * 128, 128), 128)
        qs, ks, vs = q[:, at], k[:, at], v[:, at]
        outs, tops = [], []
        for sub in range(2):
            mine = lo if sub == 0 else jnp.logical_not(lo)
            s = nt(jnp.where(mine, qs, jnp.zeros_like(qs)), ks)
            s = s + slope[2 * hp + sub] * reach[...]
            top = jnp.max(s, axis=-1, keepdims=True)
            e = jnp.exp(s - top).astype(BF16)
            outs.append(nn(e, jnp.where(mine, vs, jnp.ones_like(vs))))
            tops.append(top)
        num = jnp.where(lo, outs[0], outs[1])
        den = pltpu.roll(jnp.where(lo, outs[1], outs[0]), HEAD_DIM, 1)
        mixed[:, at] = (num / den).astype(BF16)
        lse_t = (jnp.where(lo, tops[0], tops[1]) + jnp.log(den)).T
        lse[hp] = jnp.concatenate([lse_t[0:1], lse_t[HEAD_DIM : HEAD_DIM + 1]], axis=0)
        return 0

    lax.fori_loop(0, q.shape[1] // 128, pair, 0)


def attend_back(q, k, v, up, mixed, lse, reach, slope, dq, dk, dv):
    lo = low_half(q.shape[0])

    def pair(hp, _):
        at = pl.ds(pl.multiple_of(hp * 128, 128), 128)
        qs, ks, vs, ups = q[:, at], k[:, at], v[:, at], up[:, at]
        prod = (ups.astype(F32) * mixed[:, at].astype(F32)).T
        tops = lse[hp]
        dqs, dks, dvs = [], [], []
        for sub in range(2):
            mine = lo if sub == 0 else jnp.logical_not(lo)
            delta = jnp.sum(prod[sub * HEAD_DIM : (sub + 1) * HEAD_DIM], axis=0, keepdims=True)
            s = nt(jnp.where(mine, ks, jnp.zeros_like(ks)), qs)
            p = jnp.exp(s + slope[2 * hp + sub] * reach[...] - tops[sub : sub + 1])
            dp = nt(jnp.where(mine, vs, jnp.zeros_like(vs)), ups)
            ds = (p * (dp - delta)).astype(BF16)
            dvs.append(nn(p.astype(BF16), ups))
            dks.append(nn(ds, qs))
            dqs.append(tn(ds, ks))
        dq[:, at] = (jnp.where(lo, dqs[0], dqs[1]) * HEAD_DIM**-0.5).astype(BF16)
        dk[:, at] = jnp.where(lo, dks[0], dks[1]).astype(BF16)
        dv[:, at] = jnp.where(lo, dvs[0], dvs[1]).astype(BF16)
        return 0

    lax.fori_loop(0, q.shape[1] // 128, pair, 0)


def add_out(base, mixed, w_out, bias, dst):
    def body(cols):
        y = nn(mixed[...], w_out[:, cols])
        dst[:, cols] = base[:, cols].astype(F32) + y + bias[:, cols]

    rows_loop(w_out.shape[1], 256, body)


def place_shards(full, place, at, keep, send):
    my, mx, mc = place[1], place[2], place[3]
    for x in range(2):
        for y in range(2):
            for c, dst in enumerate((keep, send)):
                row = (((y ^ my) * 2 + (x ^ mx)) * 2 + (c ^ mc)) * 96
                dst[x, y, at] = full[pl.ds(pl.multiple_of(row, 96), 96), :]


def feed_step(place, two, cot, gain, shift, w_in, b_in, w_out, b_out,
              merged, two_grad, keep_in, send_in, keep_out, send_out, bias_in, small,
              low, out, pull, full_in, full_out):
    step = pl.program_id(0)
    width = w_out.shape[0]
    block = 256

    @pl.when(step == 0)
    def _():
        norm_rows(two, gain, shift, low)

    for n in range(width // block):
        at = slice(n * block, (n + 1) * block)
        x = nn(low[...], w_in[:, at]) + b_in[:, at]
        inner = 0.7978845608028654 * x * (1.0 + 0.044715 * x * x)
        t = jnp.tanh(inner)
        half = 0.5 * (1.0 + t)
        hidden = (x * half).astype(BF16)
        slope = half + 0.5 * x * (1.0 - t * t) * (
            0.7978845608028654 * (1.0 + 3 * 0.044715 * x * x)
        )
        grad = (nt(cot[...], w_out[at, :]) * slope).astype(BF16)
        bias_in[0, :, at] = jnp.sum(grad.astype(F32), axis=0, keepdims=True)
        part_out = nn(hidden, w_out[at, :])
        part_pull = nt(grad, w_in[:, at])
        if n == 0:
            @pl.when(step == 0)
            def _():
                out[...] = part_out
                pull[...] = part_pull

            @pl.when(step > 0)
            def _():
                out[...] += part_out
                pull[...] += part_pull
        else:
            out[...] += part_out
            pull[...] += part_pull
        full_out[at, :] = tn(hidden, cot[...]).astype(BF16)
        full_in[at, :] = tn(grad, low[...]).astype(BF16)
    place_shards(full_in, place, 0, keep_in.at[:, :], send_in.at[:, :])
    place_shards(full_out, place, 0, keep_out.at[:, :], send_out.at[:, :])

    @pl.when(step == pl.num_programs(0) - 1)
    def _():
        small[...] = jnp.zeros_like(small)

        def body(rows):
            value, cotangent = two[rows, :], cot[rows, :].astype(F32)
            merged[rows, :] = (value + out[rows, :] + b_out[...]).astype(BF16)
            dv, dgain, dshift = norm_back_rows(value, gain[...], pull[rows, :])
            total = cotangent + dv
            two_grad[rows, :] = total
            small[0:1, :] += dgain
            small[1:2, :] += dshift
            small[2:3, :] += jnp.sum(cotangent, axis=0, keepdims=True)
            small[3:4, :] += jnp.sum(total, axis=0, keepdims=True)

        rows_loop(two.shape[0], 128, body)


def weight_grad(grads, rows, full):
    def body(cols):
        full[cols, :] = tn(grads[:, cols], rows[...]).astype(BF16)

    rows_loop(grads.shape[1], 256, body)


def attn_shards(full, place, mat, keep, send):
    my, mz = place[1], place[0]
    for x in range(2):
        for y in range(2):
            for c, dst in enumerate((keep, send)):
                row = ((x * 2 + c) * 2 + (y ^ my)) * 96
                dst[x, y, mat ^ mz] = full[pl.ds(pl.multiple_of(row, 96), 96), :]


def attention_back(place, grad, low, mixed, q, k, v, lse, reach, slope, x, y, w,
                   keep, send, full, up, dq, dk, dv):
    def cast(rows):
        low[rows, :] = grad[rows, :].astype(BF16)

    rows_loop(grad.shape[0], 128, cast)
    weight_grad(mixed, low, full)
    attn_shards(full, place, 3, keep, send)
    project(low, w.at[3], up)
    attend_back(q, k, v, up, mixed, lse, reach, slope, dq, dk, dv)
    for mat, (side, d) in enumerate(((x, dq), (y, dk), (y, dv))):
        weight_grad(d, side, full)
        attn_shards(full, place, mat, keep, send)


def cross_backward(place, two_grad, mixed, q, k, v, lse, reach, slope, radar_low, optical_low, w,
                   one, optical, gain_r, gain_o,
                   one_grad, optical_grad, keep, send, small,
                   low, full, up, dq, dk, dv):
    attention_back(place, two_grad, low, mixed, q, k, v, lse, reach, slope, radar_low, optical_low,
                   w, keep, send, full, up, dq, dk, dv)
    small[...] = jnp.zeros_like(small)

    def body(rows):
        pull = nn(dq[rows, :], w[0])
        dv_, dgain, dshift = norm_back_rows(one[rows, :], gain_r[...], pull)
        total = two_grad[rows, :] + dv_
        one_grad[rows, :] = total
        small[0:1, :] += dgain
        small[1:2, :] += dshift
        small[4:5, :] += jnp.sum(total, axis=0, keepdims=True)
        pull = nn(dk[rows, :], w[1]) + nn(dv[rows, :], w[2])
        dv_, dgain, dshift = norm_back_rows(optical[rows, :].astype(F32), gain_o[...], pull)
        optical_grad[rows, :] = dv_
        small[2:3, :] += dgain
        small[3:4, :] += dshift

    rows_loop(two_grad.shape[0], 256, body)


def self_backward(place, one_grad, mixed, q, k, v, lse, reach, slope, normed, w, radar, gain,
                  radar_grad, keep, send, small,
                  low, full, up, dq, dk, dv):
    attention_back(place, one_grad, low, mixed, q, k, v, lse, reach, slope, normed, normed,
                   w, keep, send, full, up, dq, dk, dv)
    small[...] = jnp.zeros_like(small)

    def body(rows):
        pull = nn(dq[rows, :], w[0]) + nn(dk[rows, :], w[1]) + nn(dv[rows, :], w[2])
        dv_, dgain, dshift = norm_back_rows(radar[rows, :].astype(F32), gain[...], pull)
        radar_grad[rows, :] = one_grad[rows, :] + dv_
        small[0:1, :] += dgain
        small[1:2, :] += dshift

    rows_loop(one_grad.shape[0], 256, body)


def shape(dims, dtype):
    return jax.ShapeDtypeStruct(dims, dtype)


CORE, X_BIT, Y_BIT, Z_NEAR, Z_FAR = 1, 2, 4, 8, 16


def partner(bit):
    dp, head = lax.axis_index("dp"), lax.axis_index("head")
    if bit < 4:
        return (dp, head ^ bit)
    return (dp ^ (bit // 4), head)


def greet(bits):
    barrier = pltpu.get_barrier_semaphore()
    for bit in bits:
        pl.semaphore_signal(
            barrier, inc=1, device_id=partner(bit), device_id_type=pl.DeviceIdType.MESH
        )
    pl.semaphore_wait(barrier, len(bits))


def send_to(bit, src, dst, send_sem, recv_sem):
    return pltpu.make_async_remote_copy(
        src_ref=src, dst_ref=dst, send_sem=send_sem, recv_sem=recv_sem,
        device_id=partner(bit), device_id_type=pl.DeviceIdType.MESH,
    )


class Gather:
    def __init__(self, w, send, recv):
        self.w, self.send, self.recv = w, send, recv
        self.mine = lax.axis_index("dp") % 2
        self.part = w.shape[1] // 4

    def copy(self, mat, kind):
        part, half = self.part, self.part // 2
        own = pl.ds(self.mine * half, half)
        far = pl.ds(2 * part + self.mine * half, half)
        other = pl.ds(2 * part + (1 - self.mine) * half, half)
        w = self.w.at[mat]
        up = lambda rows: pl.ds(rows.start + part, rows.size)
        bit, src, dst = (
            (CORE, pl.ds(0, part), pl.ds(part, part)),
            (X_BIT, own, far),
            (Y_BIT, far, far),
            (CORE, far, up(far)),
            (CORE, other, up(other)),
        )[kind]
        return send_to(bit, w.at[src], w.at[dst], self.send.at[mat, kind], self.recv.at[mat, kind])

    def begin(self, mat):
        self.copy(mat, 1).start()
        self.copy(mat, 0).start()

    def after_x(self, mat):
        self.copy(mat, 1).wait_recv()
        self.copy(mat, 2).start()
        self.copy(mat, 3).start()

    def after_y(self, mat):
        self.copy(mat, 2).wait_recv()
        self.copy(mat, 4).start()

    def ready(self, mat):
        for kind in (0, 3, 4):
            self.copy(mat, kind).wait_recv()

    def drain(self, mat):
        for kind in range(5):
            self.copy(mat, kind).wait_send()


def forward_body(remote, *refs):
    (radar, optical, gain_s, shift_s, gain_r, shift_r, gain_o, shift_o, bias_s, bias_c,
     table, columns, slope) = refs[:13]
    refs = refs[13:]
    if remote:
        owns, refs = refs[:8], refs[8:]
    else:
        w, refs = refs[0], refs[1:]
    if remote:
        w, refs = refs[0], refs[1:]
    (normed, radar_low, optical_low, sq, sk, sv, cq, ck, cv, s_mixed, c_mixed, s_lse, c_lse,
     two, one, reach) = refs[:16]
    if remote:
        hub = Gather(w, *refs[16:])
        part = w.shape[1] // 4
        greet((CORE, X_BIT, Y_BIT))
        for mat in range(8):
            w[mat, 0:part, :] = owns[mat][...]
            hub.begin(mat)

    def ready(mat):
        if remote:
            hub.ready(mat)

    def after_x(mat):
        if remote:
            hub.after_x(mat)

    def after_y(mat):
        if remote:
            hub.after_y(mat)

    norm_rows(radar, gain_s, shift_s, normed)
    after_x(0)
    fill_reach(table, columns, reach)
    after_x(1)
    after_y(0)
    norm_rows(optical, gain_o, shift_o, optical_low)
    after_x(2)
    after_y(1)
    ready(0)
    project(normed, w.at[0], sq, HEAD_DIM**-0.5)
    after_y(2)
    ready(1)
    project(normed, w.at[1], sk)
    after_x(3)
    ready(2)
    project(normed, w.at[2], sv)
    after_y(3)

    def tick(hp):
        if remote:
            @pl.when(hp < 4)
            def _():
                hub.after_x(hp + 4)

            @pl.when((hp > 0) & (hp < 5))
            def _():
                hub.after_y(hp + 3)

    attend(sq, sk, sv, reach, slope, s_mixed, s_lse, tick)
    ready(3)
    add_out(radar, s_mixed, w.at[3], bias_s, one)
    ready(5)
    project(optical_low, w.at[5], ck)
    ready(6)
    project(optical_low, w.at[6], cv)
    norm_rows(one, gain_r, shift_r, radar_low)
    ready(4)
    project(radar_low, w.at[4], cq, HEAD_DIM**-0.5)
    attend(cq, ck, cv, reach, slope, c_mixed, c_lse, lambda hp: None)
    ready(7)
    add_out(one, c_mixed, w.at[7], bias_c, two)
    if remote:
        for mat in range(8):
            hub.drain(mat)


def run_forward(remote, radar, optical, vectors, table, slope, weights):
    n, d = radar.shape
    low, lse, wide = shape((n, d), BF16), shape((6, 2, n), F32), shape((n, d), F32)
    outs = [low] * 11 + [lse, lse, wide, wide, shape((n, n), F32)]
    if remote:
        outs = [shape((8, d, d), BF16)] + outs
    return pl.pallas_call(
        functools.partial(forward_body, remote),
        out_shape=outs,
        in_specs=[VMEM] * 12 + [SMEM] + [VMEM] * len(weights),
        out_specs=[VMEM] * len(outs),
        scratch_shapes=[pltpu.SemaphoreType.DMA((8, 5))] * 2 if remote else [],
        compiler_params=pltpu.CompilerParams(
            vmem_limit_bytes=LIMIT, **(dict(collective_id=0, has_side_effects=True) if remote else {})
        ),
        name="forward",
        cost_estimate=pl.CostEstimate(flops=8 * 10**9, bytes_accessed=3 * 10**7, transcendentals=0),
    )(radar, optical, *vectors, table, table.T, slope, *weights)


def call(body, outs, scratch, operands, in_specs, **more):
    return pl.pallas_call(
        body,
        out_shape=outs,
        in_specs=in_specs,
        out_specs=[VMEM] * len(outs),
        scratch_shapes=scratch,
        compiler_params=pltpu.CompilerParams(vmem_limit_bytes=LIMIT),
        **more,
    )(*operands)


def run_feed(place, two, cot, gain, shift, w_in, b_in, w_out, b_out):
    n, d = two.shape
    f = w_in.shape[1]
    tile = 768
    whole = lambda *dims: pl.BlockSpec(dims, lambda i, p: (0,) * len(dims))
    slots = pl.BlockSpec((2, 2, 1, 96, d), lambda i, p: (0, 0, i ^ p[0], 0, 0))
    grad = shape((2, 2, 4, 96, d), BF16)
    return pl.pallas_call(
        feed_step,
        grid_spec=pltpu.PrefetchScalarGridSpec(
            num_scalar_prefetch=1,
            grid=(f // tile,),
            in_specs=[
                whole(n, d), whole(n, d), whole(1, d), whole(1, d),
                pl.BlockSpec((d, tile), lambda i, p: (0, i)),
                pl.BlockSpec((1, tile), lambda i, p: (0, i)),
                pl.BlockSpec((tile, d), lambda i, p: (i, 0)),
                whole(1, d),
            ],
            out_specs=[
                whole(n, d), whole(n, d), slots, slots, slots, slots,
                pl.BlockSpec((1, 1, tile), lambda i, p: (i, 0, 0)),
                whole(8, d),
            ],
            scratch_shapes=[
                pltpu.VMEM((n, d), BF16), pltpu.VMEM((n, d), F32), pltpu.VMEM((n, d), F32),
                pltpu.VMEM((tile, d), BF16), pltpu.VMEM((tile, d), BF16),
            ],
        ),
        out_shape=[
            shape((n, d), BF16), shape((n, d), F32), grad, grad, grad, grad,
            shape((f // tile, 1, tile), F32), shape((8, d), F32),
        ],
        compiler_params=pltpu.CompilerParams(vmem_limit_bytes=LIMIT),
        name="feed",
        cost_estimate=pl.CostEstimate(flops=15 * 10**9, bytes_accessed=25 * 10**6, transcendentals=0),
    )(place, two, cot, gain, shift, w_in, b_in, w_out, b_out)


def back_scratch(n, d):
    low = pltpu.VMEM((n, d), BF16)
    return [low, pltpu.VMEM((d, d), BF16), low, low, low, low]


def run_cross_backward(place, two_grad, mixed, q, k, v, lse, reach, slope, radar_low, optical_low,
                       w, one, optical, gain_r, gain_o):
    n, d = one.shape
    grad = shape((2, 2, 4, 96, d), BF16)
    wide = shape((n, d), F32)
    return call(
        cross_backward,
        [wide, wide, grad, grad, shape((8, d), F32)],
        back_scratch(n, d),
        (place, two_grad, mixed, q, k, v, lse, reach, slope, radar_low, optical_low,
         w, one, optical, gain_r, gain_o),
        [SMEM] + [VMEM] * 7 + [SMEM] + [VMEM] * 7,
        name="cross_backward",
        cost_estimate=pl.CostEstimate(flops=12 * 10**9, bytes_accessed=25 * 10**6, transcendentals=0),
    )


def run_self_backward(place, one_grad, mixed, q, k, v, lse, reach, slope, normed, w, radar, gain):
    n, d = one_grad.shape
    grad = shape((2, 2, 4, 96, d), BF16)
    return call(
        self_backward,
        [shape((n, d), F32), grad, grad, shape((8, d), F32)],
        back_scratch(n, d),
        (place, one_grad, mixed, q, k, v, lse, reach, slope, normed, w, radar, gain),
        [SMEM] + [VMEM] * 7 + [SMEM] + [VMEM] * 4,
        name="self_backward",
        cost_estimate=pl.CostEstimate(flops=12 * 10**9, bytes_accessed=25 * 10**6, transcendentals=0),
    )


def finish(place, got, dq, dk, dv, do):
    for mat, dst in enumerate((dq, dk, dv, do)):
        rows = [got[h ^ place[1], mat ^ place[0]].astype(F32) for h in range(2)]
        dst[0:96, :] = rows[0]
        dst[96:192, :] = rows[1]


def run_finish(place, got):
    d = got.shape[-1]
    q, k, v, o = call(
        finish, [shape((192, d), F32)] * 4, [], (place, got), [SMEM, VMEM], name="finish"
    )
    return q.T, k.T, v.T, o


def swap(v, bit):
    return lax.ppermute(v, ("dp", "head"), [(i, i ^ bit) for i in range(32)])


def add(a, b):
    return (a.astype(F32) + b.astype(F32)).astype(BF16)


def halves(v, axis):
    return lax.index_in_dim(v, 0, axis, False), lax.index_in_dim(v, 1, axis, False)


def scatter_sum(keep, send, x_first):
    keep = keep.reshape(2, 2, 2, 2, 96, -1)
    got = swap(send.reshape(keep.shape), CORE)
    order = [(X_BIT, 0), (Y_BIT, 0)] if x_first else [(Y_BIT, 1), (X_BIT, 0)]
    for bit, axis in order + [(Z_NEAR, 1), (Z_FAR, 0)]:
        k0, k1 = halves(keep, axis)
        g0, g1 = halves(got, axis)
        got = swap(add(k1, g1), bit)
        keep = add(k0, g0)
    return keep.astype(F32) + got.astype(F32)


def gather_sums(own):
    own = own.astype(BF16)
    both = jnp.stack([own, swap(own, Z_FAR)])
    both = jnp.stack([both, swap(both, Z_NEAR)], axis=1).reshape(4, 96, -1)
    return jnp.stack([both, swap(both, Y_BIT)])


def shards(
    radar, optical, patch_table, cotangent, norm_self_gain, norm_self_shift,
    self_query, self_key, self_value, self_out, self_out_bias, norm_radar_gain, norm_radar_shift,
    norm_optical_gain, norm_optical_shift, cross_query, cross_key, cross_value, cross_out,
    cross_out_bias, norm_feed_gain, norm_feed_shift, feed_in, feed_in_bias, feed_out, feed_out_bias,
):
    dp, head = lax.axis_size("dp"), lax.axis_size("head")
    near = (dp, head) == (8, 4)
    row = lambda v: v.reshape(1, -1)
    zero = jnp.int32(0)
    if near:
        mine = lax.axis_index("dp") * 4 + lax.axis_index("head")
        place = jnp.stack([mine // 8, mine // 4 % 2, mine // 2 % 2, mine % 2]).astype(jnp.int32)
        group = jnp.arange(4, dtype=jnp.int32) ^ lax.axis_index("head")
    else:
        place = jnp.stack([zero] * 4)
        group = jnp.arange(head, dtype=jnp.int32)
    per = HEADS // head
    heads = (group[:, None] * per + jnp.arange(per, dtype=jnp.int32)[None, :]).reshape(-1)
    slope = -jnp.exp2(-8.0 * (heads + 1).astype(F32) / HEADS)
    weights = (self_query, self_key, self_value, self_out,
               cross_query, cross_key, cross_value, cross_out)
    weights = tuple(w if i % 4 == 3 else w.T for i, w in enumerate(weights))
    if not near:
        w = lax.all_gather(jnp.stack(weights), "head", axis=1, tiled=True)
        weights = (w,)
    vectors = [row(v) for v in (
        norm_self_gain, norm_self_shift, norm_radar_gain, norm_radar_shift,
        norm_optical_gain, norm_optical_shift, self_out_bias, cross_out_bias)]
    got = run_forward(near, radar, optical, vectors, patch_table, slope, weights)
    if near:
        w, got = got[0], got[1:]
    (normed, radar_low, optical_low, sq, sk, sv, cq, ck, cv, s_mixed, c_mixed, s_lse, c_lse,
     two, one, reach) = got
    merged, two_grad, in_keep, in_send, out_keep, out_send, bias_in, feed_small = run_feed(
        place, two, cotangent, row(norm_feed_gain), row(norm_feed_shift),
        feed_in, row(feed_in_bias), feed_out, row(feed_out_bias),
    )
    one_grad, optical_grad, cross_keep, cross_send, cross_small = run_cross_backward(
        place, two_grad, c_mixed, cq, ck, cv, c_lse, reach, slope, radar_low, optical_low,
        w[4:], one, optical, row(norm_radar_gain), row(norm_optical_gain),
    )
    radar_grad, self_keep, self_send, self_small = run_self_backward(
        place, one_grad, s_mixed, sq, sk, sv, s_lse, reach, slope, normed,
        w[:4], radar, row(norm_self_gain),
    )
    d = radar.shape[1]
    small = jnp.concatenate([feed_small, cross_small, self_small, bias_in.reshape(-1, d)])
    if near:
        feed_in_grad = scatter_sum(in_keep, in_send, True)
        feed_out_grad = scatter_sum(out_keep, out_send, False)
        cross = gather_sums(scatter_sum(cross_keep, cross_send, True))
        own = gather_sums(scatter_sum(self_keep, self_send, True))
        cross, own = run_finish(place, cross), run_finish(place, own)
        for bit in (CORE, X_BIT, Y_BIT, Z_NEAR, Z_FAR):
            small = small + swap(small, bit)
    else:
        def logical(keep, send, order):
            both = jnp.stack([keep, send])
            return jnp.transpose(both, order).reshape(-1, d)

        def feed_sum(keep, send):
            return lax.psum_scatter(
                logical(keep, send, (3, 2, 1, 0, 4, 5)).astype(F32),
                ("dp", "head"), scatter_dimension=0, tiled=True,
            )

        def attn_sum(keep, send):
            total = logical(keep, send, (3, 1, 0, 2, 4, 5)).astype(F32).reshape(4, -1, d)
            total = lax.psum_scatter(total, "head", scatter_dimension=1, tiled=True)
            total = lax.psum(total, "dp")
            return total[0].T, total[1].T, total[2].T, total[3]

        feed_in_grad, feed_out_grad = feed_sum(in_keep, in_send), feed_sum(out_keep, out_send)
        cross, own = attn_sum(cross_keep, cross_send), attn_sum(self_keep, self_send)
        small = lax.psum(small, ("dp", "head"))
    bias_part = feed_in_bias.shape[0] // (dp * head)
    feed_in_bias_grad = lax.dynamic_slice_in_dim(
        small[24:28].reshape(-1),
        (lax.axis_index("dp") * head + lax.axis_index("head")) * bias_part,
        bias_part,
    )
    return (
        merged, radar_grad, optical_grad,
        small[16], small[17], *own, small[12],
        small[8], small[9], small[10], small[11], *cross, small[3],
        small[0], small[1], feed_in_grad.T, feed_in_bias_grad, feed_out_grad, small[2],
    )


def solution(mesh):
    token, rep = P(("dp", "head"), None), P()
    col, row = P(None, "head"), P("head", None)
    in_specs = (
        token, token, P(None, ("dp", "head")), token,
        rep, rep, col, col, col, row, rep,
        rep, rep, rep, rep, col, col, col, row, rep,
        rep, rep, rep, rep, rep, rep,
    )
    out_specs = (
        token, token, token,
        rep, rep, col, col, col, row, rep,
        rep, rep, rep, rep, col, col, col, row, rep,
        rep, rep, P(None, ("dp", "head")), P(("dp", "head")), token, rep,
    )
    return jax.shard_map(shards, mesh=mesh, in_specs=in_specs, out_specs=out_specs, check_vma=False)
```

```python
import functools

import jax
import jax.numpy as jnp
import numpy as np
from jax import lax
from jax.experimental import pallas as pl
from jax.experimental.pallas import tpu as pltpu
from jax.sharding import PartitionSpec as P

F32, BF16 = jnp.float32, jnp.bfloat16
HEADS, HEAD_DIM = 12, 64
EPSILON = 1e-06
FAR = 1e12
LIMIT = 60 * 2**20
VMEM = pl.BlockSpec(memory_space=pltpu.VMEM)
SMEM = pl.BlockSpec(memory_space=pltpu.SMEM)


def nn(a, b):
    return lax.dot_general(a, b, (((1,), (0,)), ((), ())), preferred_element_type=F32)


def nt(a, b):
    return lax.dot_general(a, b, (((1,), (1,)), ((), ())), preferred_element_type=F32)


def tn(a, b):
    return lax.dot_general(a, b, (((0,), (0,)), ((), ())), preferred_element_type=F32)


def rows_loop(total, block, body):
    def step(i, _):
        body(pl.ds(pl.multiple_of(i * block, block), block))
        return 0

    lax.fori_loop(0, total // block, step, 0)


def centred(v):
    c = v - jnp.mean(v, axis=-1, keepdims=True)
    return c, lax.rsqrt(jnp.mean(c * c, axis=-1, keepdims=True) + EPSILON)


def norm_rows(src, gain, shift, dst):
    def body(rows):
        c, r = centred(src[rows, :].astype(F32))
        dst[rows, :] = (c * r * gain[...] + shift[...]).astype(BF16)

    rows_loop(src.shape[0], 128, body)


def norm_back_rows(v, gain, u):
    c, r = centred(v)
    hat = c * r
    w = u * gain
    dv = r * (
        w
        - jnp.mean(w, axis=-1, keepdims=True)
        - hat * jnp.mean(w * hat, axis=-1, keepdims=True)
    )
    return dv, jnp.sum(u * hat, axis=0, keepdims=True), jnp.sum(u, axis=0, keepdims=True)


def project(x, w, dst, scale=None):
    def body(cols):
        y = nt(x[...], w[cols, :])
        dst[:, cols] = (y if scale is None else y * scale).astype(BF16)

    rows_loop(w.shape[0], 256, body)


def fill_reach(table, columns, reach):
    for i in range(3):
        line = table[i : i + 1, :].astype(F32)
        columns[i] = jnp.broadcast_to(line, (128, line.shape[1])).T

    def body(rows):
        seg, down, across = (
            columns[i, rows, 0:1] - table[i : i + 1, :].astype(F32) for i in range(3)
        )
        reach[rows, :] = jnp.where(seg == 0, jnp.sqrt(down * down + across * across), FAR)

    rows_loop(reach.shape[0], 64, body)


def low_half(length):
    return lax.broadcasted_iota(jnp.int32, (length, 128), 1) < HEAD_DIM


def attend(q, k, v, reach, slope, mixed, lse, tick):
    lo = low_half(q.shape[0])

    def pair(hp, _):
        tick(hp)
        at = pl.ds(pl.multiple_of(hp * 128, 128), 128)
        qs, ks, vs = q[:, at], k[:, at], v[:, at]
        outs, tops = [], []
        for sub in range(2):
            mine = lo if sub == 0 else jnp.logical_not(lo)
            s = nt(jnp.where(mine, qs, jnp.zeros_like(qs)), ks)
            s = s + slope[2 * hp + sub] * reach[...]
            top = jnp.max(s, axis=-1, keepdims=True)
            e = jnp.exp(s - top).astype(BF16)
            outs.append(nn(e, jnp.where(mine, vs, jnp.ones_like(vs))))
            tops.append(top)
        num = jnp.where(lo, outs[0], outs[1])
        den = pltpu.roll(jnp.where(lo, outs[1], outs[0]), HEAD_DIM, 1)
        mixed[:, at] = (num / den).astype(BF16)
        lse_t = (jnp.where(lo, tops[0], tops[1]) + jnp.log(den)).T
        lse[hp] = jnp.concatenate([lse_t[0:1], lse_t[HEAD_DIM : HEAD_DIM + 1]], axis=0)
        return 0

    lax.fori_loop(0, q.shape[1] // 128, pair, 0)


def attend_back(q, k, v, up, mixed, lse, reach, slope, dq, dk, dv, tick=lambda hp: None):
    lo = low_half(q.shape[0])

    def pair(hp, _):
        tick(hp)
        at = pl.ds(pl.multiple_of(hp * 128, 128), 128)
        qs, ks, vs, ups = q[:, at], k[:, at], v[:, at], up[:, at]
        prod = (ups.astype(F32) * mixed[:, at].astype(F32)).T
        tops = lse[hp]
        dqs, dks, dvs = [], [], []
        for sub in range(2):
            mine = lo if sub == 0 else jnp.logical_not(lo)
            delta = jnp.sum(prod[sub * HEAD_DIM : (sub + 1) * HEAD_DIM], axis=0, keepdims=True)
            s = nt(jnp.where(mine, ks, jnp.zeros_like(ks)), qs)
            p = jnp.exp(s + slope[2 * hp + sub] * reach[...] - tops[sub : sub + 1])
            dp = nt(jnp.where(mine, vs, jnp.zeros_like(vs)), ups)
            ds = (p * (dp - delta)).astype(BF16)
            dvs.append(nn(p.astype(BF16), ups))
            dks.append(nn(ds, qs))
            dqs.append(tn(ds, ks))
        dq[:, at] = (jnp.where(lo, dqs[0], dqs[1]) * HEAD_DIM**-0.5).astype(BF16)
        dk[:, at] = jnp.where(lo, dks[0], dks[1]).astype(BF16)
        dv[:, at] = jnp.where(lo, dvs[0], dvs[1]).astype(BF16)
        return 0

    lax.fori_loop(0, q.shape[1] // 128, pair, 0)


def add_out(base, mixed, w_out, bias, dst):
    def body(cols):
        y = nn(mixed[...], w_out[:, cols])
        dst[:, cols] = base[:, cols].astype(F32) + y + bias[:, cols]

    rows_loop(w_out.shape[1], 256, body)


def place_shards(full, place, at, keep, send):
    my, mx, mc = place[1], place[2], place[3]
    for x in range(2):
        for y in range(2):
            for c, dst in enumerate((keep, send)):
                row = (((y ^ my) * 2 + (x ^ mx)) * 2 + (c ^ mc)) * 96
                dst[x, y, at] = full[pl.ds(pl.multiple_of(row, 96), 96), :]


def feed_step(place, two, cot, gain, shift, w_in, b_in, w_out, b_out,
              merged, two_grad, keep_in, send_in, keep_out, send_out, bias_in, small,
              low, out, pull, full_in, full_out):
    step = pl.program_id(0)
    width = w_out.shape[0]
    block = 256

    @pl.when(step == 0)
    def _():
        norm_rows(two, gain, shift, low)

    for n in range(width // block):
        at = slice(n * block, (n + 1) * block)
        x = nn(low[...], w_in[:, at]) + b_in[:, at]
        inner = 0.7978845608028654 * x * (1.0 + 0.044715 * x * x)
        t = jnp.tanh(inner)
        half = 0.5 * (1.0 + t)
        hidden = (x * half).astype(BF16)
        slope = half + 0.5 * x * (1.0 - t * t) * (
            0.7978845608028654 * (1.0 + 3 * 0.044715 * x * x)
        )
        grad = (nt(cot[...], w_out[at, :]) * slope).astype(BF16)
        bias_in[0, :, at] = jnp.sum(grad.astype(F32), axis=0, keepdims=True)
        part_out = nn(hidden, w_out[at, :])
        part_pull = nt(grad, w_in[:, at])
        if n == 0:
            @pl.when(step == 0)
            def _():
                out[...] = part_out
                pull[...] = part_pull

            @pl.when(step > 0)
            def _():
                out[...] += part_out
                pull[...] += part_pull
        else:
            out[...] += part_out
            pull[...] += part_pull
        full_out[at, :] = tn(hidden, cot[...]).astype(BF16)
        full_in[at, :] = tn(grad, low[...]).astype(BF16)
    place_shards(full_in, place, 0, keep_in.at[:, :], send_in.at[:, :])
    place_shards(full_out, place, 0, keep_out.at[:, :], send_out.at[:, :])

    @pl.when(step == pl.num_programs(0) - 1)
    def _():
        small[...] = jnp.zeros_like(small)

        def body(rows):
            value, cotangent = two[rows, :], cot[rows, :].astype(F32)
            merged[rows, :] = (value + out[rows, :] + b_out[...]).astype(BF16)
            dv, dgain, dshift = norm_back_rows(value, gain[...], pull[rows, :])
            total = cotangent + dv
            two_grad[rows, :] = total
            small[0:1, :] += dgain
            small[1:2, :] += dshift
            small[2:3, :] += jnp.sum(cotangent, axis=0, keepdims=True)
            small[3:4, :] += jnp.sum(total, axis=0, keepdims=True)

        rows_loop(two.shape[0], 128, body)


def weight_grad(grads, rows, full):
    def body(cols):
        full[cols, :] = tn(grads[:, cols], rows[...]).astype(BF16)

    rows_loop(grads.shape[1], 256, body)


def attn_shards(full, place, mat, keep, send):
    my, mz = place[1], place[0]
    for x in range(2):
        for y in range(2):
            for c, dst in enumerate((keep, send)):
                row = ((x * 2 + c) * 2 + (y ^ my)) * 96
                dst[x, y, mat ^ mz] = full[pl.ds(pl.multiple_of(row, 96), 96), :]


def attention_back(place, grad, low, mixed, q, k, v, lse, reach, slope, x, y, w,
                   keep, send, full, up, dq, dk, dv):
    def cast(rows):
        low[rows, :] = grad[rows, :].astype(BF16)

    rows_loop(grad.shape[0], 128, cast)
    weight_grad(mixed, low, full)
    attn_shards(full, place, 3, keep, send)
    project(low, w.at[3], up)
    attend_back(q, k, v, up, mixed, lse, reach, slope, dq, dk, dv)
    for mat, (side, d) in enumerate(((x, dq), (y, dk), (y, dv))):
        weight_grad(d, side, full)
        attn_shards(full, place, mat, keep, send)


def cross_backward(place, two_grad, mixed, q, k, v, lse, reach, slope, radar_low, optical_low, w,
                   one, optical, gain_r, gain_o,
                   one_grad, optical_grad, keep, send, small,
                   low, full, up, dq, dk, dv):
    attention_back(place, two_grad, low, mixed, q, k, v, lse, reach, slope, radar_low, optical_low,
                   w, keep, send, full, up, dq, dk, dv)
    small[...] = jnp.zeros_like(small)

    def body(rows):
        pull = nn(dq[rows, :], w[0])
        dv_, dgain, dshift = norm_back_rows(one[rows, :], gain_r[...], pull)
        total = two_grad[rows, :] + dv_
        one_grad[rows, :] = total
        small[0:1, :] += dgain
        small[1:2, :] += dshift
        small[4:5, :] += jnp.sum(total, axis=0, keepdims=True)
        pull = nn(dk[rows, :], w[1]) + nn(dv[rows, :], w[2])
        dv_, dgain, dshift = norm_back_rows(optical[rows, :].astype(F32), gain_o[...], pull)
        optical_grad[rows, :] = dv_
        small[2:3, :] += dgain
        small[3:4, :] += dshift

    rows_loop(two_grad.shape[0], 256, body)


def self_backward(place, one_grad, mixed, q, k, v, lse, reach, slope, normed, w, radar, gain,
                  radar_grad, keep, send, small,
                  low, full, up, dq, dk, dv):
    attention_back(place, one_grad, low, mixed, q, k, v, lse, reach, slope, normed, normed,
                   w, keep, send, full, up, dq, dk, dv)
    small[...] = jnp.zeros_like(small)

    def body(rows):
        pull = nn(dq[rows, :], w[0]) + nn(dk[rows, :], w[1]) + nn(dv[rows, :], w[2])
        dv_, dgain, dshift = norm_back_rows(radar[rows, :].astype(F32), gain[...], pull)
        radar_grad[rows, :] = one_grad[rows, :] + dv_
        small[0:1, :] += dgain
        small[1:2, :] += dshift

    rows_loop(one_grad.shape[0], 256, body)


def shape(dims, dtype):
    return jax.ShapeDtypeStruct(dims, dtype)


CORE, X_BIT, Y_BIT, Z_NEAR, Z_FAR = 1, 2, 4, 8, 16


def partner(bit):
    dp, head = lax.axis_index("dp"), lax.axis_index("head")
    if bit < 4:
        return (dp, head ^ bit)
    return (dp ^ (bit // 4), head)


def greet(bits):
    barrier = pltpu.get_barrier_semaphore()
    for bit in bits:
        pl.semaphore_signal(
            barrier, inc=1, device_id=partner(bit), device_id_type=pl.DeviceIdType.MESH
        )
    pl.semaphore_wait(barrier, len(bits))


def send_to(bit, src, dst, send_sem, recv_sem):
    return pltpu.make_async_remote_copy(
        src_ref=src, dst_ref=dst, send_sem=send_sem, recv_sem=recv_sem,
        device_id=partner(bit), device_id_type=pl.DeviceIdType.MESH,
    )


class Gather:
    def __init__(self, w, send, recv):
        self.w, self.send, self.recv = w, send, recv
        self.mine = lax.axis_index("dp") % 2
        self.part = w.shape[1] // 4

    def copy(self, mat, kind):
        part, half = self.part, self.part // 2
        own = pl.ds(self.mine * half, half)
        far = pl.ds(2 * part + self.mine * half, half)
        other = pl.ds(2 * part + (1 - self.mine) * half, half)
        w = self.w.at[mat]
        up = lambda rows: pl.ds(rows.start + part, rows.size)
        bit, src, dst = (
            (CORE, pl.ds(0, part), pl.ds(part, part)),
            (X_BIT, own, far),
            (Y_BIT, far, far),
            (CORE, far, up(far)),
            (CORE, other, up(other)),
        )[kind]
        return send_to(bit, w.at[src], w.at[dst], self.send.at[mat, kind], self.recv.at[mat, kind])

    def begin(self, mat):
        self.copy(mat, 1).start()
        self.copy(mat, 0).start()

    def after_x(self, mat):
        self.copy(mat, 1).wait_recv()
        self.copy(mat, 2).start()
        self.copy(mat, 3).start()

    def after_y(self, mat):
        self.copy(mat, 2).wait_recv()
        self.copy(mat, 4).start()

    def ready(self, mat):
        for kind in (0, 3, 4):
            self.copy(mat, kind).wait_recv()

    def drain(self, mat):
        for kind in range(5):
            self.copy(mat, kind).wait_send()


def forward_body(remote, *refs):
    (radar, optical, vectors, table, slope) = refs[:5]
    gain_s, shift_s, gain_r, shift_r, gain_o, shift_o, bias_s, bias_c = (
        vectors.at[i : i + 1, :] for i in range(8)
    )
    refs, columns = refs[5:-1], refs[-1]
    if remote:
        owns, refs = refs[:8], refs[8:]
    else:
        w, refs = refs[0], refs[1:]
    if remote:
        w, refs = refs[0], refs[1:]
    (normed, radar_low, optical_low, sq, sk, sv, cq, ck, cv, s_mixed, c_mixed, s_lse, c_lse,
     two, one, reach) = refs[:16]
    if remote:
        hub = Gather(w, *refs[16:])
        part = w.shape[1] // 4
        greet((CORE, X_BIT, Y_BIT))
        for mat in range(8):
            w[mat, 0:part, :] = owns[mat][...]
            hub.begin(mat)

    def ready(mat):
        if remote:
            hub.ready(mat)

    def after_x(mat):
        if remote:
            hub.after_x(mat)

    def after_y(mat):
        if remote:
            hub.after_y(mat)

    norm_rows(radar, gain_s, shift_s, normed)
    after_x(0)
    fill_reach(table, columns, reach)
    after_x(1)
    after_y(0)
    norm_rows(optical, gain_o, shift_o, optical_low)
    after_x(2)
    after_y(1)
    ready(0)
    project(normed, w.at[0], sq, HEAD_DIM**-0.5)
    after_y(2)
    ready(1)
    project(normed, w.at[1], sk)
    after_x(3)
    ready(2)
    project(normed, w.at[2], sv)
    after_y(3)

    def tick(hp):
        if remote:
            @pl.when(hp < 4)
            def _():
                hub.after_x(hp + 4)

            @pl.when((hp > 0) & (hp < 5))
            def _():
                hub.after_y(hp + 3)

    attend(sq, sk, sv, reach, slope, s_mixed, s_lse, tick)
    ready(3)
    add_out(radar, s_mixed, w.at[3], bias_s, one)
    ready(5)
    project(optical_low, w.at[5], ck)
    ready(6)
    project(optical_low, w.at[6], cv)
    norm_rows(one, gain_r, shift_r, radar_low)
    ready(4)
    project(radar_low, w.at[4], cq, HEAD_DIM**-0.5)
    attend(cq, ck, cv, reach, slope, c_mixed, c_lse, lambda hp: None)
    ready(7)
    add_out(one, c_mixed, w.at[7], bias_c, two)
    if remote:
        for mat in range(8):
            hub.drain(mat)


def run_forward(remote, radar, optical, vectors, table, slope, weights):
    n, d = radar.shape
    low, lse, wide = shape((n, d), BF16), shape((6, 2, n), F32), shape((n, d), F32)
    outs = [low] * 11 + [lse, lse, wide, wide, shape((n, n), F32)]
    if remote:
        outs = [shape((8, d, d), BF16)] + outs
    return pl.pallas_call(
        functools.partial(forward_body, remote),
        out_shape=outs,
        in_specs=[VMEM] * 4 + [SMEM] + [VMEM] * len(weights),
        out_specs=[VMEM] * len(outs),
        scratch_shapes=([pltpu.SemaphoreType.DMA((8, 5))] * 2 if remote else [])
        + [pltpu.VMEM((3, n, 128), F32)],
        compiler_params=pltpu.CompilerParams(
            vmem_limit_bytes=LIMIT, **(dict(collective_id=0, has_side_effects=True) if remote else {})
        ),
        name="forward",
        cost_estimate=pl.CostEstimate(flops=8 * 10**9, bytes_accessed=3 * 10**7, transcendentals=0),
    )(radar, optical, vectors, table, slope, *weights)


X_FIRST = (X_BIT, Y_BIT)
Y_FIRST = (Y_BIT, X_BIT)
PATHS = {
    "A": (X_FIRST,) * 4,
    "C": (Y_FIRST,) * 4,
    "S": (X_FIRST, X_FIRST, Y_FIRST, X_FIRST),
}
PLANE = (3, 0, 1, 2)
FIRST_SLOT = {"A": 0, "B": 4, "C": 0, "S": 4}
FIRST_BACK = {"A": 0, "C": 4, "S": 8}
UNIT = {"A": 0, "B": 1, "C": 2, "S": 3}


class Sums:
    def __init__(self, refs):
        (self.g, self.rc, self.r1, self.r2, self.rn, self.zb, self.rz, self.rf, self.all,
         self.cs, self.cr, self.s1, self.q1, self.s2, self.q2, self.sn, self.qn,
         self.sz, self.qz, self.sf, self.qf, self.sa, self.qa,
         self.sm, self.sq, self.ss, self.sr) = refs
        dp, head = lax.axis_index("dp"), lax.axis_index("head")
        self.mc, self.mx, self.my = head % 2, head // 2, dp % 2
        self.z0, self.z1 = dp // 2 % 2, dp // 4
        self.place = {X_BIT: self.mx, Y_BIT: self.my}

    def bits(self, unit, bit):
        if unit in "CS" and bit != Y_BIT:
            return 0
        return self.mc if bit == CORE else self.place[bit]

    def path(self, unit, j):
        return X_FIRST if unit == "B" else PATHS[unit][j]

    def shard_at(self, unit, j, t):
        if unit in "AB":
            y, x, c = t // 4, t // 2 % 2, t % 2
        else:
            x, c, y = t // 4, t // 2 % 2, t % 2
        where = {X_BIT: x, Y_BIT: y}
        first, second = self.path(unit, j)
        return c * 4 + where[first] * 2 + where[second]

    def put(self, unit, j, slot, row, value):
        end = row + value.shape[0]
        at = row
        while at < end:
            t = at // 96
            stop = min(end, (t + 1) * 96)
            self.g[slot, self.shard_at(unit, j, t), at - t * 96 : stop - t * 96, :] = value[
                at - row : stop - row
            ].astype(BF16)
            at = stop

    def merge(self, dst, src, at, add, count):
        def body(i, _):
            rows = pl.ds(pl.multiple_of(i % 3 * 32, 32), 32)
            k = i // 3
            total = src[at + k, rows, :].astype(F32) + add[k, rows, :].astype(F32)
            dst[at + k, rows, :] = total.astype(BF16)
            return 0

        lax.fori_loop(0, count * 3, body, 0)

    def core_copy(self, unit, slot):
        other = 4 * (1 - self.bits(unit, CORE))
        return send_to(
            CORE, self.g.at[slot, pl.ds(other, 4)], self.rc.at[slot],
            self.cs.at[slot], self.cr.at[slot],
        )

    def first_copy(self, unit, j, slot, back):
        first = self.path(unit, j)[0]
        keep = self.bits(unit, first)
        base = 4 * self.bits(unit, CORE)
        copy = send_to(
            first, self.g.at[slot, pl.ds(base + 2 * (1 - keep), 2)], self.r1.at[back],
            self.s1.at[back], self.q1.at[back],
        )
        return copy, base + 2 * keep

    def second_copy(self, unit, j, slot, back):
        first, second = self.path(unit, j)
        base = 4 * self.bits(unit, CORE) + 2 * self.bits(unit, first)
        keep = self.bits(unit, second)
        copy = send_to(
            second, self.g.at[slot, pl.ds(base + 1 - keep, 1)], self.r2.at[back],
            self.s2.at[back], self.q2.at[back],
        )
        return copy, base + keep

    def begin(self, unit, j):
        self.core_copy(unit, FIRST_SLOT[unit] + j).start()

    def near_copy(self, p):
        slot = 4 + 2 * p + 1 - self.z0
        base = 4 * self.mc
        return send_to(
            Z_NEAR, self.g.at[slot, pl.ds(base, 4)], self.rn.at[p], self.sn.at[p], self.qn.at[p]
        )

    def slots(self, unit, j):
        if unit == "B":
            return 4 + 2 * j + self.z0, 12 + j
        return FIRST_SLOT[unit] + j, FIRST_BACK[unit] + j

    def event(self, kind, unit, j):
        if kind == "1":
            slot = FIRST_SLOT[unit] + j
            self.core_copy(unit, slot).wait()
            g, base = self.g.at[slot], 4 * self.bits(unit, CORE)
            if unit == "B":
                self.merge(g, g, base, self.rc.at[slot], 4)
                if j % 2:
                    self.near_copy(j // 2).start()
                return
            copy, keep = self.first_copy(unit, j, slot, FIRST_BACK[unit] + j)
            other = base + 2 * (1 - self.bits(unit, self.path(unit, j)[0]))
            self.merge(g, g, other, self.rc.at[slot, pl.ds(other - base, 2)], 2)
            copy.start()
            self.merge(g, g, keep, self.rc.at[slot, pl.ds(keep - base, 2)], 2)
        elif kind == "n":
            slot, back = self.slots("B", j)
            self.near_copy(j).wait()
            base = 4 * self.mc
            self.merge(self.g.at[slot], self.g.at[slot], base, self.rn.at[j], 4)
            self.first_copy("B", j, slot, back)[0].start()
        elif kind == "2":
            slot, back = self.slots(unit, j)
            copy, keep = self.first_copy(unit, j, slot, back)
            copy.wait()
            self.merge(self.g.at[slot], self.g.at[slot], keep, self.r1.at[back], 2)
            self.second_copy(unit, j, slot, back)[0].start()
        elif kind == "3":
            slot, back = self.slots(unit, j)
            copy, keep = self.second_copy(unit, j, slot, back)
            copy.wait()
            u = UNIT[unit]
            if unit == "B":
                z = 2 * self.z0 + j
            else:
                plane = j if unit == "A" else PLANE[j]
                z = (plane % 2) * 2 + plane // 2
            for i in range(3):
                rows = slice(32 * i, 32 * i + 32)
                total = self.g[slot, keep, rows, :].astype(F32) + self.r2[back, 0, rows, :].astype(F32)
                self.zb[u, z, rows, :] = total.astype(BF16)
        elif kind == "4":
            copy, _ = self.z_copy(unit)
            copy.start()
        elif kind == "5":
            if unit != "B":
                copy, keep = self.z_copy(unit)
                copy.wait()
                u = UNIT[unit]
                self.merge(self.zb.at[u], self.zb.at[u], keep, self.rz.at[u], 2)
            self.far_copy(unit).start()
        elif kind == "6":
            self.far_copy(unit).wait()
            u = UNIT[unit]
            mine = 2 * self.z0 + self.z1
            total = self.zb[u, mine].astype(F32) + self.rf[u, 0].astype(F32)
            if unit in "AB":
                self.out[unit][...] = total
            else:
                self.all[u - 2, 4 * self.z0 + 2 * self.my + self.z1] = total.astype(BF16)
                self.gather_copy(unit, 0).start()
        elif kind == "7":
            self.gather_copy(unit, 0).wait()
            self.gather_copy(unit, 1).start()
        elif kind == "8":
            self.gather_copy(unit, 1).wait()
            self.gather_copy(unit, 2).start()
        elif kind == "9":
            self.gather_copy(unit, 2).wait()
        elif kind == "m":
            self.small_copy(j).wait()
            self.sm[j + 1] = self.sm[j] + self.sq[j]
            if j < 4:
                self.small_copy(j + 1).start()

    def small_copy(self, step):
        bit = (CORE, X_BIT, Y_BIT, Z_NEAR, Z_FAR)[step]
        return send_to(bit, self.sm.at[step], self.sq.at[step], self.ss.at[step], self.sr.at[step])

    def z_copy(self, unit):
        u = UNIT[unit]
        copy = send_to(
            Z_NEAR, self.zb.at[u, pl.ds(2 * (1 - self.z0), 2)], self.rz.at[u],
            self.sz.at[u], self.qz.at[u],
        )
        return copy, 2 * self.z0

    def far_copy(self, unit):
        u = UNIT[unit]
        return send_to(
            Z_FAR, self.zb.at[u, pl.ds(2 * self.z0 + 1 - self.z1, 1)], self.rf.at[u],
            self.sf.at[u], self.qf.at[u],
        )

    def gather_copy(self, unit, step):
        u = UNIT[unit] - 2
        bit, at, count = (
            (Z_FAR, 4 * self.z0 + 2 * self.my + self.z1, 1),
            (Y_BIT, 4 * self.z0 + 2 * self.my, 2),
            (Z_NEAR, 4 * self.z0, 4),
        )[step]
        part = self.all.at[u, pl.ds(at, count)]
        return send_to(bit, part, part, self.sa.at[u, step], self.qa.at[u, step])


TICKS = {
    "f1a": "1A0 1B0",
    "f2a": "1A1 1B1",
    "f2b": "2A0",
    "f3a": "1A2 1B2",
    "f3b": "3A0 2A1",
    "g": "1A3 1B3 nB0 2A2 3A1",
    "ch1": "1C0",
    "ch2": "3A2",
    "ch3": "2A3",
    "c2": "2C0 2B0 nB1 3A3 4A0",
    "c3": "1C1",
    "c4": "1C2",
    "c5": "1C3 3C0 3B0",
    "s1": "5A0",
    "sh1": "2B1 1S0 2C1",
    "sh4": "2C2",
    "sh5": "6A0",
    "s2": "2C3 3C1",
    "s2n": "1S1 3B1 5B0",
    "s3": "2S0 3C2",
    "s4": "1S2 3C3 4C0",
    "s5": "1S3",
    "tail": "3S0 mM0 6B0 2S1 5C0 2S2 2S3 3S1 mM1 3S2 6C0 3S3 4S0 mM2 7C0 5S0 mM3 8C0 6S0 mM4 7S0 9C0 8S0 9S0",
}


def ticks(hub, name):
    for word in TICKS.get(name, "").split():
        hub.event(word[0], word[1], int(word[2]))


def loop_ticks(hub, name, index, names):
    for k, at in enumerate(names):
        if at in TICKS:
            @pl.when(index == k)
            def _():
                ticks(hub, at)


def attention_unit(hub, unit, grad, low, mixed, q, k, v, lse, reach, slope, x, y, w, up, dq, dk, dv):
    tag = unit.lower()

    def cast(rows):
        low[rows, :] = grad[rows, :].astype(BF16)

    def chunk(j, grads, side):
        ticks(hub, f"{tag}{j}n")
        for n in range(grads.shape[1] // 256):
            hub.put(unit, j, FIRST_SLOT[unit] + j, 256 * n,
                    tn(grads[:, 256 * n : 256 * n + 256], side[...]))
        hub.begin(unit, j)
        ticks(hub, f"{tag}{j + 1 if j else 0}")

    rows_loop(grad.shape[0], 128, cast)
    chunk(0, mixed, low)
    project(low, w.at[3], up)
    ticks(hub, f"{tag}1")
    attend_back(q, k, v, up, mixed, lse, reach, slope, dq, dk, dv,
                lambda hp: loop_ticks(hub, tag, hp, [f"{tag}h{i}" for i in range(6)]))
    chunk(1, dq, x)
    chunk(2, dk, y)
    chunk(3, dv, y)


class Loads:
    def __init__(self, sems):
        self.sems, self.next = sems, 0

    def start(self, src, dst):
        copy = pltpu.make_async_copy(src, dst, self.sems.at[self.next])
        self.next += 1
        copy.start()
        return copy


def backward_body(*refs):
    (h_two, h_cot, h_in, h_out, h_w, h_cq, h_ck, h_cv, h_cm, h_rlow, h_olow,
     h_sq, h_sk, h_sv, h_sm, h_normed, h_one, h_opt, h_radar, h_reach,
     vectors, c_lse, s_lse, slope) = refs[:24]
    gain_s, gain_r, gain_o, gain_f, shift_f, b_out = (
        vectors.at[i : i + 1, :] for i in (0, 2, 4, 8, 9, 10)
    )
    refs = refs[24:]
    (o_merged, o_radar, o_opt, o_fin, o_fout, o_all, o_small) = refs[:7]
    (g, rc, r1, r2, rn, zb, rz, rf, wa, wb, q, k, v, mixed, x, y, two, two_grad, out, pull, one,
     cot, low, up, dq, dk, dv, reach, sm, sq) = refs[7:37]
    sems = refs[37:]
    hub = Sums((g, rc, r1, r2, rn, zb, rz, rf, o_all) + tuple(sems[:14]) + (sm, sq) + tuple(sems[14:16]))
    hub.out = {"A": o_fin, "B": o_fout}
    load = Loads(sems[16])
    tile_sems = sems[17]
    n = two.shape[0]
    width = wb.shape[1]
    steps = h_in.shape[1] // width

    def tile(i):
        at = pl.ds(pl.multiple_of(i * width, width), width)
        slot = i % 2
        return (
            pltpu.make_async_copy(h_in.at[:, at], wb.at[2 * slot], tile_sems.at[slot, 0]),
            pltpu.make_async_copy(h_out.at[at, :], wb.at[2 * slot + 1], tile_sems.at[slot, 1]),
        )

    first = [load.start(h_two, two), load.start(h_cot, cot)]
    for copy in tile(0):
        copy.start()
    later = [load.start(a, b) for a, b in (
        (h_cm, mixed), (h_w.at[pl.ds(4, 4)], wa), (h_cq, q), (h_ck, k), (h_cv, v),
        (h_rlow, x), (h_olow, y), (h_one, one), (h_reach, reach))]
    greet((CORE, X_BIT, Y_BIT, Z_NEAR, Z_FAR))
    sm[0] = jnp.zeros_like(sm[0])
    out[...] = jnp.zeros_like(out)
    pull[...] = jnp.zeros_like(pull)
    first[0].wait()
    norm_rows(two, gain_f, shift_f, low)
    first[1].wait()

    def feed(i, _):
        for copy in tile(i):
            copy.wait()

        @pl.when(i < steps - 1)
        def _():
            for copy in tile(i + 1):
                copy.start()

        w_in, w_out = wb.at[2 * (i % 2)], wb.at[2 * (i % 2) + 1]
        for m in range(width // 256):
            at = slice(m * 256, (m + 1) * 256)
            h = nn(low[...], w_in[:, at]) + vectors[pl.ds(11 + i, 1), at]
            t = jnp.tanh(0.7978845608028654 * h * (1.0 + 0.044715 * h * h))
            half = 0.5 * (1.0 + t)
            hidden = (h * half).astype(BF16)
            rise = half + 0.5 * h * (1.0 - t * t) * (
                0.7978845608028654 * (1.0 + 3 * 0.044715 * h * h)
            )
            grad = (nt(cot[...], w_out[at, :]) * rise).astype(BF16)
            sm[0, pl.ds(24 + i, 1), at] = jnp.sum(grad.astype(F32), axis=0, keepdims=True)
            out[...] += nn(hidden, w_out[at, :])
            pull[...] += nt(grad, w_in[:, at])
            hub.put("A", 0, i, 256 * m, tn(grad, low[...]))
            hub.put("B", 0, 4 + i, 256 * m, tn(hidden, cot[...]))
            if m == width // 256 - 1:
                hub.begin("A", i)
                hub.begin("B", i)
            loop_ticks(hub, "f", i, [f"f{s}{'abc'[m]}" for s in range(4)])
        return 0

    lax.fori_loop(0, steps, feed, 0)
    self_w = load.start(h_w.at[pl.ds(0, 4)], wb)

    def close(rows):
        value, cotangent = two[rows, :], cot[rows, :].astype(F32)
        dv[rows, :] = (value + out[rows, :] + b_out[...]).astype(BF16)
        dval, dgain, dshift = norm_back_rows(value, gain_f[...], pull[rows, :])
        total = cotangent + dval
        two_grad[rows, :] = total
        sm[0, 0:1, :] += dgain
        sm[0, 1:2, :] += dshift
        sm[0, 2:3, :] += jnp.sum(cotangent, axis=0, keepdims=True)
        sm[0, 3:4, :] += jnp.sum(total, axis=0, keepdims=True)

    rows_loop(n, 128, close)
    stores = [load.start(dv, o_merged)]
    opt_load = load.start(h_opt, cot)
    ticks(hub, "g")
    for copy in later:
        copy.wait()
    stores[0].wait()
    attention_unit(hub, "C", two_grad, low, mixed, q, k, v, c_lse, reach, slope, x, y, wa,
                   up, dq, dk, dv)
    later = [load.start(a, b) for a, b in (
        (h_sm, mixed), (h_sq, q), (h_sk, k), (h_sv, v), (h_normed, x), (h_radar, y))]
    opt_load.wait()

    def cross(rows):
        dval, dgain, dshift = norm_back_rows(one[rows, :], gain_r[...], nn(dq[rows, :], wa[0]))
        total = two_grad[rows, :] + dval
        out[rows, :] = total
        sm[0, 8:9, :] += dgain
        sm[0, 9:10, :] += dshift
        sm[0, 12:13, :] += jnp.sum(total, axis=0, keepdims=True)
        dval, dgain, dshift = norm_back_rows(
            cot[rows, :].astype(F32), gain_o[...], nn(dk[rows, :], wa[1]) + nn(dv[rows, :], wa[2])
        )
        pull[rows, :] = dval
        sm[0, 10:11, :] += dgain
        sm[0, 11:12, :] += dshift

    rows_loop(n, 256, cross)
    stores = [load.start(pull, o_opt)]
    ticks(hub, "c5")
    for copy in later:
        copy.wait()
    self_w.wait()
    attention_unit(hub, "S", out, low, mixed, q, k, v, s_lse, reach, slope, x, x, wb,
                   up, dq, dk, dv)

    def own(rows):
        dval, dgain, dshift = norm_back_rows(
            y[rows, :].astype(F32), gain_s[...],
            nn(dq[rows, :], wb[0]) + nn(dk[rows, :], wb[1]) + nn(dv[rows, :], wb[2]),
        )
        two[rows, :] = out[rows, :] + dval
        sm[0, 16:17, :] += dgain
        sm[0, 17:18, :] += dshift

    rows_loop(n, 256, own)
    stores.append(load.start(two, o_radar))
    hub.small_copy(0).start()
    ticks(hub, "s5")
    ticks(hub, "tail")
    o_small[...] = sm[5]
    for copy in stores:
        copy.wait()


def run_backward(two, cot, feed_in, feed_out, w, cross, own, one, optical, radar, reach,
                 vectors, c_lse, s_lse, slope):
    n, d = two.shape
    any_space = pl.BlockSpec(memory_space=pl.ANY)
    low, wide = pltpu.VMEM((n, d), BF16), pltpu.VMEM((n, d), F32)
    chunk = lambda *dims: pltpu.VMEM(dims + (96, d), BF16)
    sems = lambda *dims: pltpu.SemaphoreType.DMA(dims)
    return pl.pallas_call(
        backward_body,
        out_shape=[
            shape((n, d), BF16), shape((n, d), F32), shape((n, d), F32),
            shape((96, d), F32), shape((96, d), F32), shape((2, 8, 96, d), BF16),
            shape((32, d), F32),
        ],
        in_specs=[any_space] * 20 + [VMEM] * 3 + [SMEM],
        out_specs=[any_space] * 3 + [VMEM] * 4,
        scratch_shapes=[
            chunk(8, 8), chunk(8, 4), chunk(14, 2), chunk(14, 1), chunk(2, 4),
            chunk(4, 4), chunk(4, 2), chunk(4, 1),
            pltpu.VMEM((4, d, d), BF16), pltpu.VMEM((4, d, d), BF16),
            low, low, low, low, low, low, wide, wide, wide, wide, wide,
            low, low, low, low, low, low, pltpu.VMEM((n, n), F32),
            pltpu.VMEM((6, 32, d), F32), pltpu.VMEM((5, 32, d), F32),
            sems(8), sems(8), sems(14), sems(14), sems(14), sems(14), sems(2), sems(2),
            sems(4), sems(4), sems(4), sems(4), sems(2, 3), sems(2, 3), sems(5), sems(5),
            sems(24), sems(2, 2),
        ],
        compiler_params=pltpu.CompilerParams(
            vmem_limit_bytes=LIMIT, collective_id=1, has_side_effects=True
        ),
        name="backward",
        cost_estimate=pl.CostEstimate(flops=35 * 10**9, bytes_accessed=5 * 10**7, transcendentals=0),
    )(two, cot, feed_in, feed_out, w, *cross, *own, one, optical, radar, reach,
      vectors, c_lse, s_lse, slope)


def call(body, outs, scratch, operands, in_specs, **more):
    return pl.pallas_call(
        body,
        out_shape=outs,
        in_specs=in_specs,
        out_specs=[VMEM] * len(outs),
        scratch_shapes=scratch,
        compiler_params=pltpu.CompilerParams(vmem_limit_bytes=LIMIT),
        **more,
    )(*operands)


def run_feed(place, two, cot, gain, shift, w_in, b_in, w_out, b_out):
    n, d = two.shape
    f = w_in.shape[1]
    tile = 768
    whole = lambda *dims: pl.BlockSpec(dims, lambda i, p: (0,) * len(dims))
    slots = pl.BlockSpec((2, 2, 1, 96, d), lambda i, p: (0, 0, i ^ p[0], 0, 0))
    grad = shape((2, 2, 4, 96, d), BF16)
    return pl.pallas_call(
        feed_step,
        grid_spec=pltpu.PrefetchScalarGridSpec(
            num_scalar_prefetch=1,
            grid=(f // tile,),
            in_specs=[
                whole(n, d), whole(n, d), whole(1, d), whole(1, d),
                pl.BlockSpec((d, tile), lambda i, p: (0, i)),
                pl.BlockSpec((1, tile), lambda i, p: (0, i)),
                pl.BlockSpec((tile, d), lambda i, p: (i, 0)),
                whole(1, d),
            ],
            out_specs=[
                whole(n, d), whole(n, d), slots, slots, slots, slots,
                pl.BlockSpec((1, 1, tile), lambda i, p: (i, 0, 0)),
                whole(8, d),
            ],
            scratch_shapes=[
                pltpu.VMEM((n, d), BF16), pltpu.VMEM((n, d), F32), pltpu.VMEM((n, d), F32),
                pltpu.VMEM((tile, d), BF16), pltpu.VMEM((tile, d), BF16),
            ],
        ),
        out_shape=[
            shape((n, d), BF16), shape((n, d), F32), grad, grad, grad, grad,
            shape((f // tile, 1, tile), F32), shape((8, d), F32),
        ],
        compiler_params=pltpu.CompilerParams(vmem_limit_bytes=LIMIT),
        name="feed",
        cost_estimate=pl.CostEstimate(flops=15 * 10**9, bytes_accessed=25 * 10**6, transcendentals=0),
    )(place, two, cot, gain, shift, w_in, b_in, w_out, b_out)


def back_scratch(n, d):
    low = pltpu.VMEM((n, d), BF16)
    return [low, pltpu.VMEM((d, d), BF16), low, low, low, low]


def run_cross_backward(place, two_grad, mixed, q, k, v, lse, reach, slope, radar_low, optical_low,
                       w, one, optical, gain_r, gain_o):
    n, d = one.shape
    grad = shape((2, 2, 4, 96, d), BF16)
    wide = shape((n, d), F32)
    return call(
        cross_backward,
        [wide, wide, grad, grad, shape((8, d), F32)],
        back_scratch(n, d),
        (place, two_grad, mixed, q, k, v, lse, reach, slope, radar_low, optical_low,
         w, one, optical, gain_r, gain_o),
        [SMEM] + [VMEM] * 7 + [SMEM] + [VMEM] * 7,
        name="cross_backward",
        cost_estimate=pl.CostEstimate(flops=12 * 10**9, bytes_accessed=25 * 10**6, transcendentals=0),
    )


def run_self_backward(place, one_grad, mixed, q, k, v, lse, reach, slope, normed, w, radar, gain):
    n, d = one_grad.shape
    grad = shape((2, 2, 4, 96, d), BF16)
    return call(
        self_backward,
        [shape((n, d), F32), grad, grad, shape((8, d), F32)],
        back_scratch(n, d),
        (place, one_grad, mixed, q, k, v, lse, reach, slope, normed, w, radar, gain),
        [SMEM] + [VMEM] * 7 + [SMEM] + [VMEM] * 4,
        name="self_backward",
        cost_estimate=pl.CostEstimate(flops=12 * 10**9, bytes_accessed=25 * 10**6, transcendentals=0),
    )


def finish(got, *outs):
    for unit in range(2):
        for mat in range(4):
            for half in range(2):
                outs[4 * unit + mat][96 * half : 96 * half + 96, :] = got[
                    unit, mat % 2 * 4 + half * 2 + mat // 2
                ].astype(F32)


def run_finish(got):
    d = got.shape[-1]
    outs = call(finish, [shape((192, d), F32)] * 8, [], (got,), [VMEM], name="finish")
    outs = [o if i % 4 == 3 else o.T for i, o in enumerate(outs)]
    return outs[:4], outs[4:]


def shards(
    radar, optical, patch_table, cotangent, norm_self_gain, norm_self_shift,
    self_query, self_key, self_value, self_out, self_out_bias, norm_radar_gain, norm_radar_shift,
    norm_optical_gain, norm_optical_shift, cross_query, cross_key, cross_value, cross_out,
    cross_out_bias, norm_feed_gain, norm_feed_shift, feed_in, feed_in_bias, feed_out, feed_out_bias,
):
    dp, head = lax.axis_size("dp"), lax.axis_size("head")
    near = (dp, head) == (8, 4)
    row = lambda v: v.reshape(1, -1)
    zero = jnp.int32(0)
    if near:
        mine = lax.axis_index("dp") * 4 + lax.axis_index("head")
        place = jnp.stack([mine // 8, mine // 4 % 2, mine // 2 % 2, mine % 2]).astype(jnp.int32)
        group = jnp.arange(4, dtype=jnp.int32) ^ lax.axis_index("head")
    else:
        place = jnp.stack([zero] * 4)
        group = jnp.arange(head, dtype=jnp.int32)
    per = HEADS // head
    heads = (group[:, None] * per + jnp.arange(per, dtype=jnp.int32)[None, :]).reshape(-1)
    slope = -jnp.exp2(-8.0 * (heads + 1).astype(F32) / HEADS)
    weights = (self_query, self_key, self_value, self_out,
               cross_query, cross_key, cross_value, cross_out)
    weights = tuple(w if i % 4 == 3 else w.T for i, w in enumerate(weights))
    if not near:
        w = lax.all_gather(jnp.stack(weights), "head", axis=1, tiled=True)
        weights = (w,)
    vectors = jnp.concatenate([
        norm_self_gain, norm_self_shift, norm_radar_gain, norm_radar_shift,
        norm_optical_gain, norm_optical_shift, self_out_bias, cross_out_bias,
        norm_feed_gain, norm_feed_shift, feed_out_bias, feed_in_bias,
    ]).reshape(-1, radar.shape[1])
    got = run_forward(near, radar, optical, vectors, patch_table, slope, weights)
    if near:
        w, got = got[0], got[1:]
    (normed, radar_low, optical_low, sq, sk, sv, cq, ck, cv, s_mixed, c_mixed, s_lse, c_lse,
     two, one, reach) = got
    d = radar.shape[1]
    if near:
        merged, radar_grad, optical_grad, feed_in_grad, feed_out_grad, got, small = run_backward(
            two, cotangent, feed_in, feed_out, w,
            (cq, ck, cv, c_mixed, radar_low, optical_low), (sq, sk, sv, s_mixed, normed),
            one, optical, radar, reach,
            vectors,
            c_lse, s_lse, slope,
        )
        cross, own = run_finish(got)
    else:
        merged, two_grad, in_keep, in_send, out_keep, out_send, bias_in, feed_small = run_feed(
            place, two, cotangent, row(norm_feed_gain), row(norm_feed_shift),
            feed_in, row(feed_in_bias), feed_out, row(feed_out_bias),
        )
        one_grad, optical_grad, cross_keep, cross_send, cross_small = run_cross_backward(
            place, two_grad, c_mixed, cq, ck, cv, c_lse, reach, slope, radar_low, optical_low,
            w[4:], one, optical, row(norm_radar_gain), row(norm_optical_gain),
        )
        radar_grad, self_keep, self_send, self_small = run_self_backward(
            place, one_grad, s_mixed, sq, sk, sv, s_lse, reach, slope, normed,
            w[:4], radar, row(norm_self_gain),
        )
        d = radar.shape[1]
        small = jnp.concatenate([feed_small, cross_small, self_small, bias_in.reshape(-1, d)])
        def logical(keep, send, order):
            both = jnp.stack([keep, send])
            return jnp.transpose(both, order).reshape(-1, d)

        def feed_sum(keep, send):
            return lax.psum_scatter(
                logical(keep, send, (3, 2, 1, 0, 4, 5)).astype(F32),
                ("dp", "head"), scatter_dimension=0, tiled=True,
            )

        def attn_sum(keep, send):
            total = logical(keep, send, (3, 1, 0, 2, 4, 5)).astype(F32).reshape(4, -1, d)
            total = lax.psum_scatter(total, "head", scatter_dimension=1, tiled=True)
            total = lax.psum(total, "dp")
            return total[0].T, total[1].T, total[2].T, total[3]

        feed_in_grad, feed_out_grad = feed_sum(in_keep, in_send), feed_sum(out_keep, out_send)
        cross, own = attn_sum(cross_keep, cross_send), attn_sum(self_keep, self_send)
        small = lax.psum(small, ("dp", "head"))
    bias_part = feed_in_bias.shape[0] // (dp * head)
    feed_in_bias_grad = lax.dynamic_slice_in_dim(
        small[24:28].reshape(-1),
        (lax.axis_index("dp") * head + lax.axis_index("head")) * bias_part,
        bias_part,
    )
    return (
        merged, radar_grad, optical_grad,
        small[16], small[17], *own, small[12],
        small[8], small[9], small[10], small[11], *cross, small[3],
        small[0], small[1], feed_in_grad.T, feed_in_bias_grad, feed_out_grad, small[2],
    )


def solution(mesh):
    token, rep = P(("dp", "head"), None), P()
    col, row = P(None, "head"), P("head", None)
    in_specs = (
        token, token, P(None, ("dp", "head")), token,
        rep, rep, col, col, col, row, rep,
        rep, rep, rep, rep, col, col, col, row, rep,
        rep, rep, rep, rep, rep, rep,
    )
    out_specs = (
        token, token, token,
        rep, rep, col, col, col, row, rep,
        rep, rep, rep, rep, col, col, col, row, rep,
        rep, rep, P(None, ("dp", "head")), P(("dp", "head")), token, rep,
    )
    return jax.shard_map(shards, mesh=mesh, in_specs=in_specs, out_specs=out_specs, check_vma=False)
```

```python
import functools

import jax
import jax.numpy as jnp
import numpy as np
from jax import lax
from jax.experimental import pallas as pl
from jax.experimental.pallas import tpu as pltpu
from jax.sharding import PartitionSpec as P

F32, BF16 = jnp.float32, jnp.bfloat16
HEADS, HEAD_DIM = 12, 64
EPSILON = 1e-06
FAR = 1e12
LIMIT = 60 * 2**20
VMEM = pl.BlockSpec(memory_space=pltpu.VMEM)
SMEM = pl.BlockSpec(memory_space=pltpu.SMEM)
HBM = pl.BlockSpec(memory_space=pl.ANY)


def nn(a, b):
    return lax.dot_general(a, b, (((1,), (0,)), ((), ())), preferred_element_type=F32)


def nt(a, b):
    return lax.dot_general(a, b, (((1,), (1,)), ((), ())), preferred_element_type=F32)


def tn(a, b):
    return lax.dot_general(a, b, (((0,), (0,)), ((), ())), preferred_element_type=F32)


def rows_loop(total, block, body):
    def step(i, _):
        body(pl.ds(pl.multiple_of(i * block, block), block))
        return 0

    lax.fori_loop(0, total // block, step, 0)


def centred(v):
    c = v - jnp.mean(v, axis=-1, keepdims=True)
    return c, lax.rsqrt(jnp.mean(c * c, axis=-1, keepdims=True) + EPSILON)


def norm_rows(src, gain, shift, dst):
    def body(rows):
        c, r = centred(src[rows, :].astype(F32))
        dst[rows, :] = (c * r * gain[...] + shift[...]).astype(BF16)

    rows_loop(src.shape[0], 128, body)


def norm_back_rows(v, gain, u):
    c, r = centred(v)
    hat = c * r
    w = u * gain
    dv = r * (
        w
        - jnp.mean(w, axis=-1, keepdims=True)
        - hat * jnp.mean(w * hat, axis=-1, keepdims=True)
    )
    return dv, jnp.sum(u * hat, axis=0, keepdims=True), jnp.sum(u, axis=0, keepdims=True)


def project(x, w, dst, scale=None, half=None):
    total = w.shape[0]
    if half is None:
        blocks = [(i, 256) for i in range(0, total, 256)]
    else:
        blocks = [(half * total // 2, 256), (half * total // 2 + 256, total // 2 - 256)]
    for at, size in blocks:
        cols = slice(at, at + size)
        y = nt(x[...], w[cols, :])
        dst[:, cols] = (y if scale is None else y * scale).astype(BF16)


def fill_reach(table, columns, reach):
    for i in range(3):
        line = table[i : i + 1, :].astype(F32)
        columns[i] = jnp.broadcast_to(line, (128, line.shape[1])).T

    def body(rows):
        seg, down, across = (
            columns[i, rows, 0:1] - table[i : i + 1, :].astype(F32) for i in range(3)
        )
        reach[rows, :] = jnp.where(seg == 0, jnp.sqrt(down * down + across * across), FAR)

    rows_loop(reach.shape[0], 64, body)


def slope_of(table, group):
    return lambda h: table[3 * (h // 3 ^ group) + h % 3]


def low_half(length):
    return lax.broadcasted_iota(jnp.int32, (length, 128), 1) < HEAD_DIM


def attend(q, k, v, reach, slope, mixed, lse, tick, pairs):
    lo = low_half(q.shape[0])

    def pair(hp, _):
        tick(hp)
        at = pl.ds(pl.multiple_of(hp * 128, 128), 128)
        qs, ks, vs = q[:, at], k[:, at], v[:, at]
        outs, tops = [], []
        for sub in range(2):
            mine = lo if sub == 0 else jnp.logical_not(lo)
            s = nt(jnp.where(mine, qs, jnp.zeros_like(qs)), ks)
            s = s + slope(2 * hp + sub) * reach[...]
            top = jnp.max(s, axis=-1, keepdims=True)
            e = jnp.exp(s - top).astype(BF16)
            outs.append(nn(e, jnp.where(mine, vs, jnp.ones_like(vs))))
            tops.append(top)
        num = jnp.where(lo, outs[0], outs[1])
        den = pltpu.roll(jnp.where(lo, outs[1], outs[0]), HEAD_DIM, 1)
        mixed[:, at] = (num / den).astype(BF16)
        lse_t = (jnp.where(lo, tops[0], tops[1]) + jnp.log(den)).T
        lse[hp] = jnp.concatenate([lse_t[0:1], lse_t[HEAD_DIM : HEAD_DIM + 1]], axis=0)
        return 0

    lax.fori_loop(*pairs, pair, 0)


def attend_back(q, k, v, up, mixed, lse, reach, slope, dq, dk, dv, tick=lambda hp: None):
    lo = low_half(q.shape[0])

    def pair(hp, _):
        tick(hp)
        at = pl.ds(pl.multiple_of(hp * 128, 128), 128)
        qs, ks, vs, ups = q[:, at], k[:, at], v[:, at], up[:, at]
        prod = (ups.astype(F32) * mixed[:, at].astype(F32)).T
        tops = lse[hp]
        dqs, dks, dvs = [], [], []
        for sub in range(2):
            mine = lo if sub == 0 else jnp.logical_not(lo)
            delta = jnp.sum(prod[sub * HEAD_DIM : (sub + 1) * HEAD_DIM], axis=0, keepdims=True)
            s = nt(jnp.where(mine, ks, jnp.zeros_like(ks)), qs)
            p = jnp.exp(s + slope(2 * hp + sub) * reach[...] - tops[sub : sub + 1])
            dp = nt(jnp.where(mine, vs, jnp.zeros_like(vs)), ups)
            ds = (p * (dp - delta)).astype(BF16)
            dvs.append(nn(p.astype(BF16), ups))
            dks.append(nn(ds, qs))
            dqs.append(tn(ds, ks))
        dq[:, at] = (jnp.where(lo, dqs[0], dqs[1]) * HEAD_DIM**-0.5).astype(BF16)
        dk[:, at] = jnp.where(lo, dks[0], dks[1]).astype(BF16)
        dv[:, at] = jnp.where(lo, dvs[0], dvs[1]).astype(BF16)
        return 0

    lax.fori_loop(0, q.shape[1] // 128, pair, 0)


def add_out(base, mixed, w_out, bias, dst):
    def body(cols):
        y = nn(mixed[...], w_out[:, cols])
        dst[:, cols] = base[:, cols].astype(F32) + y + bias[:, cols]

    rows_loop(w_out.shape[1], 256, body)


def place_shards(full, place, at, keep, send):
    my, mx, mc = place[1], place[2], place[3]
    for x in range(2):
        for y in range(2):
            for c, dst in enumerate((keep, send)):
                row = (((y ^ my) * 2 + (x ^ mx)) * 2 + (c ^ mc)) * 96
                dst[x, y, at] = full[pl.ds(pl.multiple_of(row, 96), 96), :]


def feed_step(place, two, cot, gain, shift, w_in, b_in, w_out, b_out,
              merged, two_grad, keep_in, send_in, keep_out, send_out, bias_in, small,
              low, out, pull, full_in, full_out):
    step = pl.program_id(0)
    width = w_out.shape[0]
    block = 256

    @pl.when(step == 0)
    def _():
        norm_rows(two, gain, shift, low)

    for n in range(width // block):
        at = slice(n * block, (n + 1) * block)
        x = nn(low[...], w_in[:, at]) + b_in[:, at]
        inner = 0.7978845608028654 * x * (1.0 + 0.044715 * x * x)
        t = jnp.tanh(inner)
        half = 0.5 * (1.0 + t)
        hidden = (x * half).astype(BF16)
        slope = half + 0.5 * x * (1.0 - t * t) * (
            0.7978845608028654 * (1.0 + 3 * 0.044715 * x * x)
        )
        grad = (nt(cot[...], w_out[at, :]) * slope).astype(BF16)
        bias_in[0, :, at] = jnp.sum(grad.astype(F32), axis=0, keepdims=True)
        part_out = nn(hidden, w_out[at, :])
        part_pull = nt(grad, w_in[:, at])
        if n == 0:
            @pl.when(step == 0)
            def _():
                out[...] = part_out
                pull[...] = part_pull

            @pl.when(step > 0)
            def _():
                out[...] += part_out
                pull[...] += part_pull
        else:
            out[...] += part_out
            pull[...] += part_pull
        full_out[at, :] = tn(hidden, cot[...]).astype(BF16)
        full_in[at, :] = tn(grad, low[...]).astype(BF16)
    place_shards(full_in, place, 0, keep_in.at[:, :], send_in.at[:, :])
    place_shards(full_out, place, 0, keep_out.at[:, :], send_out.at[:, :])

    @pl.when(step == pl.num_programs(0) - 1)
    def _():
        small[...] = jnp.zeros_like(small)

        def body(rows):
            value, cotangent = two[rows, :], cot[rows, :].astype(F32)
            merged[rows, :] = (value + out[rows, :] + b_out[...]).astype(BF16)
            dv, dgain, dshift = norm_back_rows(value, gain[...], pull[rows, :])
            total = cotangent + dv
            two_grad[rows, :] = total
            small[0:1, :] += dgain
            small[1:2, :] += dshift
            small[2:3, :] += jnp.sum(cotangent, axis=0, keepdims=True)
            small[3:4, :] += jnp.sum(total, axis=0, keepdims=True)

        rows_loop(two.shape[0], 128, body)


def weight_grad(grads, rows, full):
    def body(cols):
        full[cols, :] = tn(grads[:, cols], rows[...]).astype(BF16)

    rows_loop(grads.shape[1], 256, body)


def attn_shards(full, place, mat, keep, send):
    my, mz = place[1], place[0]
    for x in range(2):
        for y in range(2):
            for c, dst in enumerate((keep, send)):
                row = ((x * 2 + c) * 2 + (y ^ my)) * 96
                dst[x, y, mat ^ mz] = full[pl.ds(pl.multiple_of(row, 96), 96), :]


def attention_back(place, grad, low, mixed, q, k, v, lse, reach, slope, x, y, w,
                   keep, send, full, up, dq, dk, dv):
    def cast(rows):
        low[rows, :] = grad[rows, :].astype(BF16)

    rows_loop(grad.shape[0], 128, cast)
    weight_grad(mixed, low, full)
    attn_shards(full, place, 3, keep, send)
    project(low, w.at[3], up)
    attend_back(q, k, v, up, mixed, lse, reach, slope_of(slope, 0), dq, dk, dv)
    for mat, (side, d) in enumerate(((x, dq), (y, dk), (y, dv))):
        weight_grad(d, side, full)
        attn_shards(full, place, mat, keep, send)


def cross_backward(place, two_grad, mixed, q, k, v, lse, reach, slope, radar_low, optical_low, w,
                   one, optical, gain_r, gain_o,
                   one_grad, optical_grad, keep, send, small,
                   low, full, up, dq, dk, dv):
    attention_back(place, two_grad, low, mixed, q, k, v, lse, reach, slope, radar_low, optical_low,
                   w, keep, send, full, up, dq, dk, dv)
    small[...] = jnp.zeros_like(small)

    def body(rows):
        pull = nn(dq[rows, :], w[0])
        dv_, dgain, dshift = norm_back_rows(one[rows, :], gain_r[...], pull)
        total = two_grad[rows, :] + dv_
        one_grad[rows, :] = total
        small[0:1, :] += dgain
        small[1:2, :] += dshift
        small[4:5, :] += jnp.sum(total, axis=0, keepdims=True)
        pull = nn(dk[rows, :], w[1]) + nn(dv[rows, :], w[2])
        dv_, dgain, dshift = norm_back_rows(optical[rows, :].astype(F32), gain_o[...], pull)
        optical_grad[rows, :] = dv_
        small[2:3, :] += dgain
        small[3:4, :] += dshift

    rows_loop(two_grad.shape[0], 256, body)


def self_backward(place, one_grad, mixed, q, k, v, lse, reach, slope, normed, w, radar, gain,
                  radar_grad, keep, send, small,
                  low, full, up, dq, dk, dv):
    attention_back(place, one_grad, low, mixed, q, k, v, lse, reach, slope, normed, normed,
                   w, keep, send, full, up, dq, dk, dv)
    small[...] = jnp.zeros_like(small)

    def body(rows):
        pull = nn(dq[rows, :], w[0]) + nn(dk[rows, :], w[1]) + nn(dv[rows, :], w[2])
        dv_, dgain, dshift = norm_back_rows(radar[rows, :].astype(F32), gain[...], pull)
        radar_grad[rows, :] = one_grad[rows, :] + dv_
        small[0:1, :] += dgain
        small[1:2, :] += dshift

    rows_loop(one_grad.shape[0], 256, body)


def shape(dims, dtype):
    return jax.ShapeDtypeStruct(dims, dtype)


CORE, X_BIT, Y_BIT, Z_NEAR, Z_FAR = 1, 2, 4, 8, 16


def partner(bit):
    dp, head = lax.axis_index("dp"), lax.axis_index("head")
    if bit < 4:
        return (dp, head ^ bit)
    return (dp ^ (bit // 4), head)


def greet(bits):
    barrier = pltpu.get_barrier_semaphore()
    for bit in bits:
        pl.semaphore_signal(
            barrier, inc=1, device_id=partner(bit), device_id_type=pl.DeviceIdType.MESH
        )
    pl.semaphore_wait(barrier, len(bits))


def send_to(bit, src, dst, send_sem, recv_sem):
    return pltpu.make_async_remote_copy(
        src_ref=src, dst_ref=dst, send_sem=send_sem, recv_sem=recv_sem,
        device_id=partner(bit), device_id_type=pl.DeviceIdType.MESH,
    )


ORDER = (0, 1, 2, 3, 5, 6, 4, 7)


class Gather:
    def __init__(self, w, send, recv):
        self.w, self.send, self.recv = w, send, recv
        self.mine = lax.axis_index("dp") % 2
        self.part = w.shape[1] // 4

    def copy(self, mat, kind):
        part, half = self.part, self.part // 2
        own = pl.ds(self.mine * half, half)
        far = pl.ds(2 * part + self.mine * half, half)
        other = pl.ds(2 * part + (1 - self.mine) * half, half)
        w = self.w.at[mat]
        up = lambda rows: pl.ds(rows.start + part, rows.size)
        bit, src, dst = (
            (CORE, pl.ds(0, part), pl.ds(part, part)),
            (X_BIT, own, far),
            (Y_BIT, far, far),
            (CORE, far, up(far)),
            (CORE, other, up(other)),
        )[kind]
        return send_to(bit, w.at[src], w.at[dst], self.send.at[mat, kind], self.recv.at[mat, kind])

    def begin(self, mat):
        self.copy(mat, 1).start()
        self.copy(mat, 0).start()

    def after_x(self, mat):
        self.copy(mat, 1).wait_recv()
        self.copy(mat, 2).start()
        self.copy(mat, 3).start()

    def after_y(self, mat):
        self.copy(mat, 2).wait_recv()
        self.copy(mat, 4).start()

    def core_ready(self, mat):
        self.copy(mat, 0).wait_recv()

    def ready(self, mat):
        for kind in (3, 4):
            self.copy(mat, kind).wait_recv()

    def drain(self, mat):
        for kind in range(5):
            self.copy(mat, kind).wait_send()


def load_vectors(parts, vectors):
    d = vectors.shape[1]
    at = 0
    for part in parts:
        for i in range(part.shape[0] // d):
            vectors[at : at + 1, :] = part[i * d : (i + 1) * d].reshape(1, d)
            at += 1


def forward_body(remote, *refs):
    (radar, optical, table, slopes), refs = refs[:4], refs[4:]
    parts, refs = refs[:8], refs[8:]
    owns, refs = refs[: 8 if remote else 1], refs[8 if remote else 1 :]
    outs, refs = refs[: 17 if remote else 16], refs[17 if remote else 16 :]
    vectors, columns, store_sems = refs[:3]
    refs = refs[3:]
    w, refs = (refs[0], refs[1:]) if remote else (owns[0], refs)
    kept = refs[:16]
    (normed, radar_low, optical_low, sq, sk, sv, cq, ck, cv, s_mixed, c_mixed, s_lse, c_lse,
     two, one, reach) = kept
    if remote:
        o_w, outs = outs[0], outs[1:]
        hub = Gather(w, *refs[16:])
        part = w.shape[1] // 4
        greet((CORE, X_BIT, Y_BIT))
        for mat in ORDER:
            w[mat, 0:part, :] = owns[mat][...]
            hub.begin(mat)
        slope = slope_of(slopes, lax.axis_index("head"))
    else:
        slope = slope_of(slopes, 0)
    load_vectors(parts, vectors)
    gain_s, shift_s, gain_r, shift_r, gain_o, shift_o, bias_s, bias_c = (
        vectors.at[i : i + 1, :] for i in range(8)
    )
    stores = []

    def store(src, dst):
        copy = pltpu.make_async_copy(src, dst, store_sems.at[len(stores)])
        stores.append(copy)
        copy.start()

    def done(*names):
        for ref in names:
            i = [r is ref for r in kept].index(True)
            store(ref, outs[i])

    def hop(kind, *places):
        if remote:
            for i in places:
                (hub.after_x if kind == "x" else hub.after_y)(ORDER[i])

    near_here = []

    def core_ready(*mats):
        if remote:
            for mat in mats:
                hub.core_ready(mat)
                near_here.append(mat)

    def ready(mat):
        if mat not in near_here:
            core_ready(mat)
        if remote:
            hub.ready(mat)
            store(w.at[mat], o_w.at[mat])

    def loop_hops(index, at):
        for k, hops in at.items():
            @pl.when(index == k)
            def _():
                for kind, place in hops:
                    hop(kind, place)

    scale = HEAD_DIM**-0.5
    norm_rows(radar, gain_s, shift_s, normed)
    done(normed)
    fill_reach(table, columns, reach)
    done(reach)
    norm_rows(optical, gain_o, shift_o, optical_low)
    done(optical_low)
    core_ready(0, 1, 2)
    project(normed, w.at[0], sq, scale, 0)
    project(normed, w.at[1], sk, None, 0)
    project(normed, w.at[2], sv, None, 0)
    attend(sq, sk, sv, reach, slope, s_mixed, s_lse,
           lambda hp: loop_hops(hp, {2: (("x", 0),)}), (0, 3))
    core_ready(5, 6)
    project(optical_low, w.at[5], ck, None, 0)
    hop("x", 1)
    project(optical_low, w.at[6], cv, None, 0)
    hop("x", 2)
    hop("y", 0)
    ready(0)
    project(normed, w.at[0], sq, scale, 1)
    done(sq)
    hop("x", 3)
    hop("y", 1)
    ready(1)
    project(normed, w.at[1], sk, None, 1)
    done(sk)
    hop("y", 2)
    hop("x", 4)
    ready(2)
    project(normed, w.at[2], sv, None, 1)
    done(sv)
    attend(sq, sk, sv, reach, slope, s_mixed, s_lse,
           lambda hp: loop_hops(hp, {4: (("y", 3), ("x", 5))}), (3, 6))
    done(s_mixed, s_lse)
    hop("x", 6)
    hop("y", 4)
    ready(3)
    add_out(radar, s_mixed, w.at[3], bias_s, one)
    done(one)
    ready(5)
    project(optical_low, w.at[5], ck, None, 1)
    done(ck)
    norm_rows(one, gain_r, shift_r, radar_low)
    done(radar_low)
    core_ready(4)
    project(radar_low, w.at[4], cq, scale, 0)
    attend(cq, ck, cv, reach, slope, c_mixed, c_lse,
           lambda hp: loop_hops(hp, {0: (("x", 7), ("y", 5)), 2: (("y", 6),)}), (0, 3))
    ready(6)
    project(optical_low, w.at[6], cv, None, 1)
    done(cv)
    ready(4)
    project(radar_low, w.at[4], cq, scale, 1)
    done(cq)
    attend(cq, ck, cv, reach, slope, c_mixed, c_lse,
           lambda hp: loop_hops(hp, {4: (("y", 7),)}), (3, 6))
    done(c_mixed, c_lse)
    ready(7)
    add_out(one, c_mixed, w.at[7], bias_c, two)
    done(two)
    if remote:
        for mat in range(8):
            hub.drain(mat)
    for copy in stores:
        copy.wait()


def run_forward(remote, radar, optical, vectors, table, slopes, weights):
    n, d = radar.shape
    low, lse, wide = shape((n, d), BF16), shape((6, 2, n), F32), shape((n, d), F32)
    kept = [low] * 11 + [lse, lse, wide, wide, shape((n, n), F32)]
    whole = [shape((8, d, d), BF16)] if remote else []
    return pl.pallas_call(
        functools.partial(forward_body, remote),
        out_shape=whole + kept,
        in_specs=[VMEM] * 3 + [SMEM] + [VMEM] * (len(vectors) + len(weights)),
        out_specs=[HBM] * len(whole + kept),
        scratch_shapes=[
            pltpu.VMEM((8, d), F32), pltpu.VMEM((3, n, 128), F32),
            pltpu.SemaphoreType.DMA((24,)),
        ] + [pltpu.VMEM(a.shape, a.dtype) for a in whole + kept]
        + ([pltpu.SemaphoreType.DMA((8, 5))] * 2 if remote else []),
        compiler_params=pltpu.CompilerParams(
            vmem_limit_bytes=LIMIT, **(dict(collective_id=0, has_side_effects=True) if remote else {})
        ),
        name="forward",
        cost_estimate=pl.CostEstimate(flops=8 * 10**9, bytes_accessed=3 * 10**7, transcendentals=0),
    )(radar, optical, table, slopes, *vectors, *weights)


X_FIRST = (X_BIT, Y_BIT)
Y_FIRST = (Y_BIT, X_BIT)
PATHS = {
    "A": (X_FIRST, X_FIRST, X_FIRST, X_FIRST),
    "C": (Y_FIRST, X_FIRST, Y_FIRST, X_FIRST),
    "S": (X_FIRST, Y_FIRST, X_FIRST, Y_FIRST),
}
PARTS = {"A": 1, "B": 1, "C": 3, "S": 3}
AGAIN = {
    "C": ('FYN', 'FNY', 'FYN'),
    "S": ('FYN', 'FNY', 'FYN'),
}
PLANE = (3, 0, 1, 2)
FIRST_SLOT = {"A": 0, "B": 4, "C": 0, "S": 4}
FIRST_BACK = {"A": 0, "C": 4, "S": 8}
UNIT = {"A": 0, "B": 1, "C": 2, "S": 3}


def gathered_at(unit, part, y, z0, z1):
    return 4 * z0 + 2 * y + z1 if AGAIN[unit][part] == "FYN" else 4 * y + 2 * z0 + z1


class Sums:
    def __init__(self, refs):
        (self.g, self.rc, self.r1, self.r2, self.rn, self.zb, self.rz, self.rf, self.all,
         self.cs, self.cr, self.s1, self.q1, self.s2, self.q2, self.sn, self.qn,
         self.sz, self.qz, self.sf, self.qf, self.sa, self.qa,
         self.sm, self.sq, self.ss, self.sr) = refs
        dp, head = lax.axis_index("dp"), lax.axis_index("head")
        self.mc, self.mx, self.my = head % 2, head // 2, dp % 2
        self.z0, self.z1 = dp // 2 % 2, dp // 4
        self.place = {X_BIT: self.mx, Y_BIT: self.my}

    def bits(self, unit, bit):
        if unit in "CS" and bit != Y_BIT:
            return 0
        return self.mc if bit == CORE else self.place[bit]

    def path(self, unit, j):
        return X_FIRST if unit == "B" else PATHS[unit][j]

    def shard_at(self, unit, j, t):
        if unit in "AB":
            y, x, c = t // 4, t // 2 % 2, t % 2
        else:
            x, c, y = t // 4, t // 2 % 2, t % 2
        where = {X_BIT: x, Y_BIT: y}
        first, second = self.path(unit, j)
        return c * 4 + where[first] * 2 + where[second]

    def put(self, unit, j, slot, row, value):
        end = row + value.shape[0]
        at = row
        while at < end:
            t = at // 96
            stop = min(end, (t + 1) * 96)
            self.g[slot, self.shard_at(unit, j, t), at - t * 96 : stop - t * 96, :] = value[
                at - row : stop - row
            ].astype(BF16)
            at = stop

    def rows(self, unit, part):
        size = 96 // PARTS[unit]
        return pl.ds(part * size, size)

    def merge(self, dst, at, add, back, count, rows):
        def body(i, _):
            dst[at + i, rows, :] = dst[at + i, rows, :] + add[back + i, rows, :]
            return 0

        lax.fori_loop(0, count, body, 0)

    def core_copy(self, unit, slot):
        other = 4 * (1 - self.bits(unit, CORE))
        return send_to(
            CORE, self.g.at[slot, pl.ds(other, 4)], self.rc.at[slot],
            self.cs.at[slot], self.cr.at[slot],
        )

    def first_copy(self, unit, j, slot, back, part):
        first = self.path(unit, j)[0]
        keep = self.bits(unit, first)
        base = 4 * self.bits(unit, CORE)
        rows = self.rows(unit, part)
        copy = send_to(
            first, self.g.at[slot, pl.ds(base + 2 * (1 - keep), 2), rows],
            self.r1.at[back, :, rows], self.s1.at[back, part], self.q1.at[back, part],
        )
        return copy, base + 2 * keep

    def second_copy(self, unit, j, slot, back, part):
        first, second = self.path(unit, j)
        base = 4 * self.bits(unit, CORE) + 2 * self.bits(unit, first)
        keep = self.bits(unit, second)
        rows = self.rows(unit, part)
        copy = send_to(
            second, self.g.at[slot, pl.ds(base + 1 - keep, 1), rows],
            self.r2.at[back, :, rows], self.s2.at[back, part], self.q2.at[back, part],
        )
        return copy, base + keep

    def begin(self, unit, j):
        self.core_copy(unit, FIRST_SLOT[unit] + j).start()

    def near_copy(self, p):
        slot = 4 + 2 * p + 1 - self.z0
        base = 4 * self.mc
        return send_to(
            Z_NEAR, self.g.at[slot, pl.ds(base, 4)], self.rn.at[p], self.sn.at[p], self.qn.at[p]
        )

    def slots(self, unit, j):
        if unit == "B":
            return 4 + 2 * j + self.z0, 12 + j
        return FIRST_SLOT[unit] + j, FIRST_BACK[unit] + j

    def event(self, kind, unit, j, part):
        u = UNIT.get(unit)
        if unit != "M":
            rows = self.rows(unit, part)
        if kind == "1":
            slot = FIRST_SLOT[unit] + j
            self.core_copy(unit, slot).wait()
            g, base, whole = self.g.at[slot], 4 * self.bits(unit, CORE), pl.ds(0, 96)
            if unit == "B":
                self.merge(g, base, self.rc.at[slot], 0, 4, whole)
                if j % 2:
                    self.near_copy(j // 2).start()
                return
            keep = 2 * self.bits(unit, self.path(unit, j)[0])
            for p in range(PARTS[unit]):
                self.merge(g, base + 2 - keep, self.rc.at[slot], 2 - keep, 2, self.rows(unit, p))
                self.first_copy(unit, j, slot, FIRST_BACK[unit] + j, p)[0].start()
            self.merge(g, base + keep, self.rc.at[slot], keep, 2, whole)
        elif kind == "n":
            slot, back = self.slots("B", j)
            self.near_copy(j).wait()
            self.merge(self.g.at[slot], 4 * self.mc, self.rn.at[j], 0, 4, rows)
            self.first_copy("B", j, slot, back, 0)[0].start()
        elif kind == "2":
            slot, back = self.slots(unit, j)
            copy, keep = self.first_copy(unit, j, slot, back, part)
            copy.wait()
            self.merge(self.g.at[slot], keep, self.r1.at[back], 0, 2, rows)
            self.second_copy(unit, j, slot, back, part)[0].start()
        elif kind == "3":
            slot, back = self.slots(unit, j)
            copy, keep = self.second_copy(unit, j, slot, back, part)
            copy.wait()
            if unit == "B":
                z = 2 * self.z0 + j
            else:
                plane = j if unit == "A" else PLANE[j]
                z = (plane % 2) * 2 + plane // 2
            self.zb[u, z, rows, :] = self.g[slot, keep, rows, :] + self.r2[back, 0, rows, :]
        elif kind == "4":
            self.z_copy(unit, part).start()
        elif kind == "5":
            if unit != "B":
                self.z_copy(unit, part).wait()
                self.merge(self.zb.at[u], 2 * self.z0, self.rz.at[u], 0, 2, rows)
            self.far_copy(unit, part).start()
        elif kind == "6":
            self.far_copy(unit, part).wait()
            mine = 2 * self.z0 + self.z1
            total = self.zb[u, mine, rows, :].astype(F32) + self.rf[u, 0, rows, :].astype(F32)
            if unit in "AB":
                self.out[unit][...] = total
            else:
                at = gathered_at(unit, part, self.my, self.z0, self.z1)
                self.all[u - 2, at, rows, :] = total.astype(BF16)
                self.gather_copy(unit, 0, part).start()
        elif kind == "7":
            self.gather_copy(unit, 0, part).wait()
            self.gather_copy(unit, 1, part).start()
        elif kind == "8":
            self.gather_copy(unit, 1, part).wait()
            self.gather_copy(unit, 2, part).start()
        elif kind == "9":
            self.gather_copy(unit, 2, part).wait()
        elif kind == "m":
            self.small_copy(j).wait()
            self.sm[j + 1] = self.sm[j] + self.sq[j]
            if j < 4:
                self.small_copy(j + 1).start()

    def small_copy(self, step):
        bit = (CORE, X_BIT, Y_BIT, Z_NEAR, Z_FAR)[step]
        return send_to(bit, self.sm.at[step], self.sq.at[step], self.ss.at[step], self.sr.at[step])

    def z_copy(self, unit, part):
        u, rows = UNIT[unit], self.rows(unit, part)
        return send_to(
            Z_NEAR, self.zb.at[u, pl.ds(2 * (1 - self.z0), 2), rows], self.rz.at[u, :, rows],
            self.sz.at[u, part], self.qz.at[u, part],
        )

    def far_copy(self, unit, part):
        u, rows = UNIT[unit], self.rows(unit, part)
        return send_to(
            Z_FAR, self.zb.at[u, pl.ds(2 * self.z0 + 1 - self.z1, 1), rows],
            self.rf.at[u, :, rows], self.sf.at[u, part], self.qf.at[u, part],
        )

    def gather_copy(self, unit, step, part):
        u, rows = UNIT[unit] - 2, self.rows(unit, part)
        axes = AGAIN[unit][part]
        z1 = self.z1 if step == 0 else 0
        y = self.my if "Y" not in axes[:step] else 0
        z0 = self.z0 if "N" not in axes[:step] else 0
        at = gathered_at(unit, part, y, z0, z1)
        held = self.all.at[u, pl.ds(at, 2**step), rows]
        bit = {"F": Z_FAR, "Y": Y_BIT, "N": Z_NEAR}[axes[step]]
        return send_to(bit, held, held, self.sa.at[u, step, part], self.qa.at[u, step, part])


TICKS = {
    "f1b": "1A00 1B00",
    "f2b": "1A10 1B10",
    "f3b": "1A20 2A00 1B20",
    "g": "1A30 1B30",
    "c0n": "2A10 3A00",
    "ch1": "1C00",
    "ch2": "nB00 3A10 2A20",
    "ch4": "2C00",
    "ch5": "2C01 2A30",
    "c2": "2C02",
    "c2n": "1C10 3A20",
    "c3": "nB10 2B00",
    "c3n": "3C00 1C20 3A30 4A00",
    "c4": "3C01 3C02",
    "c5": "1C30 2C10",
    "s0n": "3B00",
    "s0": "2C11",
    "s1": "2C20",
    "sh1": "1S00 2C12 2C21",
    "sh2": "5A00 2C22",
    "sh3": "3C10 3C11",
    "sh4": "3C12 2B10",
    "sh5": "2C30",
    "s2": "2C31",
    "s2n": "6A00 2C32 3B10 5B00",
    "s3": "3C20 1S10 3C30 4C00",
    "s4": "2S00 3C31",
    "s5": "1S20 3C32 1S30 2S01",
    "tail": (
        "mM00 2S10 5C00 2S02",
        "3C21 4C01 2S11 3C22",
        "4C02 6B00 2S12 2S20",
        "6C00 3S00 5C01 2S21",
        "2S30 5C02 2S22 2S31",
        "7C00 mM10 2S32 3S10",
        "6C01 3S01 3S11 3S02",
        "3S12 6C02 3S20 3S30",
        "4S00 3S21 3S31 4S01",
        "3S22 3S32 4S02 7C01",
        "8C00 7C02 5S00 mM20",
        "5S01 5S02 8C02 6S00",
        "8C01 6S01 6S02 9C00",
        "7S00 mM30 9C01 7S01",
        "7S02 8S00 9C02 8S01",
        "mM40 8S02 9S00 9S01",
        "9S02",
    ),
}


def ticks(hub, name):
    words = TICKS.get(name, ())
    for word in " ".join((words,) if isinstance(words, str) else words).split():
        hub.event(word[0], word[1], int(word[2]), int(word[3]))


def loop_ticks(hub, name, index, names):
    for k, at in enumerate(names):
        if at in TICKS:
            @pl.when(index == k)
            def _():
                ticks(hub, at)


def attention_unit(hub, unit, grad, low, mixed, q, k, v, lse, reach, slope, x, y, w, up, dq, dk, dv):
    tag = unit.lower()

    def cast(rows):
        low[rows, :] = grad[rows, :].astype(BF16)

    def chunk(j, grads, side):
        ticks(hub, f"{tag}{j}n")
        for n in range(grads.shape[1] // 256):
            hub.put(unit, j, FIRST_SLOT[unit] + j, 256 * n,
                    tn(grads[:, 256 * n : 256 * n + 256], side[...]))
        hub.begin(unit, j)
        ticks(hub, f"{tag}{j + 1 if j else 0}")

    rows_loop(grad.shape[0], 128, cast)
    chunk(0, mixed, low)
    project(low, w.at[3], up)
    ticks(hub, f"{tag}1")
    attend_back(q, k, v, up, mixed, lse, reach, slope, dq, dk, dv,
                lambda hp: loop_ticks(hub, tag, hp, [f"{tag}h{i}" for i in range(6)]))
    chunk(1, dq, x)
    chunk(2, dk, y)
    chunk(3, dv, y)


class Loads:
    def __init__(self, sems):
        self.sems, self.next = sems, 0

    def start(self, src, dst):
        copy = pltpu.make_async_copy(src, dst, self.sems.at[self.next])
        self.next += 1
        copy.start()
        return copy


def backward_body(*refs):
    (h_two, h_cot, h_in, h_out, h_w, h_cq, h_ck, h_cv, h_cm, h_rlow, h_olow,
     h_sq, h_sk, h_sv, h_sm, h_normed, h_one, h_opt, h_radar, h_reach,
     c_lse, s_lse), refs = refs[:22], refs[22:]
    parts, slopes, refs = refs[:7], refs[7], refs[8:]
    (o_merged, o_radar, o_opt, o_fin, o_fout, o_all, o_small), refs = refs[:7], refs[7:]
    vectors, refs = refs[0], refs[1:]
    (g, rc, r1, r2, rn, zb, rz, rf, wa, wb, q, k, v, mixed, x, y, two, two_grad, out, pull, one,
     cot, low, up, dq, dk, dv, reach, sm, sq), sems = refs[:30], refs[30:]
    hub = Sums((g, rc, r1, r2, rn, zb, rz, rf, o_all) + tuple(sems[:14]) + (sm, sq) + tuple(sems[14:16]))
    hub.out = {"A": o_fin, "B": o_fout}
    load = Loads(sems[16])
    tile_sems = sems[17]
    slope = slope_of(slopes, lax.axis_index("head"))
    gain_s, gain_r, gain_o, gain_f, shift_f, b_out = (
        vectors.at[i : i + 1, :] for i in range(6)
    )
    n = two.shape[0]
    width = wb.shape[1]
    steps = h_in.shape[1] // width

    def tile(i):
        at = pl.ds(pl.multiple_of(i * width, width), width)
        slot = i % 2
        return (
            pltpu.make_async_copy(h_in.at[:, at], wb.at[2 * slot], tile_sems.at[slot, 0]),
            pltpu.make_async_copy(h_out.at[at, :], wb.at[2 * slot + 1], tile_sems.at[slot, 1]),
        )

    first = [load.start(h_two, two), load.start(h_cot, cot)]
    for copy in tile(0):
        copy.start()
    later = [load.start(a, b) for a, b in (
        (h_cm, mixed), (h_w.at[pl.ds(4, 4)], wa), (h_cq, q), (h_ck, k), (h_cv, v),
        (h_rlow, x), (h_olow, y), (h_one, one), (h_reach, reach))]
    load_vectors(parts, vectors)
    greet((CORE, X_BIT, Y_BIT, Z_NEAR, Z_FAR))
    sm[0] = jnp.zeros_like(sm[0])
    out[...] = jnp.zeros_like(out)
    pull[...] = jnp.zeros_like(pull)
    first[0].wait()
    norm_rows(two, gain_f, shift_f, low)
    first[1].wait()

    def feed(i, _):
        for copy in tile(i):
            copy.wait()

        @pl.when(i < steps - 1)
        def _():
            for copy in tile(i + 1):
                copy.start()

        w_in, w_out = wb.at[2 * (i % 2)], wb.at[2 * (i % 2) + 1]
        for m in range(width // 256):
            at = slice(m * 256, (m + 1) * 256)
            h = nn(low[...], w_in[:, at]) + vectors[pl.ds(6 + i, 1), at]
            t = jnp.tanh(0.7978845608028654 * h * (1.0 + 0.044715 * h * h))
            half = 0.5 * (1.0 + t)
            hidden = (h * half).astype(BF16)
            rise = half + 0.5 * h * (1.0 - t * t) * (
                0.7978845608028654 * (1.0 + 3 * 0.044715 * h * h)
            )
            grad = (nt(cot[...], w_out[at, :]) * rise).astype(BF16)
            sm[0, pl.ds(24 + i, 1), at] = jnp.sum(grad.astype(F32), axis=0, keepdims=True)
            out[...] += nn(hidden, w_out[at, :])
            pull[...] += nt(grad, w_in[:, at])
            hub.put("A", 0, i, 256 * m, tn(grad, low[...]))
            hub.put("B", 0, 4 + i, 256 * m, tn(hidden, cot[...]))
            if m == width // 256 - 1:
                hub.begin("A", i)
                hub.begin("B", i)
            loop_ticks(hub, "f", i, [f"f{s}{'abc'[m]}" for s in range(4)])
        return 0

    lax.fori_loop(0, steps, feed, 0)
    self_w = load.start(h_w.at[pl.ds(0, 4)], wb)

    def close(rows):
        value, cotangent = two[rows, :], cot[rows, :].astype(F32)
        dv[rows, :] = (value + out[rows, :] + b_out[...]).astype(BF16)
        dval, dgain, dshift = norm_back_rows(value, gain_f[...], pull[rows, :])
        total = cotangent + dval
        two_grad[rows, :] = total
        sm[0, 0:1, :] += dgain
        sm[0, 1:2, :] += dshift
        sm[0, 2:3, :] += jnp.sum(cotangent, axis=0, keepdims=True)
        sm[0, 3:4, :] += jnp.sum(total, axis=0, keepdims=True)

    rows_loop(n, 128, close)
    stores = [load.start(dv, o_merged)]
    opt_load = load.start(h_opt, cot)
    ticks(hub, "g")
    for copy in later:
        copy.wait()
    stores[0].wait()
    attention_unit(hub, "C", two_grad, low, mixed, q, k, v, c_lse, reach, slope, x, y, wa,
                   up, dq, dk, dv)
    later = [load.start(a, b) for a, b in (
        (h_sm, mixed), (h_sq, q), (h_sk, k), (h_sv, v), (h_normed, x), (h_radar, y))]
    opt_load.wait()

    def cross(rows):
        dval, dgain, dshift = norm_back_rows(one[rows, :], gain_r[...], nn(dq[rows, :], wa[0]))
        total = two_grad[rows, :] + dval
        out[rows, :] = total
        sm[0, 8:9, :] += dgain
        sm[0, 9:10, :] += dshift
        sm[0, 12:13, :] += jnp.sum(total, axis=0, keepdims=True)
        dval, dgain, dshift = norm_back_rows(
            cot[rows, :].astype(F32), gain_o[...], nn(dk[rows, :], wa[1]) + nn(dv[rows, :], wa[2])
        )
        pull[rows, :] = dval
        sm[0, 10:11, :] += dgain
        sm[0, 11:12, :] += dshift

    rows_loop(n, 256, cross)
    stores = [load.start(pull, o_opt)]
    ticks(hub, "c5")
    for copy in later:
        copy.wait()
    self_w.wait()
    attention_unit(hub, "S", out, low, mixed, q, k, v, s_lse, reach, slope, x, x, wb,
                   up, dq, dk, dv)

    def own(rows):
        dval, dgain, dshift = norm_back_rows(
            y[rows, :].astype(F32), gain_s[...],
            nn(dq[rows, :], wb[0]) + nn(dk[rows, :], wb[1]) + nn(dv[rows, :], wb[2]),
        )
        two[rows, :] = out[rows, :] + dval
        sm[0, 16:17, :] += dgain
        sm[0, 17:18, :] += dshift

    rows_loop(n, 256, own)
    stores.append(load.start(two, o_radar))
    hub.small_copy(0).start()
    ticks(hub, "s5")
    ticks(hub, "tail")
    o_small[...] = sm[5]
    for copy in stores:
        copy.wait()


def run_backward(two, cot, feed_in, feed_out, w, cross, own, one, optical, radar, reach,
                 c_lse, s_lse, vectors, slopes):
    n, d = two.shape
    low, wide = pltpu.VMEM((n, d), BF16), pltpu.VMEM((n, d), F32)
    chunk = lambda *dims: pltpu.VMEM(dims + (96, d), BF16)
    sems = lambda *dims: pltpu.SemaphoreType.DMA(dims)
    parts = max(PARTS.values())
    return pl.pallas_call(
        backward_body,
        out_shape=[
            shape((n, d), BF16), shape((n, d), F32), shape((n, d), F32),
            shape((96, d), F32), shape((96, d), F32), shape((2, 8, 96, d), BF16),
            shape((32, d), F32),
        ],
        in_specs=[HBM] * 20 + [VMEM] * (2 + len(vectors)) + [SMEM],
        out_specs=[HBM] * 3 + [VMEM] * 4,
        scratch_shapes=[
            pltpu.VMEM((16, d), F32),
            chunk(8, 8), chunk(8, 4), chunk(14, 2), chunk(14, 1), chunk(2, 4),
            chunk(4, 4), chunk(4, 2), chunk(4, 1),
            pltpu.VMEM((4, d, d), BF16), pltpu.VMEM((4, d, d), BF16),
            low, low, low, low, low, low, wide, wide, wide, wide, wide,
            low, low, low, low, low, low, pltpu.VMEM((n, n), F32),
            pltpu.VMEM((6, 32, d), F32), pltpu.VMEM((5, 32, d), F32),
            sems(8), sems(8), sems(14, parts), sems(14, parts), sems(14, parts), sems(14, parts),
            sems(2), sems(2), sems(4, parts), sems(4, parts), sems(4, parts), sems(4, parts),
            sems(2, 3, parts), sems(2, 3, parts), sems(5), sems(5),
            sems(24), sems(2, 2),
        ],
        compiler_params=pltpu.CompilerParams(
            vmem_limit_bytes=LIMIT, collective_id=1, has_side_effects=True
        ),
        name="backward",
        cost_estimate=pl.CostEstimate(flops=35 * 10**9, bytes_accessed=5 * 10**7, transcendentals=0),
    )(two, cot, feed_in, feed_out, w, *cross, *own, one, optical, radar, reach,
      c_lse, s_lse, *vectors, slopes)


def call(body, outs, scratch, operands, in_specs, **more):
    return pl.pallas_call(
        body,
        out_shape=outs,
        in_specs=in_specs,
        out_specs=[VMEM] * len(outs),
        scratch_shapes=scratch,
        compiler_params=pltpu.CompilerParams(vmem_limit_bytes=LIMIT),
        **more,
    )(*operands)


def run_feed(place, two, cot, gain, shift, w_in, b_in, w_out, b_out):
    n, d = two.shape
    f = w_in.shape[1]
    tile = 768
    whole = lambda *dims: pl.BlockSpec(dims, lambda i, p: (0,) * len(dims))
    slots = pl.BlockSpec((2, 2, 1, 96, d), lambda i, p: (0, 0, i ^ p[0], 0, 0))
    grad = shape((2, 2, 4, 96, d), BF16)
    return pl.pallas_call(
        feed_step,
        grid_spec=pltpu.PrefetchScalarGridSpec(
            num_scalar_prefetch=1,
            grid=(f // tile,),
            in_specs=[
                whole(n, d), whole(n, d), whole(1, d), whole(1, d),
                pl.BlockSpec((d, tile), lambda i, p: (0, i)),
                pl.BlockSpec((1, tile), lambda i, p: (0, i)),
                pl.BlockSpec((tile, d), lambda i, p: (i, 0)),
                whole(1, d),
            ],
            out_specs=[
                whole(n, d), whole(n, d), slots, slots, slots, slots,
                pl.BlockSpec((1, 1, tile), lambda i, p: (i, 0, 0)),
                whole(8, d),
            ],
            scratch_shapes=[
                pltpu.VMEM((n, d), BF16), pltpu.VMEM((n, d), F32), pltpu.VMEM((n, d), F32),
                pltpu.VMEM((tile, d), BF16), pltpu.VMEM((tile, d), BF16),
            ],
        ),
        out_shape=[
            shape((n, d), BF16), shape((n, d), F32), grad, grad, grad, grad,
            shape((f // tile, 1, tile), F32), shape((8, d), F32),
        ],
        compiler_params=pltpu.CompilerParams(vmem_limit_bytes=LIMIT),
        name="feed",
        cost_estimate=pl.CostEstimate(flops=15 * 10**9, bytes_accessed=25 * 10**6, transcendentals=0),
    )(place, two, cot, gain, shift, w_in, b_in, w_out, b_out)


def back_scratch(n, d):
    low = pltpu.VMEM((n, d), BF16)
    return [low, pltpu.VMEM((d, d), BF16), low, low, low, low]


def run_cross_backward(place, two_grad, mixed, q, k, v, lse, reach, slope, radar_low, optical_low,
                       w, one, optical, gain_r, gain_o):
    n, d = one.shape
    grad = shape((2, 2, 4, 96, d), BF16)
    wide = shape((n, d), F32)
    return call(
        cross_backward,
        [wide, wide, grad, grad, shape((8, d), F32)],
        back_scratch(n, d),
        (place, two_grad, mixed, q, k, v, lse, reach, slope, radar_low, optical_low,
         w, one, optical, gain_r, gain_o),
        [SMEM] + [VMEM] * 7 + [SMEM] + [VMEM] * 7,
        name="cross_backward",
        cost_estimate=pl.CostEstimate(flops=12 * 10**9, bytes_accessed=25 * 10**6, transcendentals=0),
    )


def run_self_backward(place, one_grad, mixed, q, k, v, lse, reach, slope, normed, w, radar, gain):
    n, d = one_grad.shape
    grad = shape((2, 2, 4, 96, d), BF16)
    return call(
        self_backward,
        [shape((n, d), F32), grad, grad, shape((8, d), F32)],
        back_scratch(n, d),
        (place, one_grad, mixed, q, k, v, lse, reach, slope, normed, w, radar, gain),
        [SMEM] + [VMEM] * 7 + [SMEM] + [VMEM] * 4,
        name="self_backward",
        cost_estimate=pl.CostEstimate(flops=12 * 10**9, bytes_accessed=25 * 10**6, transcendentals=0),
    )


def finish(bias_part, got, small, merged, radar, optical, fin, fout, *refs):
    outs, sems = refs[:-1], refs[-1]
    moves = [
        pltpu.make_async_copy(src, dst, sems.at[i])
        for i, (src, dst) in enumerate(zip((merged, radar, optical, fin, fout), outs))
    ]
    for copy in moves:
        copy.start()
    mats, vectors, bias = outs[5:13], outs[13:24], outs[24]
    for u, unit in enumerate("CS"):
        size = 96 // PARTS[unit]
        for mat in range(4):
            for half in range(2):
                for part in range(PARTS[unit]):
                    at = gathered_at(unit, part, half, mat % 2, mat // 2)
                    rows = slice(96 * half + part * size, 96 * half + (part + 1) * size)
                    mats[4 * u + mat][rows, :] = got[
                        u, at, part * size : (part + 1) * size, :
                    ].astype(F32)
    for row, dst in zip((16, 17, 12, 8, 9, 10, 11, 3, 0, 1, 2), vectors):
        dst[...] = small[row : row + 1, :].reshape(dst.shape)
    mine, per = bias_part[0], small.shape[1] // bias.shape[0]
    line = small[pl.ds(24 + mine // per, 1), :]
    shift = (small.shape[1] - mine % per * bias.shape[0]) % small.shape[1]
    bias[...] = pltpu.roll(line, shift, 1)[:, : bias.shape[0]].reshape(bias.shape)
    for copy in moves:
        copy.wait()


def run_finish(mine, got, small, merged, radar, optical, fin, fout):
    d = got.shape[-1]
    moved = (merged, radar, optical, fin, fout)
    outs = pl.pallas_call(
        finish,
        out_shape=[shape(a.shape, a.dtype) for a in moved]
        + [shape((192, d), F32)] * 8 + [shape((d,), F32)] * 11 + [shape((96,), F32)],
        in_specs=[SMEM] + [VMEM] * 7,
        out_specs=[HBM] * 5 + [VMEM] * 20,
        scratch_shapes=[pltpu.SemaphoreType.DMA((5,))],
        compiler_params=pltpu.CompilerParams(vmem_limit_bytes=LIMIT),
        name="finish",
    )(mine.reshape(1), got, small, *moved)
    mats = [o if i % 4 == 3 else o.T for i, o in enumerate(outs[5:13])]
    return outs[:5], mats[:4], mats[4:], outs[13:24], outs[24]


def shards(
    radar, optical, patch_table, cotangent, norm_self_gain, norm_self_shift,
    self_query, self_key, self_value, self_out, self_out_bias, norm_radar_gain, norm_radar_shift,
    norm_optical_gain, norm_optical_shift, cross_query, cross_key, cross_value, cross_out,
    cross_out_bias, norm_feed_gain, norm_feed_shift, feed_in, feed_in_bias, feed_out, feed_out_bias,
):
    dp, head = lax.axis_size("dp"), lax.axis_size("head")
    near = (dp, head) == (8, 4)
    row = lambda v: v.reshape(1, -1)
    zero = jnp.int32(0)
    slopes = jnp.asarray(-np.exp2(-8.0 * np.arange(1, HEADS + 1) / HEADS), F32)
    mine = (lax.axis_index("dp") * head + lax.axis_index("head")).astype(jnp.int32)
    place = jnp.stack([zero] * 4)
    weights = (self_query, self_key, self_value, self_out,
               cross_query, cross_key, cross_value, cross_out)
    weights = tuple(w if i % 4 == 3 else w.T for i, w in enumerate(weights))
    if not near:
        w = lax.all_gather(jnp.stack(weights), "head", axis=1, tiled=True)
        weights = (w,)
    vectors = (norm_self_gain, norm_self_shift, norm_radar_gain, norm_radar_shift,
               norm_optical_gain, norm_optical_shift, self_out_bias, cross_out_bias)
    got = run_forward(near, radar, optical, vectors, patch_table, slopes, weights)
    if near:
        w, got = got[0], got[1:]
    (normed, radar_low, optical_low, sq, sk, sv, cq, ck, cv, s_mixed, c_mixed, s_lse, c_lse,
     two, one, reach) = got
    d = radar.shape[1]
    if near:
        merged, radar_grad, optical_grad, feed_in_grad, feed_out_grad, got, small = run_backward(
            two, cotangent, feed_in, feed_out, w,
            (cq, ck, cv, c_mixed, radar_low, optical_low), (sq, sk, sv, s_mixed, normed),
            one, optical, radar, reach,
            c_lse, s_lse,
            (norm_self_gain, norm_radar_gain, norm_optical_gain, norm_feed_gain, norm_feed_shift,
             feed_out_bias, feed_in_bias),
            slopes,
        )
        ((merged, radar_grad, optical_grad, feed_in_grad, feed_out_grad), cross, own, vectors,
         feed_in_bias_grad) = run_finish(
            mine, got, small, merged, radar_grad, optical_grad, feed_in_grad, feed_out_grad)
    else:
        merged, two_grad, in_keep, in_send, out_keep, out_send, bias_in, feed_small = run_feed(
            place, two, cotangent, row(norm_feed_gain), row(norm_feed_shift),
            feed_in, row(feed_in_bias), feed_out, row(feed_out_bias),
        )
        one_grad, optical_grad, cross_keep, cross_send, cross_small = run_cross_backward(
            place, two_grad, c_mixed, cq, ck, cv, c_lse, reach, slopes, radar_low, optical_low,
            w[4:], one, optical, row(norm_radar_gain), row(norm_optical_gain),
        )
        radar_grad, self_keep, self_send, self_small = run_self_backward(
            place, one_grad, s_mixed, sq, sk, sv, s_lse, reach, slopes, normed,
            w[:4], radar, row(norm_self_gain),
        )
        small = jnp.concatenate([feed_small, cross_small, self_small, bias_in.reshape(-1, d)])
        def logical(keep, send, order):
            both = jnp.stack([keep, send])
            return jnp.transpose(both, order).reshape(-1, d)

        def feed_sum(keep, send):
            return lax.psum_scatter(
                logical(keep, send, (3, 2, 1, 0, 4, 5)).astype(F32),
                ("dp", "head"), scatter_dimension=0, tiled=True,
            )

        def attn_sum(keep, send):
            total = logical(keep, send, (3, 1, 0, 2, 4, 5)).astype(F32).reshape(4, -1, d)
            total = lax.psum_scatter(total, "head", scatter_dimension=1, tiled=True)
            total = lax.psum(total, "dp")
            return total[0].T, total[1].T, total[2].T, total[3]

        feed_in_grad, feed_out_grad = feed_sum(in_keep, in_send), feed_sum(out_keep, out_send)
        cross, own = attn_sum(cross_keep, cross_send), attn_sum(self_keep, self_send)
        small = lax.psum(small, ("dp", "head"))
        vectors = [small[i] for i in (16, 17, 12, 8, 9, 10, 11, 3, 0, 1, 2)]
        bias_part = feed_in_bias.shape[0] // (dp * head)
        feed_in_bias_grad = lax.dynamic_slice_in_dim(
            small[24:28].reshape(-1), mine * bias_part, bias_part
        )
    return (
        merged, radar_grad, optical_grad, vectors[0], vectors[1], *own, *vectors[2:7],
        *cross, *vectors[7:10], feed_in_grad.T, feed_in_bias_grad, feed_out_grad, vectors[10],
    )


def solution(mesh):
    token, rep = P(("dp", "head"), None), P()
    col, row = P(None, "head"), P("head", None)
    in_specs = (
        token, token, P(None, ("dp", "head")), token,
        rep, rep, col, col, col, row, rep,
        rep, rep, rep, rep, col, col, col, row, rep,
        rep, rep, rep, rep, rep, rep,
    )
    out_specs = (
        token, token, token,
        rep, rep, col, col, col, row, rep,
        rep, rep, rep, rep, col, col, col, row, rep,
        rep, rep, P(None, ("dp", "head")), P(("dp", "head")), token, rep,
    )
    return jax.shard_map(shards, mesh=mesh, in_specs=in_specs, out_specs=out_specs, check_vma=False)
```

```python
import functools

import jax
import jax.numpy as jnp
import numpy as np
from jax import lax
from jax.experimental import pallas as pl
from jax.experimental.pallas import tpu as pltpu
from jax.sharding import PartitionSpec as P

F32, BF16 = jnp.float32, jnp.bfloat16
HEADS, HEAD_DIM = 12, 64
EPSILON = 1e-06
FAR = 1e12
LIMIT = 62 * 2**20
VMEM = pl.BlockSpec(memory_space=pltpu.VMEM)
SMEM = pl.BlockSpec(memory_space=pltpu.SMEM)
HBM = pl.BlockSpec(memory_space=pl.ANY)


def nn(a, b):
    return lax.dot_general(a, b, (((1,), (0,)), ((), ())), preferred_element_type=F32)


def nt(a, b):
    return lax.dot_general(a, b, (((1,), (1,)), ((), ())), preferred_element_type=F32)


def tn(a, b):
    return lax.dot_general(a, b, (((0,), (0,)), ((), ())), preferred_element_type=F32)


def rows_loop(total, block, body):
    def step(i, _):
        body(pl.ds(pl.multiple_of(i * block, block), block))
        return 0

    lax.fori_loop(0, total // block, step, 0)


def centred(v):
    c = v - jnp.mean(v, axis=-1, keepdims=True)
    return c, lax.rsqrt(jnp.mean(c * c, axis=-1, keepdims=True) + EPSILON)


def norm_rows(src, gain, shift, dst):
    def body(rows):
        c, r = centred(src[rows, :].astype(F32))
        dst[rows, :] = (c * r * gain[...] + shift[...]).astype(BF16)

    rows_loop(src.shape[0], 128, body)


def norm_back_rows(v, gain, u):
    c, r = centred(v)
    hat = c * r
    w = u * gain
    dv = r * (
        w
        - jnp.mean(w, axis=-1, keepdims=True)
        - hat * jnp.mean(w * hat, axis=-1, keepdims=True)
    )
    return dv, jnp.sum(u * hat, axis=0, keepdims=True), jnp.sum(u, axis=0, keepdims=True)


def project(x, w, dst, scale=None, half=None):
    total = w.shape[0]
    if half is None:
        blocks = [(i, 256) for i in range(0, total, 256)]
    else:
        blocks = [(half * total // 2, 256), (half * total // 2 + 256, total // 2 - 256)]
    for at, size in blocks:
        cols = slice(at, at + size)
        y = nt(x[...], w[cols, :])
        dst[:, cols] = (y if scale is None else y * scale).astype(BF16)


def fill_reach(table, columns, reach):
    for i in range(3):
        line = table[i : i + 1, :].astype(F32)
        columns[i] = jnp.broadcast_to(line, (128, line.shape[1])).T

    def body(rows):
        seg, down, across = (
            columns[i, rows, 0:1] - table[i : i + 1, :].astype(F32) for i in range(3)
        )
        reach[rows, :] = jnp.where(seg == 0, jnp.sqrt(down * down + across * across), FAR)

    rows_loop(reach.shape[0], 64, body)


def slope_of(table, group):
    return lambda h: table[3 * (h // 3 ^ group) + h % 3]


def low_half(length):
    return lax.broadcasted_iota(jnp.int32, (length, 128), 1) < HEAD_DIM


def attend(q, k, v, reach, slope, mixed, lse, tick, pairs):
    lo = low_half(q.shape[0])

    def pair(hp, _):
        tick(hp)
        at = pl.ds(pl.multiple_of(hp * 128, 128), 128)
        qs, ks, vs = q[:, at], k[:, at], v[:, at]
        outs, tops = [], []
        for sub in range(2):
            mine = lo if sub == 0 else jnp.logical_not(lo)
            s = nt(jnp.where(mine, qs, jnp.zeros_like(qs)), ks)
            s = s + slope(2 * hp + sub) * reach[...]
            top = jnp.max(s, axis=-1, keepdims=True)
            e = jnp.exp(s - top).astype(BF16)
            outs.append(nn(e, jnp.where(mine, vs, jnp.ones_like(vs))))
            tops.append(top)
        num = jnp.where(lo, outs[0], outs[1])
        den = pltpu.roll(jnp.where(lo, outs[1], outs[0]), HEAD_DIM, 1)
        mixed[:, at] = (num / den).astype(BF16)
        lse_t = (jnp.where(lo, tops[0], tops[1]) + jnp.log(den)).T
        lse[hp] = jnp.concatenate([lse_t[0:1], lse_t[HEAD_DIM : HEAD_DIM + 1]], axis=0)
        return 0

    lax.fori_loop(*pairs, pair, 0)


def attend_back(q, k, v, up, mixed, lse, reach, slope, dq, dk, dv, tick=lambda hp: None):
    lo = low_half(q.shape[0])

    def pair(hp, _):
        tick(hp)
        at = pl.ds(pl.multiple_of(hp * 128, 128), 128)
        qs, ks, vs, ups = q[:, at], k[:, at], v[:, at], up[:, at]
        prod = (ups.astype(F32) * mixed[:, at].astype(F32)).T
        tops = lse[hp]
        dqs, dks, dvs = [], [], []
        for sub in range(2):
            mine = lo if sub == 0 else jnp.logical_not(lo)
            delta = jnp.sum(prod[sub * HEAD_DIM : (sub + 1) * HEAD_DIM], axis=0, keepdims=True)
            s = nt(jnp.where(mine, ks, jnp.zeros_like(ks)), qs)
            p = jnp.exp(s + slope(2 * hp + sub) * reach[...] - tops[sub : sub + 1])
            dp = nt(jnp.where(mine, vs, jnp.zeros_like(vs)), ups)
            ds = (p * (dp - delta)).astype(BF16)
            dvs.append(nn(p.astype(BF16), ups))
            dks.append(nn(ds, qs))
            dqs.append(tn(ds, ks))
        dq[:, at] = (jnp.where(lo, dqs[0], dqs[1]) * HEAD_DIM**-0.5).astype(BF16)
        dk[:, at] = jnp.where(lo, dks[0], dks[1]).astype(BF16)
        dv[:, at] = jnp.where(lo, dvs[0], dvs[1]).astype(BF16)
        return 0

    lax.fori_loop(0, q.shape[1] // 128, pair, 0)


def add_out(base, mixed, w_out, bias, dst):
    def body(cols):
        y = nn(mixed[...], w_out[:, cols])
        dst[:, cols] = base[:, cols].astype(F32) + y + bias[:, cols]

    rows_loop(w_out.shape[1], 256, body)


def place_shards(full, place, at, keep, send):
    my, mx, mc = place[1], place[2], place[3]
    for x in range(2):
        for y in range(2):
            for c, dst in enumerate((keep, send)):
                row = (((y ^ my) * 2 + (x ^ mx)) * 2 + (c ^ mc)) * 96
                dst[x, y, at] = full[pl.ds(pl.multiple_of(row, 96), 96), :]


def feed_step(place, two, cot, gain, shift, w_in, b_in, w_out, b_out,
              merged, two_grad, keep_in, send_in, keep_out, send_out, bias_in, small,
              low, out, pull, full_in, full_out):
    step = pl.program_id(0)
    width = w_out.shape[0]
    block = 256

    @pl.when(step == 0)
    def _():
        norm_rows(two, gain, shift, low)

    for n in range(width // block):
        at = slice(n * block, (n + 1) * block)
        x = nn(low[...], w_in[:, at]) + b_in[:, at]
        inner = 0.7978845608028654 * x * (1.0 + 0.044715 * x * x)
        t = jnp.tanh(inner)
        half = 0.5 * (1.0 + t)
        hidden = (x * half).astype(BF16)
        slope = half + 0.5 * x * (1.0 - t * t) * (
            0.7978845608028654 * (1.0 + 3 * 0.044715 * x * x)
        )
        grad = (nt(cot[...], w_out[at, :]) * slope).astype(BF16)
        bias_in[0, :, at] = jnp.sum(grad.astype(F32), axis=0, keepdims=True)
        part_out = nn(hidden, w_out[at, :])
        part_pull = nt(grad, w_in[:, at])
        if n == 0:
            @pl.when(step == 0)
            def _():
                out[...] = part_out
                pull[...] = part_pull

            @pl.when(step > 0)
            def _():
                out[...] += part_out
                pull[...] += part_pull
        else:
            out[...] += part_out
            pull[...] += part_pull
        full_out[at, :] = tn(hidden, cot[...]).astype(BF16)
        full_in[at, :] = tn(grad, low[...]).astype(BF16)
    place_shards(full_in, place, 0, keep_in.at[:, :], send_in.at[:, :])
    place_shards(full_out, place, 0, keep_out.at[:, :], send_out.at[:, :])

    @pl.when(step == pl.num_programs(0) - 1)
    def _():
        small[...] = jnp.zeros_like(small)

        def body(rows):
            value, cotangent = two[rows, :], cot[rows, :].astype(F32)
            merged[rows, :] = (value + out[rows, :] + b_out[...]).astype(BF16)
            dv, dgain, dshift = norm_back_rows(value, gain[...], pull[rows, :])
            total = cotangent + dv
            two_grad[rows, :] = total
            small[0:1, :] += dgain
            small[1:2, :] += dshift
            small[2:3, :] += jnp.sum(cotangent, axis=0, keepdims=True)
            small[3:4, :] += jnp.sum(total, axis=0, keepdims=True)

        rows_loop(two.shape[0], 128, body)


def weight_grad(grads, rows, full):
    def body(cols):
        full[cols, :] = tn(grads[:, cols], rows[...]).astype(BF16)

    rows_loop(grads.shape[1], 256, body)


def attn_shards(full, place, mat, keep, send):
    my, mz = place[1], place[0]
    for x in range(2):
        for y in range(2):
            for c, dst in enumerate((keep, send)):
                row = ((x * 2 + c) * 2 + (y ^ my)) * 96
                dst[x, y, mat ^ mz] = full[pl.ds(pl.multiple_of(row, 96), 96), :]


def attention_back(place, grad, low, mixed, q, k, v, lse, reach, slope, x, y, w,
                   keep, send, full, up, dq, dk, dv):
    def cast(rows):
        low[rows, :] = grad[rows, :].astype(BF16)

    rows_loop(grad.shape[0], 128, cast)
    weight_grad(mixed, low, full)
    attn_shards(full, place, 3, keep, send)
    project(low, w.at[3], up)
    attend_back(q, k, v, up, mixed, lse, reach, slope_of(slope, 0), dq, dk, dv)
    for mat, (side, d) in enumerate(((x, dq), (y, dk), (y, dv))):
        weight_grad(d, side, full)
        attn_shards(full, place, mat, keep, send)


def cross_backward(place, two_grad, mixed, q, k, v, lse, reach, slope, radar_low, optical_low, w,
                   one, optical, gain_r, gain_o,
                   one_grad, optical_grad, keep, send, small,
                   low, full, up, dq, dk, dv):
    attention_back(place, two_grad, low, mixed, q, k, v, lse, reach, slope, radar_low, optical_low,
                   w, keep, send, full, up, dq, dk, dv)
    small[...] = jnp.zeros_like(small)

    def body(rows):
        pull = nn(dq[rows, :], w[0])
        dv_, dgain, dshift = norm_back_rows(one[rows, :], gain_r[...], pull)
        total = two_grad[rows, :] + dv_
        one_grad[rows, :] = total
        small[0:1, :] += dgain
        small[1:2, :] += dshift
        small[4:5, :] += jnp.sum(total, axis=0, keepdims=True)
        pull = nn(dk[rows, :], w[1]) + nn(dv[rows, :], w[2])
        dv_, dgain, dshift = norm_back_rows(optical[rows, :].astype(F32), gain_o[...], pull)
        optical_grad[rows, :] = dv_
        small[2:3, :] += dgain
        small[3:4, :] += dshift

    rows_loop(two_grad.shape[0], 256, body)


def self_backward(place, one_grad, mixed, q, k, v, lse, reach, slope, normed, w, radar, gain,
                  radar_grad, keep, send, small,
                  low, full, up, dq, dk, dv):
    attention_back(place, one_grad, low, mixed, q, k, v, lse, reach, slope, normed, normed,
                   w, keep, send, full, up, dq, dk, dv)
    small[...] = jnp.zeros_like(small)

    def body(rows):
        pull = nn(dq[rows, :], w[0]) + nn(dk[rows, :], w[1]) + nn(dv[rows, :], w[2])
        dv_, dgain, dshift = norm_back_rows(radar[rows, :].astype(F32), gain[...], pull)
        radar_grad[rows, :] = one_grad[rows, :] + dv_
        small[0:1, :] += dgain
        small[1:2, :] += dshift

    rows_loop(one_grad.shape[0], 256, body)


def shape(dims, dtype):
    return jax.ShapeDtypeStruct(dims, dtype)


CORE, X_BIT, Y_BIT, Z_NEAR, Z_FAR = 1, 2, 4, 8, 16


def partner(bit):
    dp, head = lax.axis_index("dp"), lax.axis_index("head")
    if bit < 4:
        return (dp, head ^ bit)
    return (dp ^ (bit // 4), head)


def greet(bits):
    greeting(bits)
    pl.semaphore_wait(pltpu.get_barrier_semaphore(), len(bits))


def greeting(bits):
    barrier = pltpu.get_barrier_semaphore()
    for bit in bits:
        pl.semaphore_signal(
            barrier, inc=1, device_id=partner(bit), device_id_type=pl.DeviceIdType.MESH
        )


def send_to(bit, src, dst, send_sem, recv_sem):
    return pltpu.make_async_remote_copy(
        src_ref=src, dst_ref=dst, send_sem=send_sem, recv_sem=recv_sem,
        device_id=partner(bit), device_id_type=pl.DeviceIdType.MESH,
    )


ORDER = (0, 1, 2, 3, 5, 6, 4, 7)


class Gather:
    def __init__(self, w, send, recv):
        self.w, self.send, self.recv = w, send, recv
        self.mine = lax.axis_index("dp") % 2
        self.part = w.shape[1] // 4

    def copy(self, mat, kind):
        part, half = self.part, self.part // 2
        own = pl.ds(self.mine * half, half)
        far = pl.ds(2 * part + self.mine * half, half)
        other = pl.ds(2 * part + (1 - self.mine) * half, half)
        w = self.w.at[mat]
        up = lambda rows: pl.ds(rows.start + part, rows.size)
        bit, src, dst = (
            (CORE, pl.ds(0, part), pl.ds(part, part)),
            (X_BIT, own, far),
            (Y_BIT, far, far),
            (CORE, far, up(far)),
            (CORE, other, up(other)),
        )[kind]
        return send_to(bit, w.at[src], w.at[dst], self.send.at[mat, kind], self.recv.at[mat, kind])

    def begin(self, mat):
        self.copy(mat, 1).start()
        self.copy(mat, 0).start()

    def after_x(self, mat):
        self.copy(mat, 1).wait_recv()
        self.copy(mat, 2).start()
        self.copy(mat, 3).start()

    def after_y(self, mat):
        self.copy(mat, 2).wait_recv()
        self.copy(mat, 4).start()

    def core_ready(self, mat):
        self.copy(mat, 0).wait_recv()

    def ready(self, mat):
        for kind in (3, 4):
            self.copy(mat, kind).wait_recv()

    def drain(self, mat):
        for kind in range(5):
            self.copy(mat, kind).wait_send()


ROOT, CUBE = 0.7978845608028654, 0.044715


def load_vectors(parts, vectors):
    d = vectors.shape[1]
    at = 0
    for part in parts:
        for i in range(part.shape[0] // d):
            vectors[at : at + 1, :] = part[i * d : (i + 1) * d].reshape(1, d)
            at += 1


def forward_body(remote, *refs):
    (radar, optical, table, slopes), refs = refs[:4], refs[4:]
    parts, refs = refs[:8], refs[8:]
    owns, refs = refs[: 8 if remote else 1], refs[8 if remote else 1 :]
    outs, refs = refs[: 17 if remote else 16], refs[17 if remote else 16 :]
    vectors, columns, store_sems = refs[:3]
    refs = refs[3:]
    w, refs = (refs[0], refs[1:]) if remote else (owns[0], refs)
    kept = refs[:16]
    (normed, radar_low, optical_low, sq, sk, sv, cq, ck, cv, s_mixed, c_mixed, s_lse, c_lse,
     two, one, reach) = kept
    if remote:
        o_w, outs = outs[0], outs[1:]
        hub = Gather(w, *refs[16:])
        part = w.shape[1] // 4
        greet((CORE, X_BIT, Y_BIT))
        for mat in ORDER:
            w[mat, 0:part, :] = owns[mat][...]
            hub.begin(mat)
        slope = slope_of(slopes, lax.axis_index("head"))
    else:
        slope = slope_of(slopes, 0)
    load_vectors(parts, vectors)
    gain_s, shift_s, gain_r, shift_r, gain_o, shift_o, bias_s, bias_c = (
        vectors.at[i : i + 1, :] for i in range(8)
    )
    stores = []

    def store(src, dst):
        copy = pltpu.make_async_copy(src, dst, store_sems.at[len(stores)])
        stores.append(copy)
        copy.start()

    def done(*names):
        for ref in names:
            i = [r is ref for r in kept].index(True)
            store(ref, outs[i])

    def hop(kind, *places):
        if remote:
            for i in places:
                (hub.after_x if kind == "x" else hub.after_y)(ORDER[i])

    near_here = []

    def core_ready(*mats):
        if remote:
            for mat in mats:
                hub.core_ready(mat)
                near_here.append(mat)

    def ready(mat):
        if mat not in near_here:
            core_ready(mat)
        if remote:
            hub.ready(mat)
            store(w.at[mat], o_w.at[mat])

    def loop_hops(index, at):
        for k, hops in at.items():
            @pl.when(index == k)
            def _():
                for kind, place in hops:
                    hop(kind, place)

    scale = HEAD_DIM**-0.5
    norm_rows(radar, gain_s, shift_s, normed)
    done(normed)
    fill_reach(table, columns, reach)
    done(reach)
    norm_rows(optical, gain_o, shift_o, optical_low)
    done(optical_low)
    core_ready(0, 1, 2)
    project(normed, w.at[0], sq, scale, 0)
    project(normed, w.at[1], sk, None, 0)
    project(normed, w.at[2], sv, None, 0)
    attend(sq, sk, sv, reach, slope, s_mixed, s_lse,
           lambda hp: loop_hops(hp, {2: (("x", 0),)}), (0, 3))
    core_ready(5, 6)
    project(optical_low, w.at[5], ck, None, 0)
    hop("x", 1)
    project(optical_low, w.at[6], cv, None, 0)
    hop("x", 2)
    hop("y", 0)
    ready(0)
    project(normed, w.at[0], sq, scale, 1)
    done(sq)
    hop("x", 3)
    hop("y", 1)
    ready(1)
    project(normed, w.at[1], sk, None, 1)
    done(sk)
    hop("y", 2)
    hop("x", 4)
    ready(2)
    project(normed, w.at[2], sv, None, 1)
    done(sv)
    attend(sq, sk, sv, reach, slope, s_mixed, s_lse,
           lambda hp: loop_hops(hp, {4: (("y", 3), ("x", 5))}), (3, 6))
    done(s_mixed, s_lse)
    hop("x", 6)
    hop("y", 4)
    ready(3)
    add_out(radar, s_mixed, w.at[3], bias_s, one)
    done(one)
    ready(5)
    project(optical_low, w.at[5], ck, None, 1)
    done(ck)
    norm_rows(one, gain_r, shift_r, radar_low)
    done(radar_low)
    core_ready(4)
    project(radar_low, w.at[4], cq, scale, 0)
    attend(cq, ck, cv, reach, slope, c_mixed, c_lse,
           lambda hp: loop_hops(hp, {0: (("x", 7), ("y", 5)), 2: (("y", 6),)}), (0, 3))
    ready(6)
    project(optical_low, w.at[6], cv, None, 1)
    done(cv)
    ready(4)
    project(radar_low, w.at[4], cq, scale, 1)
    done(cq)
    attend(cq, ck, cv, reach, slope, c_mixed, c_lse,
           lambda hp: loop_hops(hp, {4: (("y", 7),)}), (3, 6))
    done(c_mixed, c_lse)
    ready(7)
    add_out(one, c_mixed, w.at[7], bias_c, two)
    done(two)
    if remote:
        for mat in range(8):
            hub.drain(mat)
    for copy in stores:
        copy.wait()


def run_forward(remote, radar, optical, vectors, table, slopes, weights):
    n, d = radar.shape
    low, lse, wide = shape((n, d), BF16), shape((6, 2, n), F32), shape((n, d), F32)
    kept = [low] * 11 + [lse, lse, wide, wide, shape((n, n), F32)]
    whole = [shape((8, d, d), BF16)] if remote else []
    return pl.pallas_call(
        functools.partial(forward_body, remote),
        out_shape=whole + kept,
        in_specs=[VMEM] * 3 + [SMEM] + [VMEM] * (len(vectors) + len(weights)),
        out_specs=[HBM] * len(whole + kept),
        scratch_shapes=[
            pltpu.VMEM((8, d), F32), pltpu.VMEM((3, n, 128), F32),
            pltpu.SemaphoreType.DMA((24,)),
        ] + [pltpu.VMEM(a.shape, a.dtype) for a in whole + kept]
        + ([pltpu.SemaphoreType.DMA((8, 5))] * 2 if remote else []),
        compiler_params=pltpu.CompilerParams(
            vmem_limit_bytes=LIMIT, **(dict(collective_id=0, has_side_effects=True) if remote else {})
        ),
        name="forward",
        cost_estimate=pl.CostEstimate(flops=8 * 10**9, bytes_accessed=3 * 10**7, transcendentals=0),
    )(radar, optical, table, slopes, *vectors, *weights)


PATHS = {
    "A": ("XY", "YX", "XY", "XY"),
    "B": ("XY", "YX", "YX", "YX"),
    "C": ("NYX", "NYX", "XYN", "XYN"),
    "S": ("YXN", "YXN", "YXN", "XYN"),
}
AGAIN = {
    "C": ("NY", "NY", "NY", "NY"),
    "S": ("NY", "YN", "NY", "NY"),
}
NEAR_PAIR = 0
FIRST_SLOT = {"A": 0, "B": 4, "C": 8, "S": 0}
FIRST_BACK = {"A": 0, "C": 4, "S": 8, "B": 12}
UNIT = {"A": 0, "B": 1, "C": 0, "S": 1}
AXES = {"X": X_BIT, "Y": Y_BIT, "N": Z_NEAR, "F": Z_FAR}


def core_slot(unit, j):
    return {"A": j % 2, "B": 2 + j % 2}.get(unit, j)


class Sums:
    def __init__(self, refs):
        (self.g, self.rc, self.r1, self.r2, self.r3, self.rf, self.rn, self.zb, self.zn, self.zf,
         self.all,
         self.cs, self.cr, self.s1, self.q1, self.s2, self.q2, self.s3, self.q3, self.sf, self.qf,
         self.sn, self.qn, self.sz, self.qz, self.sa, self.qa,
         self.sm, self.sq, self.ss, self.sr) = refs
        dp, head = lax.axis_index("dp"), lax.axis_index("head")
        self.mc, self.mx, self.my = head % 2, head // 2, dp % 2
        self.z0, self.z1 = dp // 2 % 2, dp // 4
        columns = self.g.shape[-1] // 2
        self.columns = [
            pl.ds(pl.multiple_of(columns * z, columns), columns) for z in (self.z1, 1 - self.z1)
        ]

    def mine(self, unit):
        if unit in "CS":
            return {"C": 0, "X": 0, "Y": self.my, "N": self.z0}
        return {"C": self.mc, "X": self.mx, "Y": self.my}

    def slots(self, unit, j):
        slot = FIRST_SLOT[unit] + j
        if unit == "B" and j // 2 == NEAR_PAIR:
            slot = 4 + 2 * NEAR_PAIR + self.z0
        return slot, FIRST_BACK[unit] + j

    def part(self, unit, j, held, sent=None):
        at = {"X": slice(None), "Y": slice(None), "N": slice(None)}
        mine = self.mine(unit)
        for axis in held:
            at[axis] = mine[axis]
        if sent:
            at[sent] = 1 - mine[sent]
        return self.g.at[self.slots(unit, j)[0], mine["C"], at["X"], at["Y"], at["N"]]

    def put(self, unit, slot, row, value):
        end = row + value.shape[0]
        at = row
        while at < end:
            t, half = at // 96, at // 48 % 2
            stop = min(end, at // 48 * 48 + 48)
            if unit in "AB":
                y, x, c = t // 4, t // 2 % 2, t % 2
            else:
                x, c, y = t // 4, t // 2 % 2, t % 2
            self.g[slot, c, x, y, half, at % 48 : at % 48 + stop - at, :] = value[
                at - row : stop - row
            ].astype(BF16)
            at = stop

    def add(self, part, got):
        for at in np.ndindex(*part.shape[:-2]):
            part[*at] = part[*at] + got[*at]

    def core_copy(self, unit, j):
        slot = FIRST_SLOT[unit] + j
        return send_to(
            CORE, self.g.at[slot, 1 - self.mine(unit)["C"]], self.rc.at[core_slot(unit, j)],
            self.cs.at[slot], self.cr.at[slot],
        )

    def step_copy(self, unit, j, step):
        path = PATHS[unit][j]
        back = FIRST_BACK[unit] + j
        got, send, recv = (
            (self.r1, self.s1, self.q1), (self.r2, self.s2, self.q2), (self.r3, self.s3, self.q3)
        )[step]
        if step == 2:
            back -= 4
        return send_to(
            AXES[path[step]], self.part(unit, j, path[:step], path[step]), got.at[back],
            send.at[back], recv.at[back],
        ), got.at[back]

    def begin(self, unit, j):
        self.core_copy(unit, j).start()

    def event(self, kind, unit, j):
        u = UNIT.get(unit)
        attention = unit in "CS"
        if kind == "1":
            self.core_copy(unit, j).wait()
            mine, got = self.mine(unit), self.rc.at[core_slot(unit, j)]
            chunk = self.g.at[FIRST_SLOT[unit] + j, mine["C"]]
            if unit == "B" and j // 2 == NEAR_PAIR:
                self.add(chunk, got)
                if j % 2:
                    self.near_copy().start()
                return
            axis = PATHS[unit][j][0]
            place = "XYN".index(axis)
            for keep in (1 - mine[axis], mine[axis]):
                at = [slice(None)] * 3
                at[place] = keep
                self.add(chunk.at[*at], got.at[*at])
                if keep is not mine[axis]:
                    self.step_copy(unit, j, 0)[0].start()
        elif kind == "n":
            self.near_copy().wait()
            self.add(self.part("B", 2 * j, ""), self.rn)
            self.step_copy("B", 2 * j, 0)[0].start()
        elif kind in "23" or (kind == "5" and attention):
            step = {"2": 0, "3": 1, "5": 2}[kind]
            path = PATHS[unit][j]
            copy, got = self.step_copy(unit, j, step)
            copy.wait()
            part = self.part(unit, j, path[: step + 1])
            if step == 1 and not attention:
                early = unit == "B" and j // 2 == NEAR_PAIR
                z = 2 * (self.z0 if early else j % 2) + j // 2
                for half in range(2):
                    self.zb[u, z, half] = part[half] + got[half]
                return
            if step == 2:
                part[...] = part[...] + got[...]
                self.far_quarter(unit, j).start()
            else:
                self.add(part, got)
                self.step_copy(unit, j, step + 1)[0].start()
        elif kind == "4":
            self.z_copy(unit).start()
        elif kind == "5":
            self.z_copy(unit).wait()
            at = self.near_shards(unit)
            self.add(self.zb.at[u, pl.ds(2 * self.z0 + at.start, at.size)], self.zn.at[u, at])
            self.far_copy(u).start()
        elif kind == "6":
            if attention:
                self.far_quarter(unit, j).wait()
                columns = self.columns[0]
                own = self.part(unit, j, "XYN")[:, columns]
                total = own.astype(F32) + self.rf[u, j].astype(F32)
                self.all[u, j, self.my, self.z0, :, columns] = total.astype(BF16)
                self.gather_copy(unit, j, 0).start()
                return
            self.far_copy(u).wait()
            mine = 2 * self.z0 + self.z1
            self.out[unit][...] = self.zb[u, mine].astype(F32) + self.zf[u].astype(F32)
        elif kind in "789":
            step = int(kind) - 7
            self.gather_copy(unit, j, step).wait()
            if step < 2:
                self.gather_copy(unit, j, step + 1).start()
        elif kind == "m":
            self.small_copy(j).wait()
            self.sm[j + 1] = self.sm[j] + self.sq[j]
            if j < 4:
                self.small_copy(j + 1).start()

    def small_copy(self, step):
        bit = (CORE, X_BIT, Y_BIT, Z_NEAR, Z_FAR)[step]
        return send_to(bit, self.sm.at[step], self.sq.at[step], self.ss.at[step], self.sr.at[step])

    def far_quarter(self, unit, j):
        at = FIRST_BACK[unit] - 4 + j
        return send_to(
            Z_FAR, self.part(unit, j, "XYN").at[:, self.columns[1]], self.rf.at[UNIT[unit], j],
            self.sf.at[at], self.qf.at[at],
        )

    def near_shards(self, unit):
        return pl.ds(1 - NEAR_PAIR, 1) if unit == "B" else pl.ds(0, 2)

    def z_copy(self, unit):
        u, at = UNIT[unit], self.near_shards(unit)
        return send_to(
            Z_NEAR, self.zb.at[u, pl.ds(2 * (1 - self.z0) + at.start, at.size)], self.zn.at[u, at],
            self.sn.at[u], self.qn.at[u],
        )

    def near_copy(self):
        return send_to(
            Z_NEAR, self.g.at[4 + 2 * NEAR_PAIR + 1 - self.z0, self.mc], self.rn,
            self.sn.at[2], self.qn.at[2],
        )

    def far_copy(self, u):
        return send_to(
            Z_FAR, self.zb.at[u, 2 * self.z0 + 1 - self.z1], self.zf.at[u], self.sz.at[u], self.qz.at[u]
        )

    def gather_copy(self, unit, j, step):
        whole = self.all.at[UNIT[unit], j]
        axis = ("F" + AGAIN[unit][j])[step]
        if step == 0:
            held = whole.at[self.my, self.z0, :, self.columns[0]]
        elif step == 1:
            held = whole.at[self.my, self.z0]
        else:
            held = whole.at[self.my] if axis == "Y" else whole.at[:, self.z0]
        at = FIRST_BACK[unit] - 4 + j
        return send_to(AXES[axis], held, held, self.sa.at[step, at], self.qa.at[step, at])


TICKS = {
    "f1a": "1A0",
    "f1b": "1B0",
    "f1o": "1A1",
    "f2g": "1B1",
    "f2o": "1A2",
    "f3a": "1B2",
    "g": "1B3",
    "c0n": "1A3",
    "ch0": "2A1",
    "ch1": "1C0",
    "ch2": "2A2",
    "ch4": "nB0",
    "ch5": "2A0",
    "c2n": "2A3",
    "c4": "1C1 2B3",
    "c5": "2B0",
    "s0n": "2B2 3A1 3A0 3A2",
    "s0": "3A3 4A0 1S0",
    "sh0": "1C2",
    "sh1": "3B3",
    "sh2": "3B0 1C3 3B2 4B0",
    "sh3": "2C1",
    "sh4": "5A0 2C0",
    "sh5": "2C2",
    "s2": "5B0",
    "s2n": "3C1 1S1 2S0 3C0",
    "s3": "5C1 3C2",
    "s4": (
        "2C3 1S2 3S0 1S3",
        "5C0 2S1 6C1 5S0",
        "6C0 6A0 3C3 5C2",
    ),
    "s5": (
        "2S3 7C1 3S1 6B0",
        "2S2 6S0",
    ),
    "tail": (
        "5C3 mM0 7C0 6C2",
        "5S1 3S3 8C1 7C2",
        "3S2 5S3 8C0 6S1",
        "5S2 6C3 7S0 8C2",
        "6S3 mM1 7C3 7S1",
        "9C0 6S2 8S0 7S3",
        "mM2 8C3 9C1 7S2",
        "8S1 8S3 9C2 9S0",
        "mM3 9C3 8S2 9S2",
        "9S1 9S3 mM4",
    ),
}


def ticks(hub, name):
    words = TICKS.get(name, ())
    for word in " ".join((words,) if isinstance(words, str) else words).split():
        hub.event(word[0], word[1], int(word[2]))


def loop_ticks(hub, name, index, names):
    for k, at in enumerate(names):
        if at in TICKS:
            @pl.when(index == k)
            def _():
                ticks(hub, at)


def attention_unit(hub, unit, grad, low, mixed, q, k, v, lse, reach, slope, x, y, w, up, dq, dk, dv):
    tag = unit.lower()

    def cast(rows):
        low[rows, :] = grad[rows, :].astype(BF16)

    def chunk(j, grads, side):
        ticks(hub, f"{tag}{j}n")
        for n in range(grads.shape[1] // 256):
            hub.put(unit, FIRST_SLOT[unit] + j, 256 * n,
                    tn(grads[:, 256 * n : 256 * n + 256], side[...]))
        hub.begin(unit, j)
        ticks(hub, f"{tag}{j + 1 if j else 0}")

    rows_loop(grad.shape[0], 128, cast)
    chunk(0, mixed, low)
    project(low, w.at[3], up)
    ticks(hub, f"{tag}1")
    attend_back(q, k, v, up, mixed, lse, reach, slope, dq, dk, dv,
                lambda hp: loop_ticks(hub, tag, hp, [f"{tag}h{i}" for i in range(6)]))
    chunk(1, dq, x)
    chunk(2, dk, y)
    chunk(3, dv, y)


class Loads:
    def __init__(self, sems):
        self.sems, self.next = sems, 0

    def start(self, src, dst):
        copy = pltpu.make_async_copy(src, dst, self.sems.at[self.next])
        self.next += 1
        copy.start()
        return copy


def backward_body(*refs):
    (h_two, h_cot, h_in, h_out, h_w, h_cq, h_ck, h_cv, h_cm, h_rlow, h_olow,
     h_sq, h_sk, h_sv, h_sm, h_normed, h_one, h_opt, h_radar, h_reach,
     c_lse, s_lse), refs = refs[:22], refs[22:]
    parts, slopes, refs = refs[:7], refs[7], refs[8:]
    (o_merged, o_radar, o_opt, o_fin, o_fout, o_all, o_small), refs = refs[:7], refs[7:]
    vectors, refs = refs[0], refs[1:]
    sums, refs = refs[:10], refs[10:]
    (wa, wb, q, k, v, mixed, x, y, two, two_grad, out, pull, one,
     cot, low, up, dq, dk, dv, reach, sm, sq), sems = refs[:22], refs[22:]
    hub = Sums(sums + (o_all,) + tuple(sems[:16]) + (sm, sq) + tuple(sems[16:18]))
    hub.out = {"A": o_fin, "B": o_fout}
    load = Loads(sems[18])
    tile_sems = sems[19]
    slope = slope_of(slopes, lax.axis_index("head"))
    gain_s, gain_r, gain_o, gain_f, shift_f, b_out = (
        vectors.at[i : i + 1, :] for i in range(6)
    )
    n = two.shape[0]
    width = wb.shape[1]
    steps = h_in.shape[1] // width

    def tile(i):
        at = pl.ds(pl.multiple_of(i * width, width), width)
        slot = i % 2
        return (
            pltpu.make_async_copy(h_in.at[:, at], wb.at[2 * slot], tile_sems.at[slot, 0]),
            pltpu.make_async_copy(h_out.at[at, :], wb.at[2 * slot + 1], tile_sems.at[slot, 1]),
        )

    greeting((CORE, X_BIT, Y_BIT, Z_NEAR, Z_FAR))
    first = [load.start(h_two, two), load.start(h_cot, cot)]
    for copy in tile(0):
        copy.start()
    later = [load.start(a, b) for a, b in (
        (h_cm, mixed), (h_w.at[pl.ds(4, 4)], wa), (h_cq, q), (h_ck, k), (h_cv, v),
        (h_rlow, x), (h_olow, y), (h_one, one), (h_reach, reach))]
    load_vectors(parts, vectors)
    sm[0] = jnp.zeros_like(sm[0])
    out[...] = jnp.zeros_like(out)
    pull[...] = jnp.zeros_like(pull)
    first[0].wait()
    norm_rows(two, gain_f, shift_f, low)
    first[1].wait()

    def feed(i, _):
        for copy in tile(i):
            copy.wait()

        @pl.when(i < steps - 1)
        def _():
            for copy in tile(i + 1):
                copy.start()

        w_in, w_out = wb.at[2 * (i % 2)], wb.at[2 * (i % 2) + 1]
        hidden, grad = up, dq
        blocks = [slice(m, m + 256) for m in range(0, width, 256)]

        def feed_ticks(name):
            loop_ticks(hub, "f", i, [f"f{s}{name}" for s in range(4)])

        for n, at in enumerate(blocks):
            if n:
                feed_ticks("ab"[n - 1])
            h = nn(low[...], w_in[:, at]) + vectors[pl.ds(6 + i, 1), at]
            square = h * h
            half = 0.5 + 0.5 * jnp.tanh(h * (ROOT + ROOT * CUBE * square))
            hidden[:, at] = (h * half).astype(BF16)
            rise = half * (
                1.0 + h * (1.0 - half) * (2 * ROOT + 6 * ROOT * CUBE * square)
            )
            part = (nt(cot[...], w_out[at, :]) * rise).astype(BF16)
            grad[:, at] = part
            sm[0, pl.ds(24 + i, 1), at] = jnp.sum(part.astype(F32), axis=0, keepdims=True)
        feed_ticks("c")
        for n, at in enumerate(blocks):
            hub.put("A", i, at.start, tn(grad[:, at], low[...]))
            if n == 2:
                hub.begin("A", i)
            feed_ticks("de"[n] if n < 2 else "f")
        for n, at in enumerate(blocks):
            hub.put("B", 4 + i, at.start, tn(hidden[:, at], cot[...]))
            if n == 2:
                hub.begin("B", i)
            feed_ticks("ghi"[n])
        for n, at in enumerate(blocks):
            out[:, at] += nn(hidden[...], w_out[:, at])
            feed_ticks("jkl"[n])
            pull[:, at] += nt(grad[...], w_in[at, :])
            feed_ticks("mno"[n])
        return 0

    pl.semaphore_wait(pltpu.get_barrier_semaphore(), 5)
    lax.fori_loop(0, steps, feed, 0)
    self_w = load.start(h_w.at[pl.ds(0, 4)], wb)

    def close(rows):
        value, cotangent = two[rows, :], cot[rows, :].astype(F32)
        dv[rows, :] = (value + out[rows, :] + b_out[...]).astype(BF16)
        dval, dgain, dshift = norm_back_rows(value, gain_f[...], pull[rows, :])
        total = cotangent + dval
        two_grad[rows, :] = total
        sm[0, 0:1, :] += dgain
        sm[0, 1:2, :] += dshift
        sm[0, 2:3, :] += jnp.sum(cotangent, axis=0, keepdims=True)
        sm[0, 3:4, :] += jnp.sum(total, axis=0, keepdims=True)

    rows_loop(n, 128, close)
    stores = [load.start(dv, o_merged)]
    opt_load = load.start(h_opt, cot)
    ticks(hub, "g")
    for copy in later:
        copy.wait()
    stores[0].wait()
    attention_unit(hub, "C", two_grad, low, mixed, q, k, v, c_lse, reach, slope, x, y, wa,
                   up, dq, dk, dv)
    later = [load.start(a, b) for a, b in (
        (h_sm, mixed), (h_sq, q), (h_sk, k), (h_sv, v), (h_normed, x), (h_radar, y))]
    opt_load.wait()

    def cross(rows):
        dval, dgain, dshift = norm_back_rows(one[rows, :], gain_r[...], nn(dq[rows, :], wa[0]))
        total = two_grad[rows, :] + dval
        out[rows, :] = total
        sm[0, 8:9, :] += dgain
        sm[0, 9:10, :] += dshift
        sm[0, 12:13, :] += jnp.sum(total, axis=0, keepdims=True)
        dval, dgain, dshift = norm_back_rows(
            cot[rows, :].astype(F32), gain_o[...], nn(dk[rows, :], wa[1]) + nn(dv[rows, :], wa[2])
        )
        pull[rows, :] = dval
        sm[0, 10:11, :] += dgain
        sm[0, 11:12, :] += dshift

    rows_loop(n, 256, cross)
    stores = [load.start(pull, o_opt)]
    ticks(hub, "c5")
    for copy in later:
        copy.wait()
    self_w.wait()
    attention_unit(hub, "S", out, low, mixed, q, k, v, s_lse, reach, slope, x, x, wb,
                   up, dq, dk, dv)

    def own(rows):
        dval, dgain, dshift = norm_back_rows(
            y[rows, :].astype(F32), gain_s[...],
            nn(dq[rows, :], wb[0]) + nn(dk[rows, :], wb[1]) + nn(dv[rows, :], wb[2]),
        )
        two[rows, :] = out[rows, :] + dval
        sm[0, 16:17, :] += dgain
        sm[0, 17:18, :] += dshift

    rows_loop(n, 256, own)
    stores.append(load.start(two, o_radar))
    hub.small_copy(0).start()
    ticks(hub, "s5")
    ticks(hub, "tail")
    o_small[...] = sm[5]
    for copy in stores:
        copy.wait()


def run_backward(two, cot, feed_in, feed_out, w, cross, own, one, optical, radar, reach,
                 c_lse, s_lse, vectors, slopes):
    n, d = two.shape
    low, wide = pltpu.VMEM((n, d), BF16), pltpu.VMEM((n, d), F32)
    chunk = lambda *dims: pltpu.VMEM(dims + (48, d), BF16)
    sems = lambda *dims: pltpu.SemaphoreType.DMA(dims)
    return pl.pallas_call(
        backward_body,
        out_shape=[
            shape((n, d), BF16), shape((n, d), F32), shape((n, d), F32),
            shape((2, 48, d), F32), shape((2, 48, d), F32), shape((2, 4, 2, 2, 48, d), BF16),
            shape((32, d), F32),
        ],
        in_specs=[HBM] * 20 + [VMEM] * (2 + len(vectors)) + [SMEM],
        out_specs=[HBM] * 3 + [VMEM] * 4,
        scratch_shapes=[
            pltpu.VMEM((16, d), F32),
            chunk(12, 2, 2, 2, 2), chunk(4, 2, 2, 2), chunk(16, 2, 2), chunk(16, 2), chunk(8),
            pltpu.VMEM((2, 4, 48, d // 2), BF16), chunk(2, 2, 2),
            chunk(2, 4, 2), chunk(2, 2, 2), chunk(2, 2),
            pltpu.VMEM((4, d, d), BF16), pltpu.VMEM((4, d, d), BF16),
            low, low, low, low, low, low, wide, wide, wide, wide, wide,
            low, low, low, low, low, low, pltpu.VMEM((n, n), F32),
            pltpu.VMEM((6, 32, d), F32), pltpu.VMEM((5, 32, d), F32),
            sems(12), sems(12), sems(16), sems(16), sems(16), sems(16), sems(8), sems(8),
            sems(8), sems(8), sems(3), sems(3), sems(2), sems(2),
            sems(3, 8), sems(3, 8), sems(5), sems(5),
            sems(24), sems(2, 2),
        ],
        compiler_params=pltpu.CompilerParams(
            vmem_limit_bytes=LIMIT, collective_id=1, has_side_effects=True
        ),
        name="backward",
        cost_estimate=pl.CostEstimate(flops=35 * 10**9, bytes_accessed=5 * 10**7, transcendentals=0),
    )(two, cot, feed_in, feed_out, w, *cross, *own, one, optical, radar, reach,
      c_lse, s_lse, *vectors, slopes)


def call(body, outs, scratch, operands, in_specs, **more):
    return pl.pallas_call(
        body,
        out_shape=outs,
        in_specs=in_specs,
        out_specs=[VMEM] * len(outs),
        scratch_shapes=scratch,
        compiler_params=pltpu.CompilerParams(vmem_limit_bytes=LIMIT),
        **more,
    )(*operands)


def run_feed(place, two, cot, gain, shift, w_in, b_in, w_out, b_out):
    n, d = two.shape
    f = w_in.shape[1]
    tile = 768
    whole = lambda *dims: pl.BlockSpec(dims, lambda i, p: (0,) * len(dims))
    slots = pl.BlockSpec((2, 2, 1, 96, d), lambda i, p: (0, 0, i ^ p[0], 0, 0))
    grad = shape((2, 2, 4, 96, d), BF16)
    return pl.pallas_call(
        feed_step,
        grid_spec=pltpu.PrefetchScalarGridSpec(
            num_scalar_prefetch=1,
            grid=(f // tile,),
            in_specs=[
                whole(n, d), whole(n, d), whole(1, d), whole(1, d),
                pl.BlockSpec((d, tile), lambda i, p: (0, i)),
                pl.BlockSpec((1, tile), lambda i, p: (0, i)),
                pl.BlockSpec((tile, d), lambda i, p: (i, 0)),
                whole(1, d),
            ],
            out_specs=[
                whole(n, d), whole(n, d), slots, slots, slots, slots,
                pl.BlockSpec((1, 1, tile), lambda i, p: (i, 0, 0)),
                whole(8, d),
            ],
            scratch_shapes=[
                pltpu.VMEM((n, d), BF16), pltpu.VMEM((n, d), F32), pltpu.VMEM((n, d), F32),
                pltpu.VMEM((tile, d), BF16), pltpu.VMEM((tile, d), BF16),
            ],
        ),
        out_shape=[
            shape((n, d), BF16), shape((n, d), F32), grad, grad, grad, grad,
            shape((f // tile, 1, tile), F32), shape((8, d), F32),
        ],
        compiler_params=pltpu.CompilerParams(vmem_limit_bytes=LIMIT),
        name="feed",
        cost_estimate=pl.CostEstimate(flops=15 * 10**9, bytes_accessed=25 * 10**6, transcendentals=0),
    )(place, two, cot, gain, shift, w_in, b_in, w_out, b_out)


def back_scratch(n, d):
    low = pltpu.VMEM((n, d), BF16)
    return [low, pltpu.VMEM((d, d), BF16), low, low, low, low]


def run_cross_backward(place, two_grad, mixed, q, k, v, lse, reach, slope, radar_low, optical_low,
                       w, one, optical, gain_r, gain_o):
    n, d = one.shape
    grad = shape((2, 2, 4, 96, d), BF16)
    wide = shape((n, d), F32)
    return call(
        cross_backward,
        [wide, wide, grad, grad, shape((8, d), F32)],
        back_scratch(n, d),
        (place, two_grad, mixed, q, k, v, lse, reach, slope, radar_low, optical_low,
         w, one, optical, gain_r, gain_o),
        [SMEM] + [VMEM] * 7 + [SMEM] + [VMEM] * 7,
        name="cross_backward",
        cost_estimate=pl.CostEstimate(flops=12 * 10**9, bytes_accessed=25 * 10**6, transcendentals=0),
    )


def run_self_backward(place, one_grad, mixed, q, k, v, lse, reach, slope, normed, w, radar, gain):
    n, d = one_grad.shape
    grad = shape((2, 2, 4, 96, d), BF16)
    return call(
        self_backward,
        [shape((n, d), F32), grad, grad, shape((8, d), F32)],
        back_scratch(n, d),
        (place, one_grad, mixed, q, k, v, lse, reach, slope, normed, w, radar, gain),
        [SMEM] + [VMEM] * 7 + [SMEM] + [VMEM] * 4,
        name="self_backward",
        cost_estimate=pl.CostEstimate(flops=12 * 10**9, bytes_accessed=25 * 10**6, transcendentals=0),
    )


def finish(bias_part, got, small, merged, radar, optical, fin, fout, *refs):
    outs, sems = refs[:-1], refs[-1]
    moves = [
        pltpu.make_async_copy(src, dst, sems.at[i])
        for i, (src, dst) in enumerate(zip((merged, radar, optical, fin, fout), outs))
    ]
    for copy in moves:
        copy.start()
    mats, vectors, bias = outs[5:13], outs[13:24], outs[24]
    for u in range(2):
        for j, mat in enumerate((3, 0, 1, 2)):
            for half in range(2):
                for part in range(2):
                    at = 96 * half + 48 * part
                    mats[4 * u + mat][at : at + 48, :] = got[u, j, half, part].astype(F32)
    for row, dst in zip((16, 17, 12, 8, 9, 10, 11, 3, 0, 1, 2), vectors):
        dst[...] = small[row : row + 1, :].reshape(dst.shape)
    mine, per = bias_part[0], small.shape[1] // bias.shape[0]
    line = small[pl.ds(24 + mine // per, 1), :]
    shift = (small.shape[1] - mine % per * bias.shape[0]) % small.shape[1]
    bias[...] = pltpu.roll(line, shift, 1)[:, : bias.shape[0]].reshape(bias.shape)
    for copy in moves:
        copy.wait()


def run_finish(mine, got, small, merged, radar, optical, fin, fout):
    d = got.shape[-1]
    moved = (merged, radar, optical, fin, fout)
    outs = pl.pallas_call(
        finish,
        out_shape=[shape(a.shape, a.dtype) for a in moved]
        + [shape((192, d), F32)] * 8 + [shape((d,), F32)] * 11 + [shape((96,), F32)],
        in_specs=[SMEM] + [VMEM] * 7,
        out_specs=[HBM] * 5 + [VMEM] * 20,
        scratch_shapes=[pltpu.SemaphoreType.DMA((5,))],
        compiler_params=pltpu.CompilerParams(vmem_limit_bytes=LIMIT),
        name="finish",
    )(mine.reshape(1), got, small, *moved)
    mats = [o if i % 4 == 3 else o.T for i, o in enumerate(outs[5:13])]
    outs = list(outs)
    outs[3:5] = [o.reshape(-1, d) for o in outs[3:5]]
    return outs[:5], mats[:4], mats[4:], outs[13:24], outs[24]


def shards(
    radar, optical, patch_table, cotangent, norm_self_gain, norm_self_shift,
    self_query, self_key, self_value, self_out, self_out_bias, norm_radar_gain, norm_radar_shift,
    norm_optical_gain, norm_optical_shift, cross_query, cross_key, cross_value, cross_out,
    cross_out_bias, norm_feed_gain, norm_feed_shift, feed_in, feed_in_bias, feed_out, feed_out_bias,
):
    dp, head = lax.axis_size("dp"), lax.axis_size("head")
    near = (dp, head) == (8, 4)
    row = lambda v: v.reshape(1, -1)
    zero = jnp.int32(0)
    slopes = jnp.asarray(-np.exp2(-8.0 * np.arange(1, HEADS + 1) / HEADS), F32)
    mine = (lax.axis_index("dp") * head + lax.axis_index("head")).astype(jnp.int32)
    place = jnp.stack([zero] * 4)
    weights = (self_query, self_key, self_value, self_out,
               cross_query, cross_key, cross_value, cross_out)
    weights = tuple(w if i % 4 == 3 else w.T for i, w in enumerate(weights))
    if not near:
        w = lax.all_gather(jnp.stack(weights), "head", axis=1, tiled=True)
        weights = (w,)
    vectors = (norm_self_gain, norm_self_shift, norm_radar_gain, norm_radar_shift,
               norm_optical_gain, norm_optical_shift, self_out_bias, cross_out_bias)
    got = run_forward(near, radar, optical, vectors, patch_table, slopes, weights)
    if near:
        w, got = got[0], got[1:]
    (normed, radar_low, optical_low, sq, sk, sv, cq, ck, cv, s_mixed, c_mixed, s_lse, c_lse,
     two, one, reach) = got
    d = radar.shape[1]
    if near:
        merged, radar_grad, optical_grad, feed_in_grad, feed_out_grad, got, small = run_backward(
            two, cotangent, feed_in, feed_out, w,
            (cq, ck, cv, c_mixed, radar_low, optical_low), (sq, sk, sv, s_mixed, normed),
            one, optical, radar, reach,
            c_lse, s_lse,
            (norm_self_gain, norm_radar_gain, norm_optical_gain, norm_feed_gain, norm_feed_shift,
             feed_out_bias, feed_in_bias),
            slopes,
        )
        ((merged, radar_grad, optical_grad, feed_in_grad, feed_out_grad), cross, own, vectors,
         feed_in_bias_grad) = run_finish(
            mine, got, small, merged, radar_grad, optical_grad, feed_in_grad, feed_out_grad)
    else:
        merged, two_grad, in_keep, in_send, out_keep, out_send, bias_in, feed_small = run_feed(
            place, two, cotangent, row(norm_feed_gain), row(norm_feed_shift),
            feed_in, row(feed_in_bias), feed_out, row(feed_out_bias),
        )
        one_grad, optical_grad, cross_keep, cross_send, cross_small = run_cross_backward(
            place, two_grad, c_mixed, cq, ck, cv, c_lse, reach, slopes, radar_low, optical_low,
            w[4:], one, optical, row(norm_radar_gain), row(norm_optical_gain),
        )
        radar_grad, self_keep, self_send, self_small = run_self_backward(
            place, one_grad, s_mixed, sq, sk, sv, s_lse, reach, slopes, normed,
            w[:4], radar, row(norm_self_gain),
        )
        small = jnp.concatenate([feed_small, cross_small, self_small, bias_in.reshape(-1, d)])
        def logical(keep, send, order):
            both = jnp.stack([keep, send])
            return jnp.transpose(both, order).reshape(-1, d)

        def feed_sum(keep, send):
            return lax.psum_scatter(
                logical(keep, send, (3, 2, 1, 0, 4, 5)).astype(F32),
                ("dp", "head"), scatter_dimension=0, tiled=True,
            )

        def attn_sum(keep, send):
            total = logical(keep, send, (3, 1, 0, 2, 4, 5)).astype(F32).reshape(4, -1, d)
            total = lax.psum_scatter(total, "head", scatter_dimension=1, tiled=True)
            total = lax.psum(total, "dp")
            return total[0].T, total[1].T, total[2].T, total[3]

        feed_in_grad, feed_out_grad = feed_sum(in_keep, in_send), feed_sum(out_keep, out_send)
        cross, own = attn_sum(cross_keep, cross_send), attn_sum(self_keep, self_send)
        small = lax.psum(small, ("dp", "head"))
        vectors = [small[i] for i in (16, 17, 12, 8, 9, 10, 11, 3, 0, 1, 2)]
        bias_part = feed_in_bias.shape[0] // (dp * head)
        feed_in_bias_grad = lax.dynamic_slice_in_dim(
            small[24:28].reshape(-1), mine * bias_part, bias_part
        )
    return (
        merged, radar_grad, optical_grad, vectors[0], vectors[1], *own, *vectors[2:7],
        *cross, *vectors[7:10], feed_in_grad.T, feed_in_bias_grad, feed_out_grad, vectors[10],
    )


def solution(mesh):
    token, rep = P(("dp", "head"), None), P()
    col, row = P(None, "head"), P("head", None)
    in_specs = (
        token, token, P(None, ("dp", "head")), token,
        rep, rep, col, col, col, row, rep,
        rep, rep, rep, rep, col, col, col, row, rep,
        rep, rep, rep, rep, rep, rep,
    )
    out_specs = (
        token, token, token,
        rep, rep, col, col, col, row, rep,
        rep, rep, rep, rep, col, col, col, row, rep,
        rep, rep, P(None, ("dp", "head")), P(("dp", "head")), token, rep,
    )
    return jax.shard_map(shards, mesh=mesh, in_specs=in_specs, out_specs=out_specs, check_vma=False)
```

```python
import functools

import jax
import jax.numpy as jnp
import numpy as np
from jax import lax
from jax.experimental import pallas as pl
from jax.experimental.pallas import tpu as pltpu
from jax.sharding import PartitionSpec as P

F32, BF16 = jnp.float32, jnp.bfloat16
HEADS, HEAD_DIM = 12, 64
EPSILON = 1e-06
FAR = 1e12
LIMIT = 62 * 2**20
VMEM = pl.BlockSpec(memory_space=pltpu.VMEM)
SMEM = pl.BlockSpec(memory_space=pltpu.SMEM)
HBM = pl.BlockSpec(memory_space=pl.ANY)


def nn(a, b):
    return lax.dot_general(a, b, (((1,), (0,)), ((), ())), preferred_element_type=F32)


def nt(a, b):
    return lax.dot_general(a, b, (((1,), (1,)), ((), ())), preferred_element_type=F32)


def tn(a, b):
    return lax.dot_general(a, b, (((0,), (0,)), ((), ())), preferred_element_type=F32)


def rows_loop(total, block, body):
    def step(i, _):
        body(pl.ds(pl.multiple_of(i * block, block), block))
        return 0

    lax.fori_loop(0, total // block, step, 0)


def centred(v):
    c = v - jnp.mean(v, axis=-1, keepdims=True)
    return c, lax.rsqrt(jnp.mean(c * c, axis=-1, keepdims=True) + EPSILON)


def norm_rows(src, gain, shift, dst):
    def body(rows):
        c, r = centred(src[rows, :].astype(F32))
        dst[rows, :] = (c * r * gain[...] + shift[...]).astype(BF16)

    rows_loop(src.shape[0], 128, body)


def norm_back_rows(v, gain, u):
    c, r = centred(v)
    hat = c * r
    w = u * gain
    dv = r * (
        w
        - jnp.mean(w, axis=-1, keepdims=True)
        - hat * jnp.mean(w * hat, axis=-1, keepdims=True)
    )
    return dv, jnp.sum(u * hat, axis=0, keepdims=True), jnp.sum(u, axis=0, keepdims=True)


def project(x, w, dst, scale=None, half=None):
    total = w.shape[0]
    if half is None:
        blocks = [(i, 256) for i in range(0, total, 256)]
    else:
        blocks = [(half * total // 2, 256), (half * total // 2 + 256, total // 2 - 256)]
    for at, size in blocks:
        cols = slice(at, at + size)
        y = nt(x[...], w[cols, :])
        dst[:, cols] = (y if scale is None else y * scale).astype(BF16)


def fill_reach(table, columns, reach):
    for i in range(3):
        line = table[i : i + 1, :].astype(F32)
        columns[i] = jnp.broadcast_to(line, (128, line.shape[1])).T

    def body(rows):
        seg, down, across = (
            columns[i, rows, 0:1] - table[i : i + 1, :].astype(F32) for i in range(3)
        )
        reach[rows, :] = jnp.where(seg == 0, jnp.sqrt(down * down + across * across), FAR)

    rows_loop(reach.shape[0], 64, body)


def slope_of(table, group):
    return lambda h: table[3 * (h // 3 ^ group) + h % 3]


def low_half(length):
    return lax.broadcasted_iota(jnp.int32, (length, 128), 1) < HEAD_DIM


def attend(q, k, v, reach, slope, mixed, lse, tick, pairs):
    lo = low_half(q.shape[0])

    def pair(hp, _):
        tick(hp)
        at = pl.ds(pl.multiple_of(hp * 128, 128), 128)
        qs, ks, vs = q[:, at], k[:, at], v[:, at]
        outs, tops = [], []
        for sub in range(2):
            mine = lo if sub == 0 else jnp.logical_not(lo)
            s = nt(jnp.where(mine, qs, jnp.zeros_like(qs)), ks)
            s = s + slope(2 * hp + sub) * reach[...]
            top = jnp.max(s, axis=-1, keepdims=True)
            e = jnp.exp(s - top).astype(BF16)
            outs.append(nn(e, jnp.where(mine, vs, jnp.ones_like(vs))))
            tops.append(top)
        num = jnp.where(lo, outs[0], outs[1])
        den = pltpu.roll(jnp.where(lo, outs[1], outs[0]), HEAD_DIM, 1)
        mixed[:, at] = (num / den).astype(BF16)
        lse_t = (jnp.where(lo, tops[0], tops[1]) + jnp.log(den)).T
        lse[hp] = jnp.concatenate([lse_t[0:1], lse_t[HEAD_DIM : HEAD_DIM + 1]], axis=0)
        return 0

    lax.fori_loop(*pairs, pair, 0)


def attend_back(q, k, v, up, mixed, lse, reach, slope, dq, dk, dv, tick=lambda hp: None):
    lo = low_half(q.shape[0])

    def pair(hp, _):
        tick(hp)
        at = pl.ds(pl.multiple_of(hp * 128, 128), 128)
        qs, ks, vs, ups = q[:, at], k[:, at], v[:, at], up[:, at]
        prod = (ups.astype(F32) * mixed[:, at].astype(F32)).T
        tops = lse[hp]
        dqs, dks, dvs = [], [], []
        for sub in range(2):
            mine = lo if sub == 0 else jnp.logical_not(lo)
            delta = jnp.sum(prod[sub * HEAD_DIM : (sub + 1) * HEAD_DIM], axis=0, keepdims=True)
            s = nt(jnp.where(mine, ks, jnp.zeros_like(ks)), qs)
            p = jnp.exp(s + slope(2 * hp + sub) * reach[...] - tops[sub : sub + 1])
            dp = nt(jnp.where(mine, vs, jnp.zeros_like(vs)), ups)
            ds = (p * (dp - delta)).astype(BF16)
            dvs.append(nn(p.astype(BF16), ups))
            dks.append(nn(ds, qs))
            dqs.append(tn(ds, ks))
        dq[:, at] = (jnp.where(lo, dqs[0], dqs[1]) * HEAD_DIM**-0.5).astype(BF16)
        dk[:, at] = jnp.where(lo, dks[0], dks[1]).astype(BF16)
        dv[:, at] = jnp.where(lo, dvs[0], dvs[1]).astype(BF16)
        return 0

    lax.fori_loop(0, q.shape[1] // 128, pair, 0)


def add_out(base, mixed, w_out, bias, dst):
    def body(cols):
        y = nn(mixed[...], w_out[:, cols])
        dst[:, cols] = base[:, cols].astype(F32) + y + bias[:, cols]

    rows_loop(w_out.shape[1], 256, body)


def place_shards(full, place, at, keep, send):
    my, mx, mc = place[1], place[2], place[3]
    for x in range(2):
        for y in range(2):
            for c, dst in enumerate((keep, send)):
                row = (((y ^ my) * 2 + (x ^ mx)) * 2 + (c ^ mc)) * 96
                dst[x, y, at] = full[pl.ds(pl.multiple_of(row, 96), 96), :]


def feed_step(place, two, cot, gain, shift, w_in, b_in, w_out, b_out,
              merged, two_grad, keep_in, send_in, keep_out, send_out, bias_in, small,
              low, out, pull, full_in, full_out):
    step = pl.program_id(0)
    width = w_out.shape[0]
    block = 256

    @pl.when(step == 0)
    def _():
        norm_rows(two, gain, shift, low)

    for n in range(width // block):
        at = slice(n * block, (n + 1) * block)
        x = nn(low[...], w_in[:, at]) + b_in[:, at]
        inner = 0.7978845608028654 * x * (1.0 + 0.044715 * x * x)
        t = jnp.tanh(inner)
        half = 0.5 * (1.0 + t)
        hidden = (x * half).astype(BF16)
        slope = half + 0.5 * x * (1.0 - t * t) * (
            0.7978845608028654 * (1.0 + 3 * 0.044715 * x * x)
        )
        grad = (nt(cot[...], w_out[at, :]) * slope).astype(BF16)
        bias_in[0, :, at] = jnp.sum(grad.astype(F32), axis=0, keepdims=True)
        part_out = nn(hidden, w_out[at, :])
        part_pull = nt(grad, w_in[:, at])
        if n == 0:
            @pl.when(step == 0)
            def _():
                out[...] = part_out
                pull[...] = part_pull

            @pl.when(step > 0)
            def _():
                out[...] += part_out
                pull[...] += part_pull
        else:
            out[...] += part_out
            pull[...] += part_pull
        full_out[at, :] = tn(hidden, cot[...]).astype(BF16)
        full_in[at, :] = tn(grad, low[...]).astype(BF16)
    place_shards(full_in, place, 0, keep_in.at[:, :], send_in.at[:, :])
    place_shards(full_out, place, 0, keep_out.at[:, :], send_out.at[:, :])

    @pl.when(step == pl.num_programs(0) - 1)
    def _():
        small[...] = jnp.zeros_like(small)

        def body(rows):
            value, cotangent = two[rows, :], cot[rows, :].astype(F32)
            merged[rows, :] = (value + out[rows, :] + b_out[...]).astype(BF16)
            dv, dgain, dshift = norm_back_rows(value, gain[...], pull[rows, :])
            total = cotangent + dv
            two_grad[rows, :] = total
            small[0:1, :] += dgain
            small[1:2, :] += dshift
            small[2:3, :] += jnp.sum(cotangent, axis=0, keepdims=True)
            small[3:4, :] += jnp.sum(total, axis=0, keepdims=True)

        rows_loop(two.shape[0], 128, body)


def weight_grad(grads, rows, full):
    def body(cols):
        full[cols, :] = tn(grads[:, cols], rows[...]).astype(BF16)

    rows_loop(grads.shape[1], 256, body)


def attn_shards(full, place, mat, keep, send):
    my, mz = place[1], place[0]
    for x in range(2):
        for y in range(2):
            for c, dst in enumerate((keep, send)):
                row = ((x * 2 + c) * 2 + (y ^ my)) * 96
                dst[x, y, mat ^ mz] = full[pl.ds(pl.multiple_of(row, 96), 96), :]


def attention_back(place, grad, low, mixed, q, k, v, lse, reach, slope, x, y, w,
                   keep, send, full, up, dq, dk, dv):
    def cast(rows):
        low[rows, :] = grad[rows, :].astype(BF16)

    rows_loop(grad.shape[0], 128, cast)
    weight_grad(mixed, low, full)
    attn_shards(full, place, 3, keep, send)
    project(low, w.at[3], up)
    attend_back(q, k, v, up, mixed, lse, reach, slope_of(slope, 0), dq, dk, dv)
    for mat, (side, d) in enumerate(((x, dq), (y, dk), (y, dv))):
        weight_grad(d, side, full)
        attn_shards(full, place, mat, keep, send)


def cross_backward(place, two_grad, mixed, q, k, v, lse, reach, slope, radar_low, optical_low, w,
                   one, optical, gain_r, gain_o,
                   one_grad, optical_grad, keep, send, small,
                   low, full, up, dq, dk, dv):
    attention_back(place, two_grad, low, mixed, q, k, v, lse, reach, slope, radar_low, optical_low,
                   w, keep, send, full, up, dq, dk, dv)
    small[...] = jnp.zeros_like(small)

    def body(rows):
        pull = nn(dq[rows, :], w[0])
        dv_, dgain, dshift = norm_back_rows(one[rows, :], gain_r[...], pull)
        total = two_grad[rows, :] + dv_
        one_grad[rows, :] = total
        small[0:1, :] += dgain
        small[1:2, :] += dshift
        small[4:5, :] += jnp.sum(total, axis=0, keepdims=True)
        pull = nn(dk[rows, :], w[1]) + nn(dv[rows, :], w[2])
        dv_, dgain, dshift = norm_back_rows(optical[rows, :].astype(F32), gain_o[...], pull)
        optical_grad[rows, :] = dv_
        small[2:3, :] += dgain
        small[3:4, :] += dshift

    rows_loop(two_grad.shape[0], 256, body)


def self_backward(place, one_grad, mixed, q, k, v, lse, reach, slope, normed, w, radar, gain,
                  radar_grad, keep, send, small,
                  low, full, up, dq, dk, dv):
    attention_back(place, one_grad, low, mixed, q, k, v, lse, reach, slope, normed, normed,
                   w, keep, send, full, up, dq, dk, dv)
    small[...] = jnp.zeros_like(small)

    def body(rows):
        pull = nn(dq[rows, :], w[0]) + nn(dk[rows, :], w[1]) + nn(dv[rows, :], w[2])
        dv_, dgain, dshift = norm_back_rows(radar[rows, :].astype(F32), gain[...], pull)
        radar_grad[rows, :] = one_grad[rows, :] + dv_
        small[0:1, :] += dgain
        small[1:2, :] += dshift

    rows_loop(one_grad.shape[0], 256, body)


def shape(dims, dtype):
    return jax.ShapeDtypeStruct(dims, dtype)


CORE, X_BIT, Y_BIT, Z_NEAR, Z_FAR = 1, 2, 4, 8, 16


def partner(bit):
    dp, head = lax.axis_index("dp"), lax.axis_index("head")
    if bit < 4:
        return (dp, head ^ bit)
    return (dp ^ (bit // 4), head)


def greet(bits):
    greeting(bits)
    pl.semaphore_wait(pltpu.get_barrier_semaphore(), len(bits))


def greeting(bits):
    barrier = pltpu.get_barrier_semaphore()
    for bit in bits:
        pl.semaphore_signal(
            barrier, inc=1, device_id=partner(bit), device_id_type=pl.DeviceIdType.MESH
        )


def send_to(bit, src, dst, send_sem, recv_sem):
    return pltpu.make_async_remote_copy(
        src_ref=src, dst_ref=dst, send_sem=send_sem, recv_sem=recv_sem,
        device_id=partner(bit), device_id_type=pl.DeviceIdType.MESH,
    )


ORDER = (0, 1, 2, 3, 5, 6, 4, 7)


class Gather:
    def __init__(self, w, owns, send, recv, local):
        self.w, self.owns, self.send, self.recv, self.local = w, owns, send, recv, local
        self.mine = lax.axis_index("dp") % 2
        self.part = w.shape[1] // 4

    def copy(self, mat, kind):
        part, half = self.part, self.part // 2
        own = self.owns[mat].at[pl.ds(pl.multiple_of(self.mine * half, half), half)]
        far = pl.ds(2 * part + self.mine * half, half)
        other = pl.ds(2 * part + (1 - self.mine) * half, half)
        w = self.w.at[mat]
        up = lambda rows: pl.ds(rows.start + part, rows.size)
        bit, src, dst = (
            (CORE, self.owns[mat], pl.ds(part, part)),
            (X_BIT, own, far),
            (Y_BIT, w.at[far], far),
            (CORE, w.at[far], up(far)),
            (CORE, w.at[other], up(other)),
        )[kind]
        return send_to(bit, src, w.at[dst], self.send.at[mat, kind], self.recv.at[mat, kind])

    def begin(self, mat):
        self.copy(mat, 1).start()
        self.copy(mat, 0).start()
        self.here(mat).start()

    def here(self, mat):
        return pltpu.make_async_copy(
            self.owns[mat], self.w.at[mat, pl.ds(0, self.part)], self.local.at[mat]
        )

    def after_x(self, mat):
        self.copy(mat, 1).wait_recv()
        self.copy(mat, 2).start()
        self.copy(mat, 3).start()

    def after_y(self, mat):
        self.copy(mat, 2).wait_recv()
        self.copy(mat, 4).start()

    def core_ready(self, mat):
        self.here(mat).wait()
        self.copy(mat, 0).wait_recv()

    def ready(self, mat):
        for kind in (3, 4):
            self.copy(mat, kind).wait_recv()

    def drain(self, mat):
        for kind in range(5):
            self.copy(mat, kind).wait_send()


ROOT, CUBE = 0.7978845608028654, 0.044715


def load_vectors(parts, vectors):
    d = vectors.shape[1]
    at = 0
    for part in parts:
        for i in range(part.shape[0] // d):
            vectors[at : at + 1, :] = part[i * d : (i + 1) * d].reshape(1, d)
            at += 1


class Loads:
    def __init__(self, sems):
        self.sems, self.next = sems, 0

    def start(self, src, dst):
        copy = pltpu.make_async_copy(src, dst, self.sems.at[self.next])
        self.next += 1
        copy.start()
        return copy


def forward_body(remote, *refs):
    arrived, refs = refs[:3], refs[3:]
    slopes, refs = refs[0], refs[1:]
    vector_parts, refs = refs[:8], refs[8:]
    owns, refs = refs[: 8 if remote else 1], refs[8 if remote else 1 :]
    outs, refs = refs[: 17 if remote else 16], refs[17 if remote else 16 :]
    vectors, columns, store_sems, load_sems = refs[:4]
    refs = refs[4:]
    (radar, optical, table), parts, refs = refs[:3], refs[3:11], refs[11:]
    load = Loads(load_sems)
    coming = [load.start(a, b) for a, b in zip(arrived + vector_parts, (radar, optical, table) + parts)]
    w, refs = (refs[0], refs[1:]) if remote else (owns[0], refs)
    kept = refs[:16]
    (normed, radar_low, optical_low, sq, sk, sv, cq, ck, cv, s_mixed, c_mixed, s_lse, c_lse,
     two, one, reach) = kept
    if remote:
        o_w, outs = outs[0], outs[1:]
        hub = Gather(w, owns, *refs[16:])
        greet((CORE, X_BIT, Y_BIT))
        for mat in ORDER:
            hub.begin(mat)
        slope = slope_of(slopes, lax.axis_index("head"))
    else:
        slope = slope_of(slopes, 0)
    for copy in coming:
        copy.wait()
    load_vectors(parts, vectors)
    gain_s, shift_s, gain_r, shift_r, gain_o, shift_o, bias_s, bias_c = (
        vectors.at[i : i + 1, :] for i in range(8)
    )
    stores = []

    def store(src, dst):
        copy = pltpu.make_async_copy(src, dst, store_sems.at[len(stores)])
        stores.append(copy)
        copy.start()

    def done(*names):
        for ref in names:
            i = [r is ref for r in kept].index(True)
            store(ref, outs[i])

    def hop(kind, *places):
        if remote:
            for i in places:
                (hub.after_x if kind == "x" else hub.after_y)(ORDER[i])

    near_here = []

    def core_ready(*mats):
        if remote:
            for mat in mats:
                hub.core_ready(mat)
                near_here.append(mat)

    def ready(mat):
        if mat not in near_here:
            core_ready(mat)
        if remote:
            hub.ready(mat)
            store(w.at[mat], o_w.at[mat])

    def loop_hops(index, at):
        for k, hops in at.items():
            @pl.when(index == k)
            def _():
                for kind, place in hops:
                    hop(kind, place)

    scale = HEAD_DIM**-0.5
    norm_rows(radar, gain_s, shift_s, normed)
    done(normed)
    fill_reach(table, columns, reach)
    done(reach)
    norm_rows(optical, gain_o, shift_o, optical_low)
    done(optical_low)
    core_ready(0, 1, 2)
    project(normed, w.at[0], sq, scale, 0)
    project(normed, w.at[1], sk, None, 0)
    project(normed, w.at[2], sv, None, 0)
    attend(sq, sk, sv, reach, slope, s_mixed, s_lse,
           lambda hp: loop_hops(hp, {2: (("x", 0),)}), (0, 3))
    core_ready(5, 6)
    project(optical_low, w.at[5], ck, None, 0)
    hop("x", 1)
    project(optical_low, w.at[6], cv, None, 0)
    hop("x", 2)
    hop("y", 0)
    ready(0)
    project(normed, w.at[0], sq, scale, 1)
    done(sq)
    hop("x", 3)
    hop("y", 1)
    ready(1)
    project(normed, w.at[1], sk, None, 1)
    done(sk)
    hop("y", 2)
    hop("x", 4)
    ready(2)
    project(normed, w.at[2], sv, None, 1)
    done(sv)
    attend(sq, sk, sv, reach, slope, s_mixed, s_lse,
           lambda hp: loop_hops(hp, {4: (("y", 3), ("x", 5))}), (3, 6))
    done(s_mixed, s_lse)
    hop("x", 6)
    hop("y", 4)
    ready(3)
    add_out(radar, s_mixed, w.at[3], bias_s, one)
    done(one)
    ready(5)
    project(optical_low, w.at[5], ck, None, 1)
    done(ck)
    norm_rows(one, gain_r, shift_r, radar_low)
    done(radar_low)
    core_ready(4)
    project(radar_low, w.at[4], cq, scale, 0)
    attend(cq, ck, cv, reach, slope, c_mixed, c_lse,
           lambda hp: loop_hops(hp, {0: (("x", 7), ("y", 5)), 2: (("y", 6),)}), (0, 3))
    ready(6)
    project(optical_low, w.at[6], cv, None, 1)
    done(cv)
    ready(4)
    project(radar_low, w.at[4], cq, scale, 1)
    done(cq)
    attend(cq, ck, cv, reach, slope, c_mixed, c_lse,
           lambda hp: loop_hops(hp, {4: (("y", 7),)}), (3, 6))
    done(c_mixed, c_lse)
    ready(7)
    add_out(one, c_mixed, w.at[7], bias_c, two)
    done(two)
    if remote:
        for mat in range(8):
            hub.drain(mat)
    for copy in stores:
        copy.wait()


def run_forward(remote, radar, optical, vectors, table, slopes, weights):
    n, d = radar.shape
    low, lse, wide = shape((n, d), BF16), shape((6, 2, n), F32), shape((n, d), F32)
    kept = [low] * 11 + [lse, lse, wide, wide, shape((n, n), F32)]
    whole = [shape((8, d, d), BF16)] if remote else []
    return pl.pallas_call(
        functools.partial(forward_body, remote),
        out_shape=whole + kept,
        in_specs=[HBM] * 3 + [SMEM] + [HBM] * len(vectors)
        + [HBM if remote else VMEM] * len(weights),
        out_specs=[HBM] * len(whole + kept),
        scratch_shapes=[
            pltpu.VMEM((8, d), F32), pltpu.VMEM((3, n, 128), F32),
            pltpu.SemaphoreType.DMA((24,)), pltpu.SemaphoreType.DMA((11,)),
        ] + [pltpu.VMEM(a.shape, a.dtype) for a in (radar, optical, table) + vectors] + [pltpu.VMEM(a.shape, a.dtype) for a in whole + kept]
        + ([pltpu.SemaphoreType.DMA((8, 5))] * 2 + [pltpu.SemaphoreType.DMA((8,))] if remote else []),
        compiler_params=pltpu.CompilerParams(
            vmem_limit_bytes=LIMIT, **(dict(collective_id=0, has_side_effects=True) if remote else {})
        ),
        name="forward",
        cost_estimate=pl.CostEstimate(flops=8 * 10**9, bytes_accessed=3 * 10**7, transcendentals=0),
    )(radar, optical, table, slopes, *vectors, *weights)


PATHS = {
    "A": ("XY", "YX", "XY", "XY"),
    "B": ("XY", "YX", "YX", "YX"),
    "C": ("NYX", "NYX", "XYN", "XYN"),
    "S": ("YXN", "YXN", "YXN", "XYN"),
}
AGAIN = {
    "C": ("NY", "NY", "NY", "NY"),
    "S": ("NY", "YN", "NY", "NY"),
}
NEAR_PAIR = 0
FIRST_SLOT = {"A": 0, "B": 4, "C": 8, "S": 0}
FIRST_BACK = {"A": 0, "C": 4, "S": 8, "B": 12}
UNIT = {"A": 0, "B": 1, "C": 0, "S": 1}
AXES = {"X": X_BIT, "Y": Y_BIT, "N": Z_NEAR, "F": Z_FAR}


def core_slot(unit, j):
    return {"A": j % 2, "B": 2 + j % 2}.get(unit, j)


class Sums:
    def __init__(self, refs):
        (self.g, self.rc, self.r1, self.r2, self.r3, self.rf, self.rn, self.zb, self.zn, self.zf,
         self.all,
         self.cs, self.cr, self.s1, self.q1, self.s2, self.q2, self.s3, self.q3, self.sf, self.qf,
         self.sn, self.qn, self.sz, self.qz, self.sa, self.qa,
         self.sm, self.sq, self.ss, self.sr) = refs
        dp, head = lax.axis_index("dp"), lax.axis_index("head")
        self.mc, self.mx, self.my = head % 2, head // 2, dp % 2
        self.z0, self.z1 = dp // 2 % 2, dp // 4
        columns = self.g.shape[-1] // 2
        self.columns = [
            pl.ds(pl.multiple_of(columns * z, columns), columns) for z in (self.z1, 1 - self.z1)
        ]

    def mine(self, unit):
        if unit in "CS":
            return {"C": 0, "X": 0, "Y": self.my, "N": self.z0}
        return {"C": self.mc, "X": self.mx, "Y": self.my}

    def slots(self, unit, j):
        slot = FIRST_SLOT[unit] + j
        if unit == "B" and j // 2 == NEAR_PAIR:
            slot = 4 + 2 * NEAR_PAIR + self.z0
        return slot, FIRST_BACK[unit] + j

    def part(self, unit, j, held, sent=None):
        at = {"X": slice(None), "Y": slice(None), "N": slice(None)}
        mine = self.mine(unit)
        for axis in held:
            at[axis] = mine[axis]
        if sent:
            at[sent] = 1 - mine[sent]
        return self.g.at[self.slots(unit, j)[0], mine["C"], at["X"], at["Y"], at["N"]]

    def put(self, unit, slot, row, value):
        end = row + value.shape[0]
        at = row
        while at < end:
            t, half = at // 96, at // 48 % 2
            stop = min(end, at // 48 * 48 + 48)
            if unit in "AB":
                y, x, c = t // 4, t // 2 % 2, t % 2
            else:
                x, c, y = t // 4, t // 2 % 2, t % 2
            self.g[slot, c, x, y, half, at % 48 : at % 48 + stop - at, :] = value[
                at - row : stop - row
            ].astype(BF16)
            at = stop

    def add(self, part, got):
        for at in np.ndindex(*part.shape[:-2]):
            part[*at] = part[*at] + got[*at]

    def core_copy(self, unit, j):
        slot = FIRST_SLOT[unit] + j
        return send_to(
            CORE, self.g.at[slot, 1 - self.mine(unit)["C"]], self.rc.at[core_slot(unit, j)],
            self.cs.at[slot], self.cr.at[slot],
        )

    def step_copy(self, unit, j, step):
        path = PATHS[unit][j]
        back = FIRST_BACK[unit] + j
        got, send, recv = (
            (self.r1, self.s1, self.q1), (self.r2, self.s2, self.q2), (self.r3, self.s3, self.q3)
        )[step]
        if step == 2:
            back -= 4
        return send_to(
            AXES[path[step]], self.part(unit, j, path[:step], path[step]), got.at[back],
            send.at[back], recv.at[back],
        ), got.at[back]

    def begin(self, unit, j):
        self.core_copy(unit, j).start()

    def event(self, kind, unit, j):
        u = UNIT.get(unit)
        attention = unit in "CS"
        if kind == "1":
            self.core_copy(unit, j).wait()
            mine, got = self.mine(unit), self.rc.at[core_slot(unit, j)]
            chunk = self.g.at[FIRST_SLOT[unit] + j, mine["C"]]
            if unit == "B" and j // 2 == NEAR_PAIR:
                self.add(chunk, got)
                if j % 2:
                    self.near_copy().start()
                return
            axis = PATHS[unit][j][0]
            place = "XYN".index(axis)
            for keep in (1 - mine[axis], mine[axis]):
                at = [slice(None)] * 3
                at[place] = keep
                self.add(chunk.at[*at], got.at[*at])
                if keep is not mine[axis]:
                    self.step_copy(unit, j, 0)[0].start()
        elif kind == "n":
            self.near_copy().wait()
            self.add(self.part("B", 2 * j, ""), self.rn)
            self.step_copy("B", 2 * j, 0)[0].start()
        elif kind in "23" or (kind == "5" and attention):
            step = {"2": 0, "3": 1, "5": 2}[kind]
            path = PATHS[unit][j]
            copy, got = self.step_copy(unit, j, step)
            copy.wait()
            part = self.part(unit, j, path[: step + 1])
            if step == 1 and not attention:
                early = unit == "B" and j // 2 == NEAR_PAIR
                z = 2 * (self.z0 if early else j % 2) + j // 2
                for half in range(2):
                    self.zb[u, z, half] = part[half] + got[half]
                return
            if step == 2:
                part[...] = part[...] + got[...]
                self.far_quarter(unit, j).start()
            else:
                self.add(part, got)
                self.step_copy(unit, j, step + 1)[0].start()
        elif kind == "4":
            self.z_copy(unit).start()
        elif kind == "5":
            self.z_copy(unit).wait()
            at = self.near_shards(unit)
            self.add(self.zb.at[u, pl.ds(2 * self.z0 + at.start, at.size)], self.zn.at[u, at])
            self.far_copy(u).start()
        elif kind == "6":
            if attention:
                self.far_quarter(unit, j).wait()
                columns = self.columns[0]
                own = self.part(unit, j, "XYN")[:, columns]
                total = own.astype(F32) + self.rf[u, j].astype(F32)
                self.all[u, j, self.my, self.z0, :, columns] = total.astype(BF16)
                self.gather_copy(unit, j, 0).start()
                return
            self.far_copy(u).wait()
            mine = 2 * self.z0 + self.z1
            self.out[unit][...] = self.zb[u, mine].astype(F32) + self.zf[u].astype(F32)
            self.stores.append(self.load.start(self.out[unit], self.done[unit]))
        elif kind in "789":
            step = int(kind) - 7
            self.gather_copy(unit, j, step).wait()
            if step < 2:
                self.gather_copy(unit, j, step + 1).start()
            else:
                self.stores.append(self.load.start(self.all.at[u, j], self.done["all"].at[u, j]))
        elif kind == "m":
            self.small_copy(j).wait()
            self.sm[j + 1] = self.sm[j] + self.sq[j]
            if j < 4:
                self.small_copy(j + 1).start()

    def small_copy(self, step):
        bit = (CORE, X_BIT, Y_BIT, Z_NEAR, Z_FAR)[step]
        return send_to(bit, self.sm.at[step], self.sq.at[step], self.ss.at[step], self.sr.at[step])

    def far_quarter(self, unit, j):
        at = FIRST_BACK[unit] - 4 + j
        return send_to(
            Z_FAR, self.part(unit, j, "XYN").at[:, self.columns[1]], self.rf.at[UNIT[unit], j],
            self.sf.at[at], self.qf.at[at],
        )

    def near_shards(self, unit):
        return pl.ds(1 - NEAR_PAIR, 1) if unit == "B" else pl.ds(0, 2)

    def z_copy(self, unit):
        u, at = UNIT[unit], self.near_shards(unit)
        return send_to(
            Z_NEAR, self.zb.at[u, pl.ds(2 * (1 - self.z0) + at.start, at.size)], self.zn.at[u, at],
            self.sn.at[u], self.qn.at[u],
        )

    def near_copy(self):
        return send_to(
            Z_NEAR, self.g.at[4 + 2 * NEAR_PAIR + 1 - self.z0, self.mc], self.rn,
            self.sn.at[2], self.qn.at[2],
        )

    def far_copy(self, u):
        return send_to(
            Z_FAR, self.zb.at[u, 2 * self.z0 + 1 - self.z1], self.zf.at[u], self.sz.at[u], self.qz.at[u]
        )

    def gather_copy(self, unit, j, step):
        whole = self.all.at[UNIT[unit], j]
        axis = ("F" + AGAIN[unit][j])[step]
        if step == 0:
            held = whole.at[self.my, self.z0, :, self.columns[0]]
        elif step == 1:
            held = whole.at[self.my, self.z0]
        else:
            held = whole.at[self.my] if axis == "Y" else whole.at[:, self.z0]
        at = FIRST_BACK[unit] - 4 + j
        return send_to(AXES[axis], held, held, self.sa.at[step, at], self.qa.at[step, at])


TICKS = {
    "f1a": "1A0",
    "f1b": "1B0",
    "f1o": "1A1",
    "f2g": "1B1",
    "f2o": "1A2",
    "f3a": "1B2",
    "g": "1B3",
    "c0n": "1A3",
    "ch0": "2A1",
    "ch1": "1C0",
    "ch2": "2A2",
    "ch4": "nB0",
    "ch5": "2A0",
    "c2n": "2A3",
    "c4": "1C1 2B3",
    "c5": "2B0",
    "s0n": "2B2 3A1 3A0 3A2",
    "s0": "3A3 4A0 1S0",
    "sh0": "1C2",
    "sh1": "3B3",
    "sh2": "3B0 1C3 3B2 4B0",
    "sh3": "2C1",
    "sh4": "5A0 2C0",
    "sh5": "2C2",
    "s2": "5B0",
    "s2n": "3C1 1S1 2S0 3C0",
    "s3": "5C1 3C2",
    "s4": (
        "2C3 1S2 3S0 1S3",
        "5C0 2S1 6C1 5S0",
        "6C0 6A0 3C3 5C2",
    ),
    "s5": (
        "2S3 7C1 3S1 6B0",
        "2S2 6S0",
    ),
    "tail": (
        "5C3 mM0 7C0 6C2",
        "5S1 3S3 8C1 7C2",
        "3S2 5S3 8C0 6S1",
        "5S2 6C3 7S0 8C2",
        "6S3 mM1 7C3 7S1",
        "9C0 6S2 8S0 7S3",
        "mM2 8C3 9C1 7S2",
        "8S1 8S3 9C2 9S0",
        "mM3 9C3 8S2 9S2",
        "9S1 9S3 mM4",
    ),
}


def ticks(hub, name):
    words = TICKS.get(name, ())
    for word in " ".join((words,) if isinstance(words, str) else words).split():
        hub.event(word[0], word[1], int(word[2]))


def loop_ticks(hub, name, index, names):
    for k, at in enumerate(names):
        if at in TICKS:
            @pl.when(index == k)
            def _():
                ticks(hub, at)


def attention_unit(hub, unit, grad, low, mixed, q, k, v, lse, reach, slope, x, y, w, up, dq, dk, dv):
    tag = unit.lower()

    def cast(rows):
        low[rows, :] = grad[rows, :].astype(BF16)

    def chunk(j, grads, side):
        ticks(hub, f"{tag}{j}n")
        for n in range(grads.shape[1] // 256):
            hub.put(unit, FIRST_SLOT[unit] + j, 256 * n,
                    tn(grads[:, 256 * n : 256 * n + 256], side[...]))
        hub.begin(unit, j)
        ticks(hub, f"{tag}{j + 1 if j else 0}")

    rows_loop(grad.shape[0], 128, cast)
    chunk(0, mixed, low)
    project(low, w.at[3], up)
    ticks(hub, f"{tag}1")
    attend_back(q, k, v, up, mixed, lse, reach, slope, dq, dk, dv,
                lambda hp: loop_ticks(hub, tag, hp, [f"{tag}h{i}" for i in range(6)]))
    chunk(1, dq, x)
    chunk(2, dk, y)
    chunk(3, dv, y)


def backward_body(*refs):
    (h_two, h_cot, h_in, h_out, h_w, h_cq, h_ck, h_cv, h_cm, h_rlow, h_olow,
     h_sq, h_sk, h_sv, h_sm, h_normed, h_one, h_opt, h_radar, h_reach,
     h_clse, h_slse), refs = refs[:22], refs[22:]
    vector_parts, slopes, refs = refs[:7], refs[7], refs[8:]
    (o_merged, o_radar, o_opt, o_fin, o_fout, o_all, o_small), refs = refs[:7], refs[7:]
    vectors, c_lse, s_lse, fin, fout, gathered, refs = *refs[:6], refs[6:]
    parts, refs = refs[:7], refs[7:]
    sums, refs = refs[:10], refs[10:]
    (wa, wb, q, k, v, mixed, x, y, two, two_grad, out, pull, one,
     cot, low, up, dq, dk, dv, reach, sm, sq), sems = refs[:22], refs[22:]
    hub = Sums(sums + (gathered,) + tuple(sems[:16]) + (sm, sq) + tuple(sems[16:18]))
    load = Loads(sems[18])
    hub.out = {"A": fin, "B": fout}
    hub.done = {"A": o_fin, "B": o_fout, "all": o_all}
    hub.load, hub.stores = load, []
    tile_sems = sems[19]
    slope = slope_of(slopes, lax.axis_index("head"))
    gain_s, gain_r, gain_o, gain_f, shift_f, b_out = (
        vectors.at[i : i + 1, :] for i in range(6)
    )
    n = two.shape[0]
    width = wb.shape[1]
    steps = h_in.shape[1] // width

    def tile(i):
        at = pl.ds(pl.multiple_of(i * width, width), width)
        slot = i % 2
        return (
            pltpu.make_async_copy(h_in.at[:, at], wb.at[2 * slot], tile_sems.at[slot, 0]),
            pltpu.make_async_copy(h_out.at[at, :], wb.at[2 * slot + 1], tile_sems.at[slot, 1]),
        )

    greeting((CORE, X_BIT, Y_BIT, Z_NEAR, Z_FAR))
    coming = [load.start(a, b) for a, b in zip(vector_parts, parts)]
    first = [load.start(h_two, two), load.start(h_cot, cot)]
    for copy in tile(0):
        copy.start()
    for copy in coming:
        copy.wait()
    load_vectors(parts, vectors)
    sm[0] = jnp.zeros_like(sm[0])
    out[...] = jnp.zeros_like(out)
    pull[...] = jnp.zeros_like(pull)
    first[0].wait()
    norm_rows(two, gain_f, shift_f, low)
    first[1].wait()
    later = [load.start(a, b) for a, b in (
        (h_cm, mixed), (h_w.at[pl.ds(4, 4)], wa), (h_cq, q), (h_ck, k), (h_cv, v),
        (h_rlow, x), (h_olow, y), (h_one, one), (h_reach, reach), (h_clse, c_lse),
        (h_slse, s_lse))]

    def feed(i, _):
        for copy in tile(i):
            copy.wait()

        @pl.when(i < steps - 1)
        def _():
            for copy in tile(i + 1):
                copy.start()

        w_in, w_out = wb.at[2 * (i % 2)], wb.at[2 * (i % 2) + 1]
        hidden, grad = up, dq
        blocks = [slice(m, m + 256) for m in range(0, width, 256)]

        def feed_ticks(name):
            loop_ticks(hub, "f", i, [f"f{s}{name}" for s in range(4)])

        for n, at in enumerate(blocks):
            if n:
                feed_ticks("ab"[n - 1])
            h = nn(low[...], w_in[:, at]) + vectors[pl.ds(6 + i, 1), at]
            square = h * h
            half = 0.5 + 0.5 * jnp.tanh(h * (ROOT + ROOT * CUBE * square))
            hidden[:, at] = (h * half).astype(BF16)
            rise = half * (
                1.0 + h * (1.0 - half) * (2 * ROOT + 6 * ROOT * CUBE * square)
            )
            part = (nt(cot[...], w_out[at, :]) * rise).astype(BF16)
            grad[:, at] = part
            sm[0, pl.ds(24 + i, 1), at] = jnp.sum(part.astype(F32), axis=0, keepdims=True)
        feed_ticks("c")
        for n, at in enumerate(blocks):
            hub.put("A", i, at.start, tn(grad[:, at], low[...]))
            if n == 2:
                hub.begin("A", i)
            feed_ticks("de"[n] if n < 2 else "f")
        for n, at in enumerate(blocks):
            hub.put("B", 4 + i, at.start, tn(hidden[:, at], cot[...]))
            if n == 2:
                hub.begin("B", i)
            feed_ticks("ghi"[n])
        for n, at in enumerate(blocks):
            out[:, at] += nn(hidden[...], w_out[:, at])
            feed_ticks("jkl"[n])
            pull[:, at] += nt(grad[...], w_in[at, :])
            feed_ticks("mno"[n])
        return 0

    pl.semaphore_wait(pltpu.get_barrier_semaphore(), 5)
    lax.fori_loop(0, steps, feed, 0)
    self_w = load.start(h_w.at[pl.ds(0, 4)], wb)

    def close(rows):
        value, cotangent = two[rows, :], cot[rows, :].astype(F32)
        dv[rows, :] = (value + out[rows, :] + b_out[...]).astype(BF16)
        dval, dgain, dshift = norm_back_rows(value, gain_f[...], pull[rows, :])
        total = cotangent + dval
        two_grad[rows, :] = total
        sm[0, 0:1, :] += dgain
        sm[0, 1:2, :] += dshift
        sm[0, 2:3, :] += jnp.sum(cotangent, axis=0, keepdims=True)
        sm[0, 3:4, :] += jnp.sum(total, axis=0, keepdims=True)

    rows_loop(n, 128, close)
    stores = [load.start(dv, o_merged)]
    opt_load = load.start(h_opt, cot)
    ticks(hub, "g")
    for copy in later:
        copy.wait()
    stores[0].wait()
    attention_unit(hub, "C", two_grad, low, mixed, q, k, v, c_lse, reach, slope, x, y, wa,
                   up, dq, dk, dv)
    later = [load.start(a, b) for a, b in (
        (h_sm, mixed), (h_sq, q), (h_sk, k), (h_sv, v), (h_normed, x), (h_radar, y))]
    opt_load.wait()

    def cross(rows):
        dval, dgain, dshift = norm_back_rows(one[rows, :], gain_r[...], nn(dq[rows, :], wa[0]))
        total = two_grad[rows, :] + dval
        out[rows, :] = total
        sm[0, 8:9, :] += dgain
        sm[0, 9:10, :] += dshift
        sm[0, 12:13, :] += jnp.sum(total, axis=0, keepdims=True)
        dval, dgain, dshift = norm_back_rows(
            cot[rows, :].astype(F32), gain_o[...], nn(dk[rows, :], wa[1]) + nn(dv[rows, :], wa[2])
        )
        pull[rows, :] = dval
        sm[0, 10:11, :] += dgain
        sm[0, 11:12, :] += dshift

    rows_loop(n, 256, cross)
    stores = [load.start(pull, o_opt)]
    ticks(hub, "c5")
    for copy in later:
        copy.wait()
    self_w.wait()
    attention_unit(hub, "S", out, low, mixed, q, k, v, s_lse, reach, slope, x, x, wb,
                   up, dq, dk, dv)

    def own(rows):
        dval, dgain, dshift = norm_back_rows(
            y[rows, :].astype(F32), gain_s[...],
            nn(dq[rows, :], wb[0]) + nn(dk[rows, :], wb[1]) + nn(dv[rows, :], wb[2]),
        )
        two[rows, :] = out[rows, :] + dval
        sm[0, 16:17, :] += dgain
        sm[0, 17:18, :] += dshift

    rows_loop(n, 256, own)
    stores.append(load.start(two, o_radar))
    hub.small_copy(0).start()
    ticks(hub, "s5")
    ticks(hub, "tail")
    stores.append(load.start(sm.at[5], o_small))
    for copy in stores + hub.stores:
        copy.wait()


def run_backward(two, cot, feed_in, feed_out, w, cross, own, one, optical, radar, reach,
                 c_lse, s_lse, vectors, slopes):
    n, d = two.shape
    low, wide = pltpu.VMEM((n, d), BF16), pltpu.VMEM((n, d), F32)
    chunk = lambda *dims: pltpu.VMEM(dims + (48, d), BF16)
    sems = lambda *dims: pltpu.SemaphoreType.DMA(dims)
    return pl.pallas_call(
        backward_body,
        out_shape=[
            shape((n, d), BF16), shape((n, d), F32), shape((n, d), F32),
            shape((2, 48, d), F32), shape((2, 48, d), F32), shape((2, 4, 2, 2, 48, d), BF16),
            shape((32, d), F32),
        ],
        in_specs=[HBM] * (22 + len(vectors)) + [SMEM],
        out_specs=[HBM] * 7,
        scratch_shapes=[
            pltpu.VMEM((16, d), F32), pltpu.VMEM(c_lse.shape, F32), pltpu.VMEM(s_lse.shape, F32),
            pltpu.VMEM((2, 48, d), F32), pltpu.VMEM((2, 48, d), F32), chunk(2, 4, 2, 2),
            *(pltpu.VMEM(a.shape, F32) for a in vectors),
            chunk(12, 2, 2, 2, 2), chunk(4, 2, 2, 2), chunk(16, 2, 2), chunk(16, 2), chunk(8),
            pltpu.VMEM((2, 4, 48, d // 2), BF16), chunk(2, 2, 2),
            chunk(2, 4, 2), chunk(2, 2, 2), chunk(2, 2),
            pltpu.VMEM((4, d, d), BF16), pltpu.VMEM((4, d, d), BF16),
            low, low, low, low, low, low, wide, wide, wide, wide, wide,
            low, low, low, low, low, low, pltpu.VMEM((n, n), F32),
            pltpu.VMEM((6, 32, d), F32), pltpu.VMEM((5, 32, d), F32),
            sems(12), sems(12), sems(16), sems(16), sems(16), sems(16), sems(8), sems(8),
            sems(8), sems(8), sems(3), sems(3), sems(2), sems(2),
            sems(3, 8), sems(3, 8), sems(5), sems(5),
            sems(48), sems(2, 2),
        ],
        compiler_params=pltpu.CompilerParams(
            vmem_limit_bytes=LIMIT, collective_id=1, has_side_effects=True
        ),
        name="backward",
        cost_estimate=pl.CostEstimate(flops=35 * 10**9, bytes_accessed=5 * 10**7, transcendentals=0),
    )(two, cot, feed_in, feed_out, w, *cross, *own, one, optical, radar, reach,
      c_lse, s_lse, *vectors, slopes)


def call(body, outs, scratch, operands, in_specs, **more):
    return pl.pallas_call(
        body,
        out_shape=outs,
        in_specs=in_specs,
        out_specs=[VMEM] * len(outs),
        scratch_shapes=scratch,
        compiler_params=pltpu.CompilerParams(vmem_limit_bytes=LIMIT),
        **more,
    )(*operands)


def run_feed(place, two, cot, gain, shift, w_in, b_in, w_out, b_out):
    n, d = two.shape
    f = w_in.shape[1]
    tile = 768
    whole = lambda *dims: pl.BlockSpec(dims, lambda i, p: (0,) * len(dims))
    slots = pl.BlockSpec((2, 2, 1, 96, d), lambda i, p: (0, 0, i ^ p[0], 0, 0))
    grad = shape((2, 2, 4, 96, d), BF16)
    return pl.pallas_call(
        feed_step,
        grid_spec=pltpu.PrefetchScalarGridSpec(
            num_scalar_prefetch=1,
            grid=(f // tile,),
            in_specs=[
                whole(n, d), whole(n, d), whole(1, d), whole(1, d),
                pl.BlockSpec((d, tile), lambda i, p: (0, i)),
                pl.BlockSpec((1, tile), lambda i, p: (0, i)),
                pl.BlockSpec((tile, d), lambda i, p: (i, 0)),
                whole(1, d),
            ],
            out_specs=[
                whole(n, d), whole(n, d), slots, slots, slots, slots,
                pl.BlockSpec((1, 1, tile), lambda i, p: (i, 0, 0)),
                whole(8, d),
            ],
            scratch_shapes=[
                pltpu.VMEM((n, d), BF16), pltpu.VMEM((n, d), F32), pltpu.VMEM((n, d), F32),
                pltpu.VMEM((tile, d), BF16), pltpu.VMEM((tile, d), BF16),
            ],
        ),
        out_shape=[
            shape((n, d), BF16), shape((n, d), F32), grad, grad, grad, grad,
            shape((f // tile, 1, tile), F32), shape((8, d), F32),
        ],
        compiler_params=pltpu.CompilerParams(vmem_limit_bytes=LIMIT),
        name="feed",
        cost_estimate=pl.CostEstimate(flops=15 * 10**9, bytes_accessed=25 * 10**6, transcendentals=0),
    )(place, two, cot, gain, shift, w_in, b_in, w_out, b_out)


def back_scratch(n, d):
    low = pltpu.VMEM((n, d), BF16)
    return [low, pltpu.VMEM((d, d), BF16), low, low, low, low]


def run_cross_backward(place, two_grad, mixed, q, k, v, lse, reach, slope, radar_low, optical_low,
                       w, one, optical, gain_r, gain_o):
    n, d = one.shape
    grad = shape((2, 2, 4, 96, d), BF16)
    wide = shape((n, d), F32)
    return call(
        cross_backward,
        [wide, wide, grad, grad, shape((8, d), F32)],
        back_scratch(n, d),
        (place, two_grad, mixed, q, k, v, lse, reach, slope, radar_low, optical_low,
         w, one, optical, gain_r, gain_o),
        [SMEM] + [VMEM] * 7 + [SMEM] + [VMEM] * 7,
        name="cross_backward",
        cost_estimate=pl.CostEstimate(flops=12 * 10**9, bytes_accessed=25 * 10**6, transcendentals=0),
    )


def run_self_backward(place, one_grad, mixed, q, k, v, lse, reach, slope, normed, w, radar, gain):
    n, d = one_grad.shape
    grad = shape((2, 2, 4, 96, d), BF16)
    return call(
        self_backward,
        [shape((n, d), F32), grad, grad, shape((8, d), F32)],
        back_scratch(n, d),
        (place, one_grad, mixed, q, k, v, lse, reach, slope, normed, w, radar, gain),
        [SMEM] + [VMEM] * 7 + [SMEM] + [VMEM] * 4,
        name="self_backward",
        cost_estimate=pl.CostEstimate(flops=12 * 10**9, bytes_accessed=25 * 10**6, transcendentals=0),
    )


def finish(bias_part, *refs):
    sources, refs = refs[:7], refs[7:]
    outs, refs = refs[:25], refs[25:]
    in_sems, out_sems, refs = refs[0], refs[1], refs[2:]
    held, ready = refs[:7], refs[7:]
    got, small = held[:2]
    load, store = Loads(in_sems), Loads(out_sems)
    loads = [load.start(src, dst) for src, dst in zip(sources, held)]
    stores = []
    mats, vectors, bias = ready[:8], ready[8:19], ready[19]
    loads[0].wait()
    for u in range(2):
        for j, mat in enumerate((3, 0, 1, 2)):
            at = 4 * u + mat
            for half in range(2):
                for part in range(2):
                    row = 96 * half + 48 * part
                    mats[at][row : row + 48, :] = got[u, j, half, part].astype(F32)
            stores.append(store.start(mats[at], outs[5 + at]))
    for copy, src, dst in zip(loads[2:], held[2:], outs):
        copy.wait()
        stores.append(store.start(src, dst))
    loads[1].wait()
    for row, vector in zip((16, 17, 12, 8, 9, 10, 11, 3, 0, 1, 2), vectors):
        vector[...] = small[row : row + 1, :].reshape(vector.shape)
    mine, per = bias_part[0], small.shape[1] // bias.shape[0]
    line = small[pl.ds(24 + mine // per, 1), :]
    shift = (small.shape[1] - mine % per * bias.shape[0]) % small.shape[1]
    bias[...] = pltpu.roll(line, shift, 1)[:, : bias.shape[0]].reshape(bias.shape)
    for src, dst in zip(ready[8:], outs[13:]):
        stores.append(store.start(src, dst))
    for copy in stores:
        copy.wait()


def run_finish(mine, got, small, merged, radar, optical, fin, fout):
    d = got.shape[-1]
    moved = (merged, radar, optical, fin, fout)
    made = [shape((192, d), F32)] * 8 + [shape((d,), F32)] * 11 + [shape((96,), F32)]
    outs = pl.pallas_call(
        finish,
        out_shape=[shape(a.shape, a.dtype) for a in moved] + made,
        in_specs=[SMEM] + [HBM] * 7,
        out_specs=[HBM] * 25,
        scratch_shapes=[pltpu.SemaphoreType.DMA((7,)), pltpu.SemaphoreType.DMA((25,))]
        + [pltpu.VMEM(a.shape, a.dtype) for a in (got, small) + moved + tuple(made)],
        compiler_params=pltpu.CompilerParams(vmem_limit_bytes=LIMIT),
        name="finish",
    )(mine.reshape(1), got, small, *moved)
    mats = [o if i % 4 == 3 else o.T for i, o in enumerate(outs[5:13])]
    outs = list(outs)
    outs[3:5] = [o.reshape(-1, d) for o in outs[3:5]]
    return outs[:5], mats[:4], mats[4:], outs[13:24], outs[24]


def shards(
    radar, optical, patch_table, cotangent, norm_self_gain, norm_self_shift,
    self_query, self_key, self_value, self_out, self_out_bias, norm_radar_gain, norm_radar_shift,
    norm_optical_gain, norm_optical_shift, cross_query, cross_key, cross_value, cross_out,
    cross_out_bias, norm_feed_gain, norm_feed_shift, feed_in, feed_in_bias, feed_out, feed_out_bias,
):
    dp, head = lax.axis_size("dp"), lax.axis_size("head")
    near = (dp, head) == (8, 4)
    row = lambda v: v.reshape(1, -1)
    zero = jnp.int32(0)
    slopes = jnp.asarray(-np.exp2(-8.0 * np.arange(1, HEADS + 1) / HEADS), F32)
    mine = (lax.axis_index("dp") * head + lax.axis_index("head")).astype(jnp.int32)
    place = jnp.stack([zero] * 4)
    weights = (self_query, self_key, self_value, self_out,
               cross_query, cross_key, cross_value, cross_out)
    weights = tuple(w if i % 4 == 3 else w.T for i, w in enumerate(weights))
    if not near:
        w = lax.all_gather(jnp.stack(weights), "head", axis=1, tiled=True)
        weights = (w,)
    vectors = (norm_self_gain, norm_self_shift, norm_radar_gain, norm_radar_shift,
               norm_optical_gain, norm_optical_shift, self_out_bias, cross_out_bias)
    got = run_forward(near, radar, optical, vectors, patch_table, slopes, weights)
    if near:
        w, got = got[0], got[1:]
    (normed, radar_low, optical_low, sq, sk, sv, cq, ck, cv, s_mixed, c_mixed, s_lse, c_lse,
     two, one, reach) = got
    d = radar.shape[1]
    if near:
        merged, radar_grad, optical_grad, feed_in_grad, feed_out_grad, got, small = run_backward(
            two, cotangent, feed_in, feed_out, w,
            (cq, ck, cv, c_mixed, radar_low, optical_low), (sq, sk, sv, s_mixed, normed),
            one, optical, radar, reach,
            c_lse, s_lse,
            (norm_self_gain, norm_radar_gain, norm_optical_gain, norm_feed_gain, norm_feed_shift,
             feed_out_bias, feed_in_bias),
            slopes,
        )
        ((merged, radar_grad, optical_grad, feed_in_grad, feed_out_grad), cross, own, vectors,
         feed_in_bias_grad) = run_finish(
            mine, got, small, merged, radar_grad, optical_grad, feed_in_grad, feed_out_grad)
    else:
        merged, two_grad, in_keep, in_send, out_keep, out_send, bias_in, feed_small = run_feed(
            place, two, cotangent, row(norm_feed_gain), row(norm_feed_shift),
            feed_in, row(feed_in_bias), feed_out, row(feed_out_bias),
        )
        one_grad, optical_grad, cross_keep, cross_send, cross_small = run_cross_backward(
            place, two_grad, c_mixed, cq, ck, cv, c_lse, reach, slopes, radar_low, optical_low,
            w[4:], one, optical, row(norm_radar_gain), row(norm_optical_gain),
        )
        radar_grad, self_keep, self_send, self_small = run_self_backward(
            place, one_grad, s_mixed, sq, sk, sv, s_lse, reach, slopes, normed,
            w[:4], radar, row(norm_self_gain),
        )
        small = jnp.concatenate([feed_small, cross_small, self_small, bias_in.reshape(-1, d)])
        def logical(keep, send, order):
            both = jnp.stack([keep, send])
            return jnp.transpose(both, order).reshape(-1, d)

        def feed_sum(keep, send):
            return lax.psum_scatter(
                logical(keep, send, (3, 2, 1, 0, 4, 5)).astype(F32),
                ("dp", "head"), scatter_dimension=0, tiled=True,
            )

        def attn_sum(keep, send):
            total = logical(keep, send, (3, 1, 0, 2, 4, 5)).astype(F32).reshape(4, -1, d)
            total = lax.psum_scatter(total, "head", scatter_dimension=1, tiled=True)
            total = lax.psum(total, "dp")
            return total[0].T, total[1].T, total[2].T, total[3]

        feed_in_grad, feed_out_grad = feed_sum(in_keep, in_send), feed_sum(out_keep, out_send)
        cross, own = attn_sum(cross_keep, cross_send), attn_sum(self_keep, self_send)
        small = lax.psum(small, ("dp", "head"))
        vectors = [small[i] for i in (16, 17, 12, 8, 9, 10, 11, 3, 0, 1, 2)]
        bias_part = feed_in_bias.shape[0] // (dp * head)
        feed_in_bias_grad = lax.dynamic_slice_in_dim(
            small[24:28].reshape(-1), mine * bias_part, bias_part
        )
    return (
        merged, radar_grad, optical_grad, vectors[0], vectors[1], *own, *vectors[2:7],
        *cross, *vectors[7:10], feed_in_grad.T, feed_in_bias_grad, feed_out_grad, vectors[10],
    )


def solution(mesh):
    token, rep = P(("dp", "head"), None), P()
    col, row = P(None, "head"), P("head", None)
    in_specs = (
        token, token, P(None, ("dp", "head")), token,
        rep, rep, col, col, col, row, rep,
        rep, rep, rep, rep, col, col, col, row, rep,
        rep, rep, rep, rep, rep, rep,
    )
    out_specs = (
        token, token, token,
        rep, rep, col, col, col, row, rep,
        rep, rep, rep, rep, col, col, col, row, rep,
        rep, rep, P(None, ("dp", "head")), P(("dp", "head")), token, rep,
    )
    return jax.shard_map(shards, mesh=mesh, in_specs=in_specs, out_specs=out_specs, check_vma=False)
```

```python
import functools

import jax
import jax.numpy as jnp
import numpy as np
from jax import lax
from jax.experimental import pallas as pl
from jax.experimental.pallas import tpu as pltpu
from jax.sharding import PartitionSpec as P

F32, BF16 = jnp.float32, jnp.bfloat16
HEADS, HEAD_DIM = 12, 64
EPSILON = 1e-06
FAR = 1e12
LIMIT = 62 * 2**20
VMEM = pl.BlockSpec(memory_space=pltpu.VMEM)
SMEM = pl.BlockSpec(memory_space=pltpu.SMEM)
HBM = pl.BlockSpec(memory_space=pl.ANY)


def nn(a, b):
    return lax.dot_general(a, b, (((1,), (0,)), ((), ())), preferred_element_type=F32)


def nt(a, b):
    return lax.dot_general(a, b, (((1,), (1,)), ((), ())), preferred_element_type=F32)


def tn(a, b):
    return lax.dot_general(a, b, (((0,), (0,)), ((), ())), preferred_element_type=F32)


def rows_loop(total, block, body):
    def step(i, _):
        body(pl.ds(pl.multiple_of(i * block, block), block))
        return 0

    lax.fori_loop(0, total // block, step, 0)


def centred(v):
    c = v - jnp.mean(v, axis=-1, keepdims=True)
    return c, lax.rsqrt(jnp.mean(c * c, axis=-1, keepdims=True) + EPSILON)


def norm_rows(src, gain, shift, dst):
    def body(rows):
        c, r = centred(src[rows, :].astype(F32))
        dst[rows, :] = (c * r * gain[...] + shift[...]).astype(BF16)

    rows_loop(src.shape[0], 128, body)


def norm_back_rows(v, gain, u):
    c, r = centred(v)
    hat = c * r
    w = u * gain
    dv = r * (
        w
        - jnp.mean(w, axis=-1, keepdims=True)
        - hat * jnp.mean(w * hat, axis=-1, keepdims=True)
    )
    return dv, jnp.sum(u * hat, axis=0, keepdims=True), jnp.sum(u, axis=0, keepdims=True)


def project(x, w, dst, scale=None, half=None):
    total = w.shape[0]
    if half is None:
        blocks = [(i, 256) for i in range(0, total, 256)]
    else:
        blocks = [(half * total // 2, 256), (half * total // 2 + 256, total // 2 - 256)]
    for at, size in blocks:
        cols = slice(at, at + size)
        y = nt(x[...], w[cols, :])
        dst[:, cols] = (y if scale is None else y * scale).astype(BF16)


def fill_reach(table, columns, reach):
    for i in range(3):
        line = table[i : i + 1, :].astype(F32)
        columns[i] = jnp.broadcast_to(line, (128, line.shape[1])).T

    def body(rows):
        seg, down, across = (
            columns[i, rows, 0:1] - table[i : i + 1, :].astype(F32) for i in range(3)
        )
        reach[rows, :] = jnp.where(seg == 0, jnp.sqrt(down * down + across * across), FAR)

    rows_loop(reach.shape[0], 64, body)


def slope_of(table, group):
    return lambda h: table[3 * (h // 3 ^ group) + h % 3]


def low_half(length):
    return lax.broadcasted_iota(jnp.int32, (length, 128), 1) < HEAD_DIM


def attend(q, k, v, reach, slope, mixed, lse, tick, pairs):
    lo = low_half(q.shape[0])

    def pair(hp, _):
        tick(hp)
        at = pl.ds(pl.multiple_of(hp * 128, 128), 128)
        qs, ks, vs = q[:, at], k[:, at], v[:, at]
        outs, tops = [], []
        for sub in range(2):
            mine = lo if sub == 0 else jnp.logical_not(lo)
            s = nt(jnp.where(mine, qs, jnp.zeros_like(qs)), ks)
            s = s + slope(2 * hp + sub) * reach[...]
            top = jnp.max(s, axis=-1, keepdims=True)
            e = jnp.exp(s - top).astype(BF16)
            outs.append(nn(e, jnp.where(mine, vs, jnp.ones_like(vs))))
            tops.append(top)
        num = jnp.where(lo, outs[0], outs[1])
        den = pltpu.roll(jnp.where(lo, outs[1], outs[0]), HEAD_DIM, 1)
        mixed[:, at] = (num / den).astype(BF16)
        lse_t = (jnp.where(lo, tops[0], tops[1]) + jnp.log(den)).T
        lse[hp] = jnp.concatenate([lse_t[0:1], lse_t[HEAD_DIM : HEAD_DIM + 1]], axis=0)
        return 0

    lax.fori_loop(*pairs, pair, 0)


def attend_back(q, k, v, up, mixed, lse, reach, slope, dq, dk, dv, tick=lambda hp: None):
    lo = low_half(q.shape[0])

    def pair(hp, _):
        tick(hp)
        at = pl.ds(pl.multiple_of(hp * 128, 128), 128)
        qs, ks, vs, ups = q[:, at], k[:, at], v[:, at], up[:, at]
        prod = (ups.astype(F32) * mixed[:, at].astype(F32)).T
        tops = lse[hp]
        dqs, dks, dvs = [], [], []
        for sub in range(2):
            mine = lo if sub == 0 else jnp.logical_not(lo)
            delta = jnp.sum(prod[sub * HEAD_DIM : (sub + 1) * HEAD_DIM], axis=0, keepdims=True)
            s = nt(jnp.where(mine, ks, jnp.zeros_like(ks)), qs)
            p = jnp.exp(s + slope(2 * hp + sub) * reach[...] - tops[sub : sub + 1])
            dp = nt(jnp.where(mine, vs, jnp.zeros_like(vs)), ups)
            ds = (p * (dp - delta)).astype(BF16)
            dvs.append(nn(p.astype(BF16), ups))
            dks.append(nn(ds, qs))
            dqs.append(tn(ds, ks))
        dq[:, at] = (jnp.where(lo, dqs[0], dqs[1]) * HEAD_DIM**-0.5).astype(BF16)
        dk[:, at] = jnp.where(lo, dks[0], dks[1]).astype(BF16)
        dv[:, at] = jnp.where(lo, dvs[0], dvs[1]).astype(BF16)
        return 0

    lax.fori_loop(0, q.shape[1] // 128, pair, 0)


def add_out(base, mixed, w_out, bias, dst):
    def body(cols):
        y = nn(mixed[...], w_out[:, cols])
        dst[:, cols] = base[:, cols].astype(F32) + y + bias[:, cols]

    rows_loop(w_out.shape[1], 256, body)


def place_shards(full, place, at, keep, send):
    my, mx, mc = place[1], place[2], place[3]
    for x in range(2):
        for y in range(2):
            for c, dst in enumerate((keep, send)):
                row = (((y ^ my) * 2 + (x ^ mx)) * 2 + (c ^ mc)) * 96
                dst[x, y, at] = full[pl.ds(pl.multiple_of(row, 96), 96), :]


def feed_step(place, two, cot, gain, shift, w_in, b_in, w_out, b_out,
              merged, two_grad, keep_in, send_in, keep_out, send_out, bias_in, small,
              low, out, pull, full_in, full_out):
    step = pl.program_id(0)
    width = w_out.shape[0]
    block = 256

    @pl.when(step == 0)
    def _():
        norm_rows(two, gain, shift, low)

    for n in range(width // block):
        at = slice(n * block, (n + 1) * block)
        x = nn(low[...], w_in[:, at]) + b_in[:, at]
        inner = 0.7978845608028654 * x * (1.0 + 0.044715 * x * x)
        t = jnp.tanh(inner)
        half = 0.5 * (1.0 + t)
        hidden = (x * half).astype(BF16)
        slope = half + 0.5 * x * (1.0 - t * t) * (
            0.7978845608028654 * (1.0 + 3 * 0.044715 * x * x)
        )
        grad = (nt(cot[...], w_out[at, :]) * slope).astype(BF16)
        bias_in[0, :, at] = jnp.sum(grad.astype(F32), axis=0, keepdims=True)
        part_out = nn(hidden, w_out[at, :])
        part_pull = nt(grad, w_in[:, at])
        if n == 0:
            @pl.when(step == 0)
            def _():
                out[...] = part_out
                pull[...] = part_pull

            @pl.when(step > 0)
            def _():
                out[...] += part_out
                pull[...] += part_pull
        else:
            out[...] += part_out
            pull[...] += part_pull
        full_out[at, :] = tn(hidden, cot[...]).astype(BF16)
        full_in[at, :] = tn(grad, low[...]).astype(BF16)
    place_shards(full_in, place, 0, keep_in.at[:, :], send_in.at[:, :])
    place_shards(full_out, place, 0, keep_out.at[:, :], send_out.at[:, :])

    @pl.when(step == pl.num_programs(0) - 1)
    def _():
        small[...] = jnp.zeros_like(small)

        def body(rows):
            value, cotangent = two[rows, :], cot[rows, :].astype(F32)
            merged[rows, :] = (value + out[rows, :] + b_out[...]).astype(BF16)
            dv, dgain, dshift = norm_back_rows(value, gain[...], pull[rows, :])
            total = cotangent + dv
            two_grad[rows, :] = total
            small[0:1, :] += dgain
            small[1:2, :] += dshift
            small[2:3, :] += jnp.sum(cotangent, axis=0, keepdims=True)
            small[3:4, :] += jnp.sum(total, axis=0, keepdims=True)

        rows_loop(two.shape[0], 128, body)


def weight_grad(grads, rows, full):
    def body(cols):
        full[cols, :] = tn(grads[:, cols], rows[...]).astype(BF16)

    rows_loop(grads.shape[1], 256, body)


def attn_shards(full, place, mat, keep, send):
    my, mz = place[1], place[0]
    for x in range(2):
        for y in range(2):
            for c, dst in enumerate((keep, send)):
                row = ((x * 2 + c) * 2 + (y ^ my)) * 96
                dst[x, y, mat ^ mz] = full[pl.ds(pl.multiple_of(row, 96), 96), :]


def attention_back(place, grad, low, mixed, q, k, v, lse, reach, slope, x, y, w,
                   keep, send, full, up, dq, dk, dv):
    def cast(rows):
        low[rows, :] = grad[rows, :].astype(BF16)

    rows_loop(grad.shape[0], 128, cast)
    weight_grad(mixed, low, full)
    attn_shards(full, place, 3, keep, send)
    project(low, w.at[3], up)
    attend_back(q, k, v, up, mixed, lse, reach, slope_of(slope, 0), dq, dk, dv)
    for mat, (side, d) in enumerate(((x, dq), (y, dk), (y, dv))):
        weight_grad(d, side, full)
        attn_shards(full, place, mat, keep, send)


def cross_backward(place, two_grad, mixed, q, k, v, lse, reach, slope, radar_low, optical_low, w,
                   one, optical, gain_r, gain_o,
                   one_grad, optical_grad, keep, send, small,
                   low, full, up, dq, dk, dv):
    attention_back(place, two_grad, low, mixed, q, k, v, lse, reach, slope, radar_low, optical_low,
                   w, keep, send, full, up, dq, dk, dv)
    small[...] = jnp.zeros_like(small)

    def body(rows):
        pull = nn(dq[rows, :], w[0])
        dv_, dgain, dshift = norm_back_rows(one[rows, :], gain_r[...], pull)
        total = two_grad[rows, :] + dv_
        one_grad[rows, :] = total
        small[0:1, :] += dgain
        small[1:2, :] += dshift
        small[4:5, :] += jnp.sum(total, axis=0, keepdims=True)
        pull = nn(dk[rows, :], w[1]) + nn(dv[rows, :], w[2])
        dv_, dgain, dshift = norm_back_rows(optical[rows, :].astype(F32), gain_o[...], pull)
        optical_grad[rows, :] = dv_
        small[2:3, :] += dgain
        small[3:4, :] += dshift

    rows_loop(two_grad.shape[0], 256, body)


def self_backward(place, one_grad, mixed, q, k, v, lse, reach, slope, normed, w, radar, gain,
                  radar_grad, keep, send, small,
                  low, full, up, dq, dk, dv):
    attention_back(place, one_grad, low, mixed, q, k, v, lse, reach, slope, normed, normed,
                   w, keep, send, full, up, dq, dk, dv)
    small[...] = jnp.zeros_like(small)

    def body(rows):
        pull = nn(dq[rows, :], w[0]) + nn(dk[rows, :], w[1]) + nn(dv[rows, :], w[2])
        dv_, dgain, dshift = norm_back_rows(radar[rows, :].astype(F32), gain[...], pull)
        radar_grad[rows, :] = one_grad[rows, :] + dv_
        small[0:1, :] += dgain
        small[1:2, :] += dshift

    rows_loop(one_grad.shape[0], 256, body)


def shape(dims, dtype):
    return jax.ShapeDtypeStruct(dims, dtype)


CORE, X_BIT, Y_BIT, Z_NEAR, Z_FAR = 1, 2, 4, 8, 16


def partner(bit):
    dp, head = lax.axis_index("dp"), lax.axis_index("head")
    if bit < 4:
        return (dp, head ^ bit)
    return (dp ^ (bit // 4), head)


def greet(bits):
    greeting(bits)
    pl.semaphore_wait(pltpu.get_barrier_semaphore(), len(bits))


def greeting(bits):
    barrier = pltpu.get_barrier_semaphore()
    for bit in bits:
        pl.semaphore_signal(
            barrier, inc=1, device_id=partner(bit), device_id_type=pl.DeviceIdType.MESH
        )


def send_to(bit, src, dst, send_sem, recv_sem):
    return pltpu.make_async_remote_copy(
        src_ref=src, dst_ref=dst, send_sem=send_sem, recv_sem=recv_sem,
        device_id=partner(bit), device_id_type=pl.DeviceIdType.MESH,
    )


ORDER = (0, 1, 2, 3, 5, 6, 4, 7)


class Gather:
    def __init__(self, w, owns, send, recv, local):
        self.w, self.owns, self.send, self.recv, self.local = w, owns, send, recv, local
        self.mine = lax.axis_index("dp") % 2
        self.part = w.shape[1] // 4

    def copy(self, mat, kind):
        part, half = self.part, self.part // 2
        own = self.owns[mat].at[pl.ds(pl.multiple_of(self.mine * half, half), half)]
        far = pl.ds(2 * part + self.mine * half, half)
        other = pl.ds(2 * part + (1 - self.mine) * half, half)
        w = self.w.at[mat]
        up = lambda rows: pl.ds(rows.start + part, rows.size)
        bit, src, dst = (
            (CORE, self.owns[mat], pl.ds(part, part)),
            (X_BIT, own, far),
            (Y_BIT, w.at[far], far),
            (CORE, w.at[far], up(far)),
            (CORE, w.at[other], up(other)),
        )[kind]
        return send_to(bit, src, w.at[dst], self.send.at[mat, kind], self.recv.at[mat, kind])

    def begin(self, mat):
        self.copy(mat, 1).start()
        self.copy(mat, 0).start()
        self.here(mat).start()

    def here(self, mat):
        return pltpu.make_async_copy(
            self.owns[mat], self.w.at[mat, pl.ds(0, self.part)], self.local.at[mat]
        )

    def after_x(self, mat):
        self.copy(mat, 1).wait_recv()
        self.copy(mat, 2).start()
        self.copy(mat, 3).start()

    def after_y(self, mat):
        self.copy(mat, 2).wait_recv()
        self.copy(mat, 4).start()

    def core_ready(self, mat):
        self.here(mat).wait()
        self.copy(mat, 0).wait_recv()

    def ready(self, mat):
        for kind in (3, 4):
            self.copy(mat, kind).wait_recv()

    def drain(self, mat):
        for kind in range(5):
            self.copy(mat, kind).wait_send()


ROOT, CUBE = 0.7978845608028654, 0.044715


def load_vectors(parts, vectors):
    d = vectors.shape[1]
    at = 0
    for part in parts:
        for i in range(part.shape[0] // d):
            vectors[at : at + 1, :] = part[i * d : (i + 1) * d].reshape(1, d)
            at += 1


class Loads:
    def __init__(self, sems):
        self.sems, self.next = sems, 0

    def start(self, src, dst):
        copy = pltpu.make_async_copy(src, dst, self.sems.at[self.next])
        self.next += 1
        copy.start()
        return copy


def forward_body(remote, *refs):
    arrived, refs = refs[:3], refs[3:]
    slopes, refs = refs[0], refs[1:]
    vector_parts, refs = refs[:8], refs[8:]
    owns, refs = refs[: 8 if remote else 1], refs[8 if remote else 1 :]
    outs, refs = refs[: 17 if remote else 16], refs[17 if remote else 16 :]
    vectors, columns, store_sems, load_sems = refs[:4]
    refs = refs[4:]
    (radar, optical, table), parts, refs = refs[:3], refs[3:11], refs[11:]
    load = Loads(load_sems)
    coming = [load.start(a, b) for a, b in zip(arrived + vector_parts, (radar, optical, table) + parts)]
    w, refs = (refs[0], refs[1:]) if remote else (owns[0], refs)
    kept = refs[:16]
    (normed, radar_low, optical_low, sq, sk, sv, cq, ck, cv, s_mixed, c_mixed, s_lse, c_lse,
     two, one, reach) = kept
    if remote:
        o_w, outs = outs[0], outs[1:]
        hub = Gather(w, owns, *refs[16:])
        greet((CORE, X_BIT, Y_BIT))
        for mat in ORDER:
            hub.begin(mat)
        slope = slope_of(slopes, lax.axis_index("head"))
    else:
        slope = slope_of(slopes, 0)
    for copy in coming:
        copy.wait()
    load_vectors(parts, vectors)
    gain_s, shift_s, gain_r, shift_r, gain_o, shift_o, bias_s, bias_c = (
        vectors.at[i : i + 1, :] for i in range(8)
    )
    stores = []

    def store(src, dst):
        copy = pltpu.make_async_copy(src, dst, store_sems.at[len(stores)])
        stores.append(copy)
        copy.start()

    def done(*names):
        for ref in names:
            i = [r is ref for r in kept].index(True)
            store(ref, outs[i])

    def hop(kind, *places):
        if remote:
            for i in places:
                (hub.after_x if kind == "x" else hub.after_y)(ORDER[i])

    near_here = []

    def core_ready(*mats):
        if remote:
            for mat in mats:
                hub.core_ready(mat)
                near_here.append(mat)

    def ready(mat):
        if mat not in near_here:
            core_ready(mat)
        if remote:
            hub.ready(mat)
            store(w.at[mat], o_w.at[mat])

    def loop_hops(index, at):
        for k, hops in at.items():
            @pl.when(index == k)
            def _():
                for kind, place in hops:
                    hop(kind, place)

    scale = HEAD_DIM**-0.5
    norm_rows(radar, gain_s, shift_s, normed)
    done(normed)
    fill_reach(table, columns, reach)
    done(reach)
    norm_rows(optical, gain_o, shift_o, optical_low)
    done(optical_low)
    core_ready(0, 1, 2)
    project(normed, w.at[0], sq, scale, 0)
    project(normed, w.at[1], sk, None, 0)
    project(normed, w.at[2], sv, None, 0)
    attend(sq, sk, sv, reach, slope, s_mixed, s_lse,
           lambda hp: loop_hops(hp, {2: (("x", 0),)}), (0, 3))
    core_ready(5, 6)
    project(optical_low, w.at[5], ck, None, 0)
    hop("x", 1)
    project(optical_low, w.at[6], cv, None, 0)
    hop("x", 2)
    hop("y", 0)
    ready(0)
    project(normed, w.at[0], sq, scale, 1)
    done(sq)
    hop("x", 3)
    hop("y", 1)
    ready(1)
    project(normed, w.at[1], sk, None, 1)
    done(sk)
    hop("y", 2)
    hop("x", 4)
    ready(2)
    project(normed, w.at[2], sv, None, 1)
    done(sv)
    attend(sq, sk, sv, reach, slope, s_mixed, s_lse,
           lambda hp: loop_hops(hp, {4: (("y", 3), ("x", 5))}), (3, 6))
    done(s_mixed, s_lse)
    hop("x", 6)
    hop("y", 4)
    ready(3)
    add_out(radar, s_mixed, w.at[3], bias_s, one)
    done(one)
    ready(5)
    project(optical_low, w.at[5], ck, None, 1)
    done(ck)
    norm_rows(one, gain_r, shift_r, radar_low)
    done(radar_low)
    core_ready(4)
    project(radar_low, w.at[4], cq, scale, 0)
    attend(cq, ck, cv, reach, slope, c_mixed, c_lse,
           lambda hp: loop_hops(hp, {0: (("x", 7), ("y", 5)), 2: (("y", 6),)}), (0, 3))
    ready(6)
    project(optical_low, w.at[6], cv, None, 1)
    done(cv)
    ready(4)
    project(radar_low, w.at[4], cq, scale, 1)
    done(cq)
    attend(cq, ck, cv, reach, slope, c_mixed, c_lse,
           lambda hp: loop_hops(hp, {4: (("y", 7),)}), (3, 6))
    done(c_mixed, c_lse)
    ready(7)
    add_out(one, c_mixed, w.at[7], bias_c, two)
    done(two)
    if remote:
        for mat in range(8):
            hub.drain(mat)
    for copy in stores:
        copy.wait()


def run_forward(remote, radar, optical, vectors, table, slopes, weights):
    n, d = radar.shape
    low, lse, wide = shape((n, d), BF16), shape((6, 2, n), F32), shape((n, d), F32)
    kept = [low] * 11 + [lse, lse, wide, wide, shape((n, n), F32)]
    whole = [shape((8, d, d), BF16)] if remote else []
    return pl.pallas_call(
        functools.partial(forward_body, remote),
        out_shape=whole + kept,
        in_specs=[HBM] * 3 + [SMEM] + [HBM] * len(vectors)
        + [HBM if remote else VMEM] * len(weights),
        out_specs=[HBM] * len(whole + kept),
        scratch_shapes=[
            pltpu.VMEM((8, d), F32), pltpu.VMEM((3, n, 128), F32),
            pltpu.SemaphoreType.DMA((24,)), pltpu.SemaphoreType.DMA((11,)),
        ] + [pltpu.VMEM(a.shape, a.dtype) for a in (radar, optical, table) + vectors] + [pltpu.VMEM(a.shape, a.dtype) for a in whole + kept]
        + ([pltpu.SemaphoreType.DMA((8, 5))] * 2 + [pltpu.SemaphoreType.DMA((8,))] if remote else []),
        compiler_params=pltpu.CompilerParams(
            vmem_limit_bytes=LIMIT, **(dict(collective_id=0, has_side_effects=True) if remote else {})
        ),
        name="forward",
        cost_estimate=pl.CostEstimate(flops=8 * 10**9, bytes_accessed=3 * 10**7, transcendentals=0),
    )(radar, optical, table, slopes, *vectors, *weights)


PATHS = {
    "A": ("XY", "YX", "XY", "XY"),
    "B": ("XY", "YX", "YX", "YX"),
    "C": ("NYX", "NYX", "XYN", "XYN"),
    "S": ("YXN", "YXN", "YXN", "XYN"),
}
AGAIN = {
    "C": ("NY", "NY", "NY", "NY"),
    "S": ("NY", "YN", "NY", "NY"),
}
NEAR_PAIR = 0
FIRST_SLOT = {"A": 0, "B": 4, "C": 8, "S": 0}
FIRST_BACK = {"A": 0, "C": 4, "S": 8, "B": 12}
UNIT = {"A": 0, "B": 1, "C": 0, "S": 1}
AXES = {"X": X_BIT, "Y": Y_BIT, "N": Z_NEAR, "F": Z_FAR}


def core_slot(unit, j):
    return {"A": j % 2, "B": 2 + j % 2}.get(unit, j)


class Sums:
    def __init__(self, refs):
        (self.g, self.rc, self.r1, self.r2, self.r3, self.rf, self.rn, self.zb, self.zn, self.zf,
         self.all,
         self.cs, self.cr, self.s1, self.q1, self.s2, self.q2, self.s3, self.q3, self.sf, self.qf,
         self.sn, self.qn, self.sz, self.qz, self.sa, self.qa,
         self.sm, self.sq, self.ss, self.sr) = refs
        dp, head = lax.axis_index("dp"), lax.axis_index("head")
        self.mc, self.mx, self.my = head % 2, head // 2, dp % 2
        self.z0, self.z1 = dp // 2 % 2, dp // 4
        columns = self.g.shape[-1] // 2
        self.columns = [
            pl.ds(pl.multiple_of(columns * z, columns), columns) for z in (self.z1, 1 - self.z1)
        ]

    def mine(self, unit):
        if unit in "CS":
            return {"C": 0, "X": 0, "Y": self.my, "N": self.z0}
        return {"C": self.mc, "X": self.mx, "Y": self.my}

    def slots(self, unit, j):
        slot = FIRST_SLOT[unit] + j
        if unit == "B" and j // 2 == NEAR_PAIR:
            slot = 4 + 2 * NEAR_PAIR + self.z0
        return slot, FIRST_BACK[unit] + j

    def part(self, unit, j, held, sent=None):
        at = {"X": slice(None), "Y": slice(None), "N": slice(None)}
        mine = self.mine(unit)
        for axis in held:
            at[axis] = mine[axis]
        if sent:
            at[sent] = 1 - mine[sent]
        return self.g.at[self.slots(unit, j)[0], mine["C"], at["X"], at["Y"], at["N"]]

    def put(self, unit, slot, row, value):
        end = row + value.shape[0]
        at = row
        while at < end:
            t, half = at // 96, at // 48 % 2
            stop = min(end, at // 48 * 48 + 48)
            if unit in "AB":
                y, x, c = t // 4, t // 2 % 2, t % 2
            else:
                x, c, y = t // 4, t // 2 % 2, t % 2
            self.g[slot, c, x, y, half, at % 48 : at % 48 + stop - at, :] = value[
                at - row : stop - row
            ].astype(BF16)
            at = stop

    def add(self, part, got):
        for at in np.ndindex(*part.shape[:-2]):
            part[*at] = part[*at] + got[*at]

    def core_copy(self, unit, j):
        slot = FIRST_SLOT[unit] + j
        return send_to(
            CORE, self.g.at[slot, 1 - self.mine(unit)["C"]], self.rc.at[core_slot(unit, j)],
            self.cs.at[slot], self.cr.at[slot],
        )

    def step_copy(self, unit, j, step):
        path = PATHS[unit][j]
        back = FIRST_BACK[unit] + j
        got, send, recv = (
            (self.r1, self.s1, self.q1), (self.r2, self.s2, self.q2), (self.r3, self.s3, self.q3)
        )[step]
        if step == 2:
            back -= 4
        return send_to(
            AXES[path[step]], self.part(unit, j, path[:step], path[step]), got.at[back],
            send.at[back], recv.at[back],
        ), got.at[back]

    def begin(self, unit, j):
        self.core_copy(unit, j).start()

    def event(self, kind, unit, j):
        u = UNIT.get(unit)
        attention = unit in "CS"
        if kind == "1":
            self.core_copy(unit, j).wait()
            mine, got = self.mine(unit), self.rc.at[core_slot(unit, j)]
            chunk = self.g.at[FIRST_SLOT[unit] + j, mine["C"]]
            if unit == "B" and j // 2 == NEAR_PAIR:
                self.add(chunk, got)
                if j % 2:
                    self.near_copy().start()
                return
            axis = PATHS[unit][j][0]
            place = "XYN".index(axis)
            for keep in (1 - mine[axis], mine[axis]):
                at = [slice(None)] * 3
                at[place] = keep
                self.add(chunk.at[*at], got.at[*at])
                if keep is not mine[axis]:
                    self.step_copy(unit, j, 0)[0].start()
        elif kind == "n":
            self.near_copy().wait()
            self.add(self.part("B", 2 * j, ""), self.rn)
            self.step_copy("B", 2 * j, 0)[0].start()
        elif kind in "23" or (kind == "5" and attention):
            step = {"2": 0, "3": 1, "5": 2}[kind]
            path = PATHS[unit][j]
            copy, got = self.step_copy(unit, j, step)
            copy.wait()
            part = self.part(unit, j, path[: step + 1])
            if step == 1 and not attention:
                early = unit == "B" and j // 2 == NEAR_PAIR
                z = 2 * (self.z0 if early else j % 2) + j // 2
                for half in range(2):
                    self.zb[u, z, half] = part[half] + got[half]
                return
            if step == 2:
                part[...] = part[...] + got[...]
                self.far_quarter(unit, j).start()
            else:
                self.add(part, got)
                self.step_copy(unit, j, step + 1)[0].start()
        elif kind == "4":
            self.z_copy(unit).start()
        elif kind == "5":
            self.z_copy(unit).wait()
            at = self.near_shards(unit)
            self.add(self.zb.at[u, pl.ds(2 * self.z0 + at.start, at.size)], self.zn.at[u, at])
            self.far_copy(u).start()
        elif kind == "6":
            if attention:
                self.far_quarter(unit, j).wait()
                columns = self.columns[0]
                own = self.part(unit, j, "XYN")[:, columns]
                total = own.astype(F32) + self.rf[u, j].astype(F32)
                self.all[u, j, self.my, self.z0, :, columns] = total.astype(BF16)
                self.gather_copy(unit, j, 0).start()
                return
            self.far_copy(u).wait()
            mine = 2 * self.z0 + self.z1
            self.out[unit][...] = self.zb[u, mine].astype(F32) + self.zf[u].astype(F32)
            self.stores.append(self.load.start(self.out[unit], self.done[unit]))
        elif kind in "789":
            step = int(kind) - 7
            self.gather_copy(unit, j, step).wait()
            if step < 2:
                self.gather_copy(unit, j, step + 1).start()
            else:
                self.stores.append(self.load.start(self.all.at[u, j], self.done["all"].at[u, j]))
        elif kind == "m":
            self.small_copy(j).wait()
            self.sm[j + 1] = self.sm[j] + self.sq[j]
            if j < 4:
                self.small_copy(j + 1).start()

    def small_copy(self, step):
        bit = (CORE, X_BIT, Y_BIT, Z_NEAR, Z_FAR)[step]
        return send_to(bit, self.sm.at[step], self.sq.at[step], self.ss.at[step], self.sr.at[step])

    def far_quarter(self, unit, j):
        at = FIRST_BACK[unit] - 4 + j
        return send_to(
            Z_FAR, self.part(unit, j, "XYN").at[:, self.columns[1]], self.rf.at[UNIT[unit], j],
            self.sf.at[at], self.qf.at[at],
        )

    def near_shards(self, unit):
        return pl.ds(1 - NEAR_PAIR, 1) if unit == "B" else pl.ds(0, 2)

    def z_copy(self, unit):
        u, at = UNIT[unit], self.near_shards(unit)
        return send_to(
            Z_NEAR, self.zb.at[u, pl.ds(2 * (1 - self.z0) + at.start, at.size)], self.zn.at[u, at],
            self.sn.at[u], self.qn.at[u],
        )

    def near_copy(self):
        return send_to(
            Z_NEAR, self.g.at[4 + 2 * NEAR_PAIR + 1 - self.z0, self.mc], self.rn,
            self.sn.at[2], self.qn.at[2],
        )

    def far_copy(self, u):
        return send_to(
            Z_FAR, self.zb.at[u, 2 * self.z0 + 1 - self.z1], self.zf.at[u], self.sz.at[u], self.qz.at[u]
        )

    def gather_copy(self, unit, j, step):
        whole = self.all.at[UNIT[unit], j]
        axis = ("F" + AGAIN[unit][j])[step]
        if step == 0:
            held = whole.at[self.my, self.z0, :, self.columns[0]]
        elif step == 1:
            held = whole.at[self.my, self.z0]
        else:
            held = whole.at[self.my] if axis == "Y" else whole.at[:, self.z0]
        at = FIRST_BACK[unit] - 4 + j
        return send_to(AXES[axis], held, held, self.sa.at[step, at], self.qa.at[step, at])


TICKS = {
    "f1a": "1A0",
    "f1b": "1B0",
    "f1o": "1A1",
    "f2g": "1B1",
    "f2o": "1A2",
    "f3a": "1B2",
    "g": "1B3",
    "c0n": "1A3",
    "ch0": "2A1",
    "ch1": "1C0",
    "ch2": "2A2",
    "ch4": "nB0",
    "ch5": "2A0",
    "c2n": "2A3",
    "c4": "1C1 2B3",
    "c5": "2B0",
    "s0n": "2B2 3A1 3A0 3A2",
    "s0": "3A3 4A0 1S0",
    "sh0": "1C2",
    "sh1": "3B3",
    "sh2": "3B0 1C3 3B2 4B0",
    "sh3": "2C1",
    "sh4": "5A0 2C0",
    "sh5": "2C2",
    "s2": "5B0",
    "s2n": "3C1 1S1 2S0 3C0",
    "s3": "5C1 3C2",
    "s4": (
        "2C3 1S2 3S0 1S3",
        "5C0 2S1 6C1 5S0",
        "6C0 6A0 3C3 5C2",
    ),
    "s5": (
        "2S3 7C1 3S1 6B0",
        "2S2 6S0",
    ),
    "tail": (
        "5C3 mM0 7C0 6C2",
        "5S1 3S3 8C1 7C2",
        "3S2 5S3 8C0 6S1",
        "5S2 6C3 7S0 8C2",
        "6S3 mM1 7C3 7S1",
        "9C0 6S2 8S0 7S3",
        "mM2 8C3 9C1 7S2",
        "8S1 8S3 9C2 9S0",
        "mM3 9C3 8S2 9S2",
        "9S1 9S3 mM4",
    ),
}


def ticks(hub, name):
    words = TICKS.get(name, ())
    for word in " ".join((words,) if isinstance(words, str) else words).split():
        hub.event(word[0], word[1], int(word[2]))


def loop_ticks(hub, name, index, names):
    for k, at in enumerate(names):
        if at in TICKS:
            @pl.when(index == k)
            def _():
                ticks(hub, at)


def attention_unit(hub, unit, grad, low, mixed, q, k, v, lse, reach, slope, x, y, w, up, dq, dk, dv):
    tag = unit.lower()

    def cast(rows):
        low[rows, :] = grad[rows, :].astype(BF16)

    def chunk(j, grads, side):
        ticks(hub, f"{tag}{j}n")
        for n in range(grads.shape[1] // 256):
            hub.put(unit, FIRST_SLOT[unit] + j, 256 * n,
                    tn(grads[:, 256 * n : 256 * n + 256], side[...]))
        hub.begin(unit, j)
        ticks(hub, f"{tag}{j + 1 if j else 0}")

    rows_loop(grad.shape[0], 128, cast)
    chunk(0, mixed, low)
    project(low, w.at[3], up)
    ticks(hub, f"{tag}1")
    attend_back(q, k, v, up, mixed, lse, reach, slope, dq, dk, dv,
                lambda hp: loop_ticks(hub, tag, hp, [f"{tag}h{i}" for i in range(6)]))
    chunk(1, dq, x)
    chunk(2, dk, y)
    chunk(3, dv, y)


def backward_body(*refs):
    (h_two, h_cot, h_in, h_out, h_w, h_cq, h_ck, h_cv, h_cm, h_rlow, h_olow,
     h_sq, h_sk, h_sv, h_sm, h_normed, h_one, h_opt, h_radar, h_reach,
     h_clse, h_slse), refs = refs[:22], refs[22:]
    vector_parts, slopes, refs = refs[:7], refs[7], refs[8:]
    (o_merged, o_radar, o_opt, o_fin, o_fout, o_all, o_small), refs = refs[:7], refs[7:]
    vectors, c_lse, s_lse, fin, fout, gathered, refs = *refs[:6], refs[6:]
    parts, refs = refs[:7], refs[7:]
    sums, refs = refs[:10], refs[10:]
    (wa, wb, q, k, v, mixed, x, y, two, two_grad, out, pull, one,
     cot, low, up, dq, dk, dv, reach, sm, sq), sems = refs[:22], refs[22:]
    hub = Sums(sums + (gathered,) + tuple(sems[:16]) + (sm, sq) + tuple(sems[16:18]))
    load = Loads(sems[18])
    hub.out = {"A": fin, "B": fout}
    hub.done = {"A": o_fin, "B": o_fout, "all": o_all}
    hub.load, hub.stores = load, []
    tile_sems = sems[19]
    slope = slope_of(slopes, lax.axis_index("head"))
    gain_s, gain_r, gain_o, gain_f, shift_f, b_out = (
        vectors.at[i : i + 1, :] for i in range(6)
    )
    n = two.shape[0]
    width = wb.shape[1]
    steps = h_in.shape[1] // width

    def tile(i):
        at = pl.ds(pl.multiple_of(i * width, width), width)
        slot = i % 2
        return (
            pltpu.make_async_copy(h_in.at[:, at], wb.at[2 * slot], tile_sems.at[slot, 0]),
            pltpu.make_async_copy(h_out.at[at, :], wb.at[2 * slot + 1], tile_sems.at[slot, 1]),
        )

    greeting((CORE, X_BIT, Y_BIT, Z_NEAR, Z_FAR))
    coming = [load.start(a, b) for a, b in zip(vector_parts, parts)]
    first = [load.start(h_two, two), load.start(h_cot, cot)]
    for copy in tile(0):
        copy.start()
    for copy in coming:
        copy.wait()
    load_vectors(parts, vectors)
    sm[0] = jnp.zeros_like(sm[0])
    out[...] = jnp.zeros_like(out)
    pull[...] = jnp.zeros_like(pull)
    first[0].wait()
    norm_rows(two, gain_f, shift_f, low)
    first[1].wait()
    later = [load.start(a, b) for a, b in (
        (h_cm, mixed), (h_w.at[pl.ds(4, 4)], wa), (h_cq, q), (h_ck, k), (h_cv, v),
        (h_rlow, x), (h_olow, y), (h_one, one), (h_reach, reach), (h_clse, c_lse),
        (h_slse, s_lse))]

    def feed(i, _):
        for copy in tile(i):
            copy.wait()

        @pl.when(i < steps - 1)
        def _():
            for copy in tile(i + 1):
                copy.start()

        w_in, w_out = wb.at[2 * (i % 2)], wb.at[2 * (i % 2) + 1]
        hidden, grad = up, dq
        blocks = [slice(m, m + 256) for m in range(0, width, 256)]

        def feed_ticks(name):
            loop_ticks(hub, "f", i, [f"f{s}{name}" for s in range(4)])

        for n, at in enumerate(blocks):
            if n:
                feed_ticks("ab"[n - 1])
            h = nn(low[...], w_in[:, at]) + vectors[pl.ds(6 + i, 1), at]
            square = h * h
            half = 0.5 + 0.5 * jnp.tanh(h * (ROOT + ROOT * CUBE * square))
            hidden[:, at] = (h * half).astype(BF16)
            rise = half * (
                1.0 + h * (1.0 - half) * (2 * ROOT + 6 * ROOT * CUBE * square)
            )
            part = (nt(cot[...], w_out[at, :]) * rise).astype(BF16)
            grad[:, at] = part
            sm[0, pl.ds(11 + i, 1), at] = jnp.sum(part.astype(F32), axis=0, keepdims=True)
        feed_ticks("c")
        for n, at in enumerate(blocks):
            hub.put("A", i, at.start, tn(grad[:, at], low[...]))
            if n == 2:
                hub.begin("A", i)
            feed_ticks("de"[n] if n < 2 else "f")
        for n, at in enumerate(blocks):
            hub.put("B", 4 + i, at.start, tn(hidden[:, at], cot[...]))
            if n == 2:
                hub.begin("B", i)
            feed_ticks("ghi"[n])
        for n, at in enumerate(blocks):
            out[:, at] += nn(hidden[...], w_out[:, at])
            feed_ticks("jkl"[n])
            pull[:, at] += nt(grad[...], w_in[at, :])
            feed_ticks("mno"[n])
        return 0

    pl.semaphore_wait(pltpu.get_barrier_semaphore(), 5)
    lax.fori_loop(0, steps, feed, 0)
    self_w = load.start(h_w.at[pl.ds(0, 4)], wb)

    def close(rows):
        value, cotangent = two[rows, :], cot[rows, :].astype(F32)
        dv[rows, :] = (value + out[rows, :] + b_out[...]).astype(BF16)
        dval, dgain, dshift = norm_back_rows(value, gain_f[...], pull[rows, :])
        total = cotangent + dval
        two_grad[rows, :] = total
        sm[0, 0:1, :] += dgain
        sm[0, 1:2, :] += dshift
        sm[0, 2:3, :] += jnp.sum(cotangent, axis=0, keepdims=True)
        sm[0, 3:4, :] += jnp.sum(total, axis=0, keepdims=True)

    rows_loop(n, 128, close)
    stores = [load.start(dv, o_merged)]
    opt_load = load.start(h_opt, cot)
    ticks(hub, "g")
    for copy in later:
        copy.wait()
    stores[0].wait()
    attention_unit(hub, "C", two_grad, low, mixed, q, k, v, c_lse, reach, slope, x, y, wa,
                   up, dq, dk, dv)
    later = [load.start(a, b) for a, b in (
        (h_sm, mixed), (h_sq, q), (h_sk, k), (h_sv, v), (h_normed, x), (h_radar, y))]
    opt_load.wait()

    def cross(rows):
        dval, dgain, dshift = norm_back_rows(one[rows, :], gain_r[...], nn(dq[rows, :], wa[0]))
        total = two_grad[rows, :] + dval
        out[rows, :] = total
        sm[0, 4:5, :] += dgain
        sm[0, 5:6, :] += dshift
        sm[0, 8:9, :] += jnp.sum(total, axis=0, keepdims=True)
        dval, dgain, dshift = norm_back_rows(
            cot[rows, :].astype(F32), gain_o[...], nn(dk[rows, :], wa[1]) + nn(dv[rows, :], wa[2])
        )
        pull[rows, :] = dval
        sm[0, 6:7, :] += dgain
        sm[0, 7:8, :] += dshift

    rows_loop(n, 256, cross)
    stores = [load.start(pull, o_opt)]
    ticks(hub, "c5")
    for copy in later:
        copy.wait()
    self_w.wait()
    attention_unit(hub, "S", out, low, mixed, q, k, v, s_lse, reach, slope, x, x, wb,
                   up, dq, dk, dv)

    def own(rows):
        dval, dgain, dshift = norm_back_rows(
            y[rows, :].astype(F32), gain_s[...],
            nn(dq[rows, :], wb[0]) + nn(dk[rows, :], wb[1]) + nn(dv[rows, :], wb[2]),
        )
        two[rows, :] = out[rows, :] + dval
        sm[0, 9:10, :] += dgain
        sm[0, 10:11, :] += dshift

    rows_loop(n, 256, own)
    stores.append(load.start(two, o_radar))
    hub.small_copy(0).start()
    ticks(hub, "s5")
    ticks(hub, "tail")
    stores.append(load.start(sm.at[5], o_small))
    for copy in stores + hub.stores:
        copy.wait()


def run_backward(two, cot, feed_in, feed_out, w, cross, own, one, optical, radar, reach,
                 c_lse, s_lse, vectors, slopes):
    n, d = two.shape
    low, wide = pltpu.VMEM((n, d), BF16), pltpu.VMEM((n, d), F32)
    chunk = lambda *dims: pltpu.VMEM(dims + (48, d), BF16)
    sems = lambda *dims: pltpu.SemaphoreType.DMA(dims)
    return pl.pallas_call(
        backward_body,
        out_shape=[
            shape((n, d), BF16), shape((n, d), F32), shape((n, d), F32),
            shape((2, 48, d), F32), shape((2, 48, d), F32), shape((2, 4, 2, 2, 48, d), BF16),
            shape((16, d), F32),
        ],
        in_specs=[HBM] * (22 + len(vectors)) + [SMEM],
        out_specs=[HBM] * 7,
        scratch_shapes=[
            pltpu.VMEM((16, d), F32), pltpu.VMEM(c_lse.shape, F32), pltpu.VMEM(s_lse.shape, F32),
            pltpu.VMEM((2, 48, d), F32), pltpu.VMEM((2, 48, d), F32), chunk(2, 4, 2, 2),
            *(pltpu.VMEM(a.shape, F32) for a in vectors),
            chunk(12, 2, 2, 2, 2), chunk(4, 2, 2, 2), chunk(16, 2, 2), chunk(16, 2), chunk(8),
            pltpu.VMEM((2, 4, 48, d // 2), BF16), chunk(2, 2, 2),
            chunk(2, 4, 2), chunk(2, 2, 2), chunk(2, 2),
            pltpu.VMEM((4, d, d), BF16), pltpu.VMEM((4, d, d), BF16),
            low, low, low, low, low, low, wide, wide, wide, wide, wide,
            low, low, low, low, low, low, pltpu.VMEM((n, n), F32),
            pltpu.VMEM((6, 16, d), F32), pltpu.VMEM((5, 16, d), F32),
            sems(12), sems(12), sems(16), sems(16), sems(16), sems(16), sems(8), sems(8),
            sems(8), sems(8), sems(3), sems(3), sems(2), sems(2),
            sems(3, 8), sems(3, 8), sems(5), sems(5),
            sems(48), sems(2, 2),
        ],
        compiler_params=pltpu.CompilerParams(
            vmem_limit_bytes=LIMIT, collective_id=1, has_side_effects=True
        ),
        name="backward",
        cost_estimate=pl.CostEstimate(flops=35 * 10**9, bytes_accessed=5 * 10**7, transcendentals=0),
    )(two, cot, feed_in, feed_out, w, *cross, *own, one, optical, radar, reach,
      c_lse, s_lse, *vectors, slopes)


def call(body, outs, scratch, operands, in_specs, **more):
    return pl.pallas_call(
        body,
        out_shape=outs,
        in_specs=in_specs,
        out_specs=[VMEM] * len(outs),
        scratch_shapes=scratch,
        compiler_params=pltpu.CompilerParams(vmem_limit_bytes=LIMIT),
        **more,
    )(*operands)


def run_feed(place, two, cot, gain, shift, w_in, b_in, w_out, b_out):
    n, d = two.shape
    f = w_in.shape[1]
    tile = 768
    whole = lambda *dims: pl.BlockSpec(dims, lambda i, p: (0,) * len(dims))
    slots = pl.BlockSpec((2, 2, 1, 96, d), lambda i, p: (0, 0, i ^ p[0], 0, 0))
    grad = shape((2, 2, 4, 96, d), BF16)
    return pl.pallas_call(
        feed_step,
        grid_spec=pltpu.PrefetchScalarGridSpec(
            num_scalar_prefetch=1,
            grid=(f // tile,),
            in_specs=[
                whole(n, d), whole(n, d), whole(1, d), whole(1, d),
                pl.BlockSpec((d, tile), lambda i, p: (0, i)),
                pl.BlockSpec((1, tile), lambda i, p: (0, i)),
                pl.BlockSpec((tile, d), lambda i, p: (i, 0)),
                whole(1, d),
            ],
            out_specs=[
                whole(n, d), whole(n, d), slots, slots, slots, slots,
                pl.BlockSpec((1, 1, tile), lambda i, p: (i, 0, 0)),
                whole(8, d),
            ],
            scratch_shapes=[
                pltpu.VMEM((n, d), BF16), pltpu.VMEM((n, d), F32), pltpu.VMEM((n, d), F32),
                pltpu.VMEM((tile, d), BF16), pltpu.VMEM((tile, d), BF16),
            ],
        ),
        out_shape=[
            shape((n, d), BF16), shape((n, d), F32), grad, grad, grad, grad,
            shape((f // tile, 1, tile), F32), shape((8, d), F32),
        ],
        compiler_params=pltpu.CompilerParams(vmem_limit_bytes=LIMIT),
        name="feed",
        cost_estimate=pl.CostEstimate(flops=15 * 10**9, bytes_accessed=25 * 10**6, transcendentals=0),
    )(place, two, cot, gain, shift, w_in, b_in, w_out, b_out)


def back_scratch(n, d):
    low = pltpu.VMEM((n, d), BF16)
    return [low, pltpu.VMEM((d, d), BF16), low, low, low, low]


def run_cross_backward(place, two_grad, mixed, q, k, v, lse, reach, slope, radar_low, optical_low,
                       w, one, optical, gain_r, gain_o):
    n, d = one.shape
    grad = shape((2, 2, 4, 96, d), BF16)
    wide = shape((n, d), F32)
    return call(
        cross_backward,
        [wide, wide, grad, grad, shape((8, d), F32)],
        back_scratch(n, d),
        (place, two_grad, mixed, q, k, v, lse, reach, slope, radar_low, optical_low,
         w, one, optical, gain_r, gain_o),
        [SMEM] + [VMEM] * 7 + [SMEM] + [VMEM] * 7,
        name="cross_backward",
        cost_estimate=pl.CostEstimate(flops=12 * 10**9, bytes_accessed=25 * 10**6, transcendentals=0),
    )


def run_self_backward(place, one_grad, mixed, q, k, v, lse, reach, slope, normed, w, radar, gain):
    n, d = one_grad.shape
    grad = shape((2, 2, 4, 96, d), BF16)
    return call(
        self_backward,
        [shape((n, d), F32), grad, grad, shape((8, d), F32)],
        back_scratch(n, d),
        (place, one_grad, mixed, q, k, v, lse, reach, slope, normed, w, radar, gain),
        [SMEM] + [VMEM] * 7 + [SMEM] + [VMEM] * 4,
        name="self_backward",
        cost_estimate=pl.CostEstimate(flops=12 * 10**9, bytes_accessed=25 * 10**6, transcendentals=0),
    )


def finish(bias_part, *refs):
    sources, refs = refs[:7], refs[7:]
    outs, refs = refs[:25], refs[25:]
    in_sems, out_sems, refs = refs[0], refs[1], refs[2:]
    held, ready = refs[:7], refs[7:]
    got, small = held[:2]
    load, store = Loads(in_sems), Loads(out_sems)
    loads = [load.start(src, dst) for src, dst in zip(sources, held)]
    stores = []
    mats, vectors, bias = ready[:8], ready[8:19], ready[19]
    loads[0].wait()
    for u in range(2):
        for j, mat in enumerate((3, 0, 1, 2)):
            at = 4 * u + mat
            for half in range(2):
                for part in range(2):
                    row = 96 * half + 48 * part
                    mats[at][row : row + 48, :] = got[u, j, half, part].astype(F32)
            stores.append(store.start(mats[at], outs[5 + at]))
    for copy, src, dst in zip(loads[2:], held[2:], outs):
        copy.wait()
        stores.append(store.start(src, dst))
    loads[1].wait()
    for row, vector in zip((9, 10, 8, 4, 5, 6, 7, 3, 0, 1, 2), vectors):
        vector[...] = small[row : row + 1, :].reshape(vector.shape)
    mine, per = bias_part[0], small.shape[1] // bias.shape[0]
    line = small[pl.ds(11 + mine // per, 1), :]
    shift = (small.shape[1] - mine % per * bias.shape[0]) % small.shape[1]
    bias[...] = pltpu.roll(line, shift, 1)[:, : bias.shape[0]].reshape(bias.shape)
    for src, dst in zip(ready[8:], outs[13:]):
        stores.append(store.start(src, dst))
    for copy in stores:
        copy.wait()


def run_finish(mine, got, small, merged, radar, optical, fin, fout):
    d = got.shape[-1]
    moved = (merged, radar, optical, fin, fout)
    made = [shape((192, d), F32)] * 8 + [shape((d,), F32)] * 11 + [shape((96,), F32)]
    outs = pl.pallas_call(
        finish,
        out_shape=[shape(a.shape, a.dtype) for a in moved] + made,
        in_specs=[SMEM] + [HBM] * 7,
        out_specs=[HBM] * 25,
        scratch_shapes=[pltpu.SemaphoreType.DMA((7,)), pltpu.SemaphoreType.DMA((25,))]
        + [pltpu.VMEM(a.shape, a.dtype) for a in (got, small) + moved + tuple(made)],
        compiler_params=pltpu.CompilerParams(vmem_limit_bytes=LIMIT),
        name="finish",
    )(mine.reshape(1), got, small, *moved)
    mats = [o if i % 4 == 3 else o.T for i, o in enumerate(outs[5:13])]
    outs = list(outs)
    outs[3:5] = [o.reshape(-1, d) for o in outs[3:5]]
    return outs[:5], mats[:4], mats[4:], outs[13:24], outs[24]


def shards(
    radar, optical, patch_table, cotangent, norm_self_gain, norm_self_shift,
    self_query, self_key, self_value, self_out, self_out_bias, norm_radar_gain, norm_radar_shift,
    norm_optical_gain, norm_optical_shift, cross_query, cross_key, cross_value, cross_out,
    cross_out_bias, norm_feed_gain, norm_feed_shift, feed_in, feed_in_bias, feed_out, feed_out_bias,
):
    dp, head = lax.axis_size("dp"), lax.axis_size("head")
    near = (dp, head) == (8, 4)
    row = lambda v: v.reshape(1, -1)
    zero = jnp.int32(0)
    slopes = jnp.asarray(-np.exp2(-8.0 * np.arange(1, HEADS + 1) / HEADS), F32)
    mine = (lax.axis_index("dp") * head + lax.axis_index("head")).astype(jnp.int32)
    place = jnp.stack([zero] * 4)
    weights = (self_query, self_key, self_value, self_out,
               cross_query, cross_key, cross_value, cross_out)
    weights = tuple(w if i % 4 == 3 else w.T for i, w in enumerate(weights))
    if not near:
        w = lax.all_gather(jnp.stack(weights), "head", axis=1, tiled=True)
        weights = (w,)
    vectors = (norm_self_gain, norm_self_shift, norm_radar_gain, norm_radar_shift,
               norm_optical_gain, norm_optical_shift, self_out_bias, cross_out_bias)
    got = run_forward(near, radar, optical, vectors, patch_table, slopes, weights)
    if near:
        w, got = got[0], got[1:]
    (normed, radar_low, optical_low, sq, sk, sv, cq, ck, cv, s_mixed, c_mixed, s_lse, c_lse,
     two, one, reach) = got
    d = radar.shape[1]
    if near:
        merged, radar_grad, optical_grad, feed_in_grad, feed_out_grad, got, small = run_backward(
            two, cotangent, feed_in, feed_out, w,
            (cq, ck, cv, c_mixed, radar_low, optical_low), (sq, sk, sv, s_mixed, normed),
            one, optical, radar, reach,
            c_lse, s_lse,
            (norm_self_gain, norm_radar_gain, norm_optical_gain, norm_feed_gain, norm_feed_shift,
             feed_out_bias, feed_in_bias),
            slopes,
        )
        ((merged, radar_grad, optical_grad, feed_in_grad, feed_out_grad), cross, own, vectors,
         feed_in_bias_grad) = run_finish(
            mine, got, small, merged, radar_grad, optical_grad, feed_in_grad, feed_out_grad)
    else:
        merged, two_grad, in_keep, in_send, out_keep, out_send, bias_in, feed_small = run_feed(
            place, two, cotangent, row(norm_feed_gain), row(norm_feed_shift),
            feed_in, row(feed_in_bias), feed_out, row(feed_out_bias),
        )
        one_grad, optical_grad, cross_keep, cross_send, cross_small = run_cross_backward(
            place, two_grad, c_mixed, cq, ck, cv, c_lse, reach, slopes, radar_low, optical_low,
            w[4:], one, optical, row(norm_radar_gain), row(norm_optical_gain),
        )
        radar_grad, self_keep, self_send, self_small = run_self_backward(
            place, one_grad, s_mixed, sq, sk, sv, s_lse, reach, slopes, normed,
            w[:4], radar, row(norm_self_gain),
        )
        small = jnp.concatenate([feed_small, cross_small, self_small, bias_in.reshape(-1, d)])
        def logical(keep, send, order):
            both = jnp.stack([keep, send])
            return jnp.transpose(both, order).reshape(-1, d)

        def feed_sum(keep, send):
            return lax.psum_scatter(
                logical(keep, send, (3, 2, 1, 0, 4, 5)).astype(F32),
                ("dp", "head"), scatter_dimension=0, tiled=True,
            )

        def attn_sum(keep, send):
            total = logical(keep, send, (3, 1, 0, 2, 4, 5)).astype(F32).reshape(4, -1, d)
            total = lax.psum_scatter(total, "head", scatter_dimension=1, tiled=True)
            total = lax.psum(total, "dp")
            return total[0].T, total[1].T, total[2].T, total[3]

        feed_in_grad, feed_out_grad = feed_sum(in_keep, in_send), feed_sum(out_keep, out_send)
        cross, own = attn_sum(cross_keep, cross_send), attn_sum(self_keep, self_send)
        small = lax.psum(small, ("dp", "head"))
        vectors = [small[i] for i in (16, 17, 12, 8, 9, 10, 11, 3, 0, 1, 2)]
        bias_part = feed_in_bias.shape[0] // (dp * head)
        feed_in_bias_grad = lax.dynamic_slice_in_dim(
            small[24:28].reshape(-1), mine * bias_part, bias_part
        )
    return (
        merged, radar_grad, optical_grad, vectors[0], vectors[1], *own, *vectors[2:7],
        *cross, *vectors[7:10], feed_in_grad.T, feed_in_bias_grad, feed_out_grad, vectors[10],
    )


def solution(mesh):
    token, rep = P(("dp", "head"), None), P()
    col, row = P(None, "head"), P("head", None)
    in_specs = (
        token, token, P(None, ("dp", "head")), token,
        rep, rep, col, col, col, row, rep,
        rep, rep, rep, rep, col, col, col, row, rep,
        rep, rep, rep, rep, rep, rep,
    )
    out_specs = (
        token, token, token,
        rep, rep, col, col, col, row, rep,
        rep, rep, rep, rep, col, col, col, row, rep,
        rep, rep, P(None, ("dp", "head")), P(("dp", "head")), token, rep,
    )
    return jax.shard_map(shards, mesh=mesh, in_specs=in_specs, out_specs=out_specs, check_vma=False)
```
